768 devices in a mesh: panel: 2 (over y_hi), rad: 12 (over z), ang: 32 (over x, y_lo, core).
Axes of the slice: x: 4, y: 8 (y_hi: 2, y_lo: 4; y = y_hi * 4 + y_lo), z: 12, core: 2. Of those that a mesh axis runs over, the one named last changes fastest.
Arguments:
- state: float32 [2, 7, 192, 512, 128], P('panel', None, 'rad', 'ang'), may hold values from -6 to 6
- kappa: float32 [7, 192], P(None, 'rad'), may hold values from 0.3 to 1.5
- buoyancy: float32 [192], P('rad'), may hold values from 0.5 to 2
- donor_lon: int32 [2, 512], replicated, may hold values from 0 to 510, as said below
- donor_lat: int32 [2, 512], replicated, may hold values from 1 to 125
- fractions: float32 [2, 2, 512], replicated, may hold values from 0.05 to 0.95
Outputs:
- state_next: float32 [2, 7, 192, 512, 128], P('panel', None, 'rad', 'ang')
The draws below stay inside these ranges and needn't reach their ends.
Inputs may be any that keep to these rules, and one draw needn't show every extreme that they name: donor_lon % 16 <= 14, so each donor stencil lies in one tile of 16 longitudes; of the 32 boundary points of one receiving tile of 16 longitudes at most 2 draw on one donor tile, and some draw exactly 2.
All inputs are finite; a program needn't handle non-finite values.
Results may differ from the reference program's by a relative error of at most 0.00002.
Values sent between devices are 32-bit elements; how exact they have to be, the bound alone decides.
No kernel may reach another device: no remote copies, remote signals or barrier semaphores. Data moves between devices by JAX's collectives and lax.ppermute only.
A program may use at most 64 MiB of HBM per device.

```python
import math
import jax
import jax.numpy as jnp
from jax import lax

CP = 16
LAT = 128
NR = 192
NLON = 512
SLOT = 2
N_ANG = 32


def draw_donor_lon(key, part):
    key = jax.random.fold_in(key, 1)

    def one_tile(tile_key, tile_num):
        key_a, key_b, key_c = jax.random.split(tile_key, 3)
        order = jax.random.permutation(key_a, 2 * CP)
        position = jnp.argsort(order, stable=True)
        group = position // SLOT
        sources = jax.random.permutation(key_b, N_ANG).astype(jnp.int32)
        wanted = jnp.where(tile_num == 0, N_ANG - 1, 0).astype(jnp.int32)
        where_wanted = jnp.argmax(sources == wanted)
        sources = sources.at[where_wanted].set(sources[0]).at[0].set(wanted)
        source = sources[group]
        offset = jax.random.randint(key_c, (2 * CP,), 0, CP - 1)
        forced = jnp.where(tile_num == 0, CP - 2, 0).astype(offset.dtype)
        offset = jnp.where(position == 0, forced, offset)
        return (source * CP + offset).astype(jnp.int32)
    table = jax.vmap(one_tile)(jax.random.split(key, N_ANG), jnp.arange(N_ANG, dtype=jnp.int32))
    table = table.reshape(N_ANG, 2, CP).transpose(1, 0, 2)
    return table.reshape(2, NLON)


def plant(result, own_key, low, largest):
    index_at = [jax.random.randint(jax.random.fold_in(own_key, axis), (), 0, length) for axis, length in enumerate(result.shape)]
    widest = result.shape.index(max(result.shape))
    next_to = index_at[:widest] + [(index_at[widest] + 1) % result.shape[widest]] + index_at[widest + 1:]
    return result.at[tuple(index_at)].set(low).at[tuple(next_to)].set(largest)


def levels(key, dims, pieces, low, top_value):
    loudness = 1.0
    for dim, parts in pieces:
        steps = jax.random.uniform(jax.random.fold_in(jax.random.fold_in(key, 6), dim), (parts,), jnp.float32, low / len(pieces), top_value / len(pieces))
        loudness = loudness * jnp.repeat(jnp.exp(steps), dims[dim] // parts).reshape((-1,) + (1,) * (len(dims) - 1 - dim))
    return loudness


def centred(own_key, shape, width, limit, cuts=(), held_as=jnp.bfloat16):
    values = width * jax.random.normal(own_key, shape, jnp.float32)
    if cuts:
        values = values * levels(own_key, shape, cuts, -0.22, 0.18)
    return jnp.clip(values, -limit, limit).astype(held_as)


def setup_inputs(seed: int = 0) -> dict:
    streams_of = jax.random.split(jax.random.key(seed), 7)
    return {
        "state": centred(streams_of[0], (2, 7, NR, NLON, LAT), 1.0, 6.0, ((0, 2), (2, 12), (3, 32)), jnp.float32),
        "kappa": jnp.clip(jnp.exp(math.log(1.5) - 1.60943787 * jax.random.uniform(streams_of[1], (7, NR), jnp.float32) ** levels(streams_of[1], (7, NR), ((1, 12),), -0.2, 0.2)), 0.3, 1.5),
        "buoyancy": jnp.clip(jnp.exp(math.log(2.0) - 1.3862944 * jax.random.uniform(streams_of[2], (NR,), jnp.float32) ** levels(streams_of[2], (NR,), ((0, 12),), -0.2, 0.2)), 0.5, 2.0),
        "donor_lon": draw_donor_lon(jax.random.fold_in(streams_of[6], 71), 0),
        "donor_lat": plant(jax.random.randint(streams_of[4], (2, NLON), 1, LAT - 2), jax.random.fold_in(streams_of[4], 1), 1, (LAT - 2) - 1).astype(jnp.int32),
        "fractions": jnp.clip(jax.random.uniform(streams_of[5], (2, 2, NLON), jnp.float32, 0.05, 0.95), 0.05, 0.95),
    }


step_size = 0.1


def spatial(padded, kappa, buoyancy):
    grid = jnp.pad(padded, ((0, 0), (0, 0), (0, 0), (1, 1)))
    center = grid[:, 1:-1, 1:-1, 1:-1]
    plus = [grid[:, 2:, 1:-1, 1:-1], grid[:, 1:-1, 2:, 1:-1], grid[:, 1:-1, 1:-1, 2:]]
    minus = [grid[:, :-2, 1:-1, 1:-1], grid[:, 1:-1, :-2, 1:-1], grid[:, 1:-1, 1:-1, :-2]]
    laplace = (plus[0] + minus[0]) + (plus[1] + minus[1]) + (plus[2] + minus[2]) - 6.0 * center
    grads = [0.5 * (plus[0] - minus[0]), 0.5 * (plus[1] - minus[1]), 0.5 * (plus[2] - minus[2])]
    along_u = center[0] * grads[0] + center[1] * grads[1] + center[2] * grads[2]
    along_b = center[3] * grads[0] + center[4] * grads[1] + center[5] * grads[2]
    forcing = jnp.concatenate([along_b[3:6], along_b[0:3], jnp.zeros_like(center[6:7])], 0)
    lift = jnp.concatenate([buoyancy[None, :, None, None] * center[6:7], jnp.zeros_like(center[1:7])], 0)
    return kappa[:, :, None, None] * laplace - along_u + forcing + lift


def blend(local, lon_idx, lat_idx, frac_lon, frac_lat):
    w_one = (1.0 - frac_lon) * (1.0 - frac_lat)
    w_two = frac_lon * (1.0 - frac_lat)
    w_three = (1.0 - frac_lon) * frac_lat
    w_four = frac_lon * frac_lat
    return (w_one * local[:, :, lon_idx, lat_idx] + w_two * local[:, :, lon_idx + 1, lat_idx]
            + w_three * local[:, :, lon_idx, lat_idx + 1] + w_four * local[:, :, lon_idx + 1, lat_idx + 1])


def reference(state, kappa, buoyancy, donor_lon, donor_lat, fractions):
    def advance(field):
        padded = jnp.pad(field, ((0, 0), (1, 1), (1, 1), (0, 0)))
        return spatial(padded, kappa, buoyancy)

    def couple(field):
        other = field[::-1]
        values = lax.map(lambda pf: blend(pf, donor_lon, donor_lat, fractions[0], fractions[1]), other)
        field = field.at[:, :, :, :, 0].set(values[:, :, :, 0])
        return field.at[:, :, :, :, LAT - 1].set(values[:, :, :, 1])

    rates_zero = lax.map(advance, state)
    first = couple(state + step_size * rates_zero)
    rates_one = lax.map(advance, first)
    return couple(0.5 * (state + first + step_size * rates_one))
```

```python
import jax
import jax.numpy as jnp
from jax import lax
from jax.experimental import pallas as pl
from jax.experimental.pallas import tpu as pltpu
from jax.sharding import PartitionSpec as P

step_size = 0.1
HIGHEST = lax.Precision.HIGHEST
VMEM = pl.BlockSpec(memory_space=pltpu.VMEM)
F32 = jnp.float32

NF = 7
LV = 16
CP = 16
LAT = 128
ROWS = 24
NPTS = NF * LV


def params(**more):
    return pltpu.CompilerParams(vmem_limit_bytes=40 * 1024 * 1024, **more)


def picks(match, kid, slot):
    low = jnp.min(jnp.where(match, kid, 4096.0), axis=1, keepdims=True)
    high = jnp.max(jnp.where(match, kid, -1.0), axis=1, keepdims=True)
    low_or_none = jnp.where(low < 4096.0, low, -8.0)
    high_or_none = jnp.where(high > low, high, -8.0)
    return jnp.where(slot == 0, low_or_none, high_or_none)


def tables_kernel(where_ref, lon_ref, lat_ref, frac_ref, weights_ref, place_ref):
    n_ang = lon_ref.shape[1] // CP
    nlon = lon_ref.shape[1]
    rows = 2 * n_ang
    points = 2 * nlon
    panel = where_ref[0]
    tile = where_ref[2]

    def flat(ref):
        return jnp.concatenate([ref[0:1, :], ref[1:2, :]], axis=1)

    lon_k = flat(lon_ref)
    owner_k = lon_k >> 4
    off_k = (lon_k & 15).astype(F32)
    lat_k = flat(lat_ref).astype(F32)
    fx_k = jnp.concatenate([frac_ref[0, 0:1, :], frac_ref[0, 1:2, :]], axis=1)
    fy_k = jnp.concatenate([frac_ref[1, 0:1, :], frac_ref[1, 1:2, :]], axis=1)

    kid = lax.broadcasted_iota(jnp.int32, (1, points), 1)
    dest_k = (kid & (nlon - 1)) >> 4
    kid = kid.astype(F32)

    row = lax.broadcasted_iota(jnp.int32, (rows, 1), 0)
    match = (dest_k == (row >> 1)) & (owner_k == tile)
    pick = picks(match, kid, row & 1)
    chosen = kid == pick

    def of(value):
        return jnp.sum(jnp.where(chosen, value, 0.0), axis=1, keepdims=True)

    off, lat, fx, fy = of(off_k), of(lat_k), of(fx_k), of(fy_k)
    lane = lax.broadcasted_iota(jnp.int32, (rows, LAT), 1).astype(F32)
    lat_weight = jnp.where(lane == lat, 1.0 - fy, 0.0) + jnp.where(lane == lat + 1.0, fy, 0.0)
    lat_weight = jnp.where(pick >= 0.0, lat_weight, 0.0)
    for j in range(CP):
        lon_weight = jnp.where(off == j, 1.0 - fx, 0.0) + jnp.where(off == j - 1.0, fx, 0.0)
        weights_ref[:, j * LAT : (j + 1) * LAT] = lon_weight * lat_weight

    row = lax.broadcasted_iota(jnp.int32, (2 * rows, 1), 0)
    donor = (row & (rows - 1)) >> 1
    match = (owner_k == donor) & (dest_k == tile)
    pick = picks(match, kid, row & 1)
    pick = jnp.where(row // rows == 1 - panel, pick, -8.0).astype(jnp.int32)
    target = ((pick >> (nlon.bit_length() - 1)) << 4) + (pick & 15)
    target = jnp.where(pick >= 0, target, -1)
    lane = lax.broadcasted_iota(jnp.int32, (2 * rows, 128), 1)
    place_ref[...] = jnp.where(lane == target, 1.0, 0.0)


def tables(where, donor_lon, donor_lat, fractions):
    n_ang = donor_lon.shape[1] // CP
    return pl.pallas_call(
        tables_kernel,
        out_shape=(
            jax.ShapeDtypeStruct((2 * n_ang, CP * LAT), F32),
            jax.ShapeDtypeStruct((4 * n_ang, 128), F32),
        ),
        in_specs=[pl.BlockSpec(memory_space=pltpu.SMEM), VMEM, VMEM, VMEM],
        out_specs=(VMEM, VMEM),
        compiler_params=params(),
        cost_estimate=pl.CostEstimate(flops=4_000_000, bytes_accessed=1_000_000, transcendentals=0),
        name="tables",
    )(where, donor_lon, donor_lat, fractions)


def rates(load, count):
    along = [load(f, 0) for f in range(NF)]
    center = [a[:count] for a in along]
    half_u = [0.5 * center[d] for d in range(3)]
    half_b = [0.5 * center[3 + d] for d in range(3)]
    lap, adv, mag = [], [], []
    for f in range(NF):
        wide = along[f]
        up, down = load(f, 1)[:count], load(f, -1)[:count]
        east = pltpu.roll(wide, ROWS - 1, 0)[:count]
        west = pltpu.roll(wide, 1, 0)[:count]
        north = pltpu.roll(center[f], LAT - 1, 1)
        south = pltpu.roll(center[f], 1, 1)
        diffs = [up - down, east - west, north - south]
        lap.append((up + down) + (east + west) + (north + south) - 6.0 * center[f])
        adv.append(half_u[0] * diffs[0] + half_u[1] * diffs[1] + half_u[2] * diffs[2])
        if f < 6:
            mag.append(half_b[0] * diffs[0] + half_b[1] * diffs[1] + half_b[2] * diffs[2])
    return center, lap, adv, mag


def rate_of(f, kappa, buoyancy, center, lap, adv, mag):
    rate = kappa * lap[f] - adv[f]
    if f < 6:
        rate = rate + mag[(f + 3) % 6]
    if f == 0:
        rate = rate + buoyancy * center[6]
    return rate


def interpolate(weights_ref, rows_of):
    field = jnp.concatenate([rows_of(j) for j in range(CP)], axis=1)
    values = lax.dot_general(
        weights_ref[...], field, (((1,), (1,)), ((), ())), precision=HIGHEST, preferred_element_type=F32
    )
    return jnp.concatenate([values, jnp.zeros((values.shape[0], 128 - NPTS), F32)], axis=1)


def send(send_ref, values):
    n = values.shape[0]
    send_ref[0:n, :] = values
    send_ref[n : 2 * n, :] = values


def first_kernel(
    where_ref, state_ref, below_ref, above_ref, coef_ref, rad_below_ref, rad_above_ref, weights_ref,
    first_ref, send_ref, wide_ref,
):
    def at(f, level):
        start = (f * (LV + 4) + level) * ROWS
        return pl.ds(pl.multiple_of(start, 8) if not isinstance(start, int) else start, ROWS)

    for f in range(NF):
        for r in range(LV):
            base = (f * (LV + 4) + r + 2) * ROWS
            wide_ref[base : base + 16, :] = state_ref[0, f, r]
            wide_ref[base + 16 : base + 18, :] = above_ref[0, f, r]
            wide_ref[base + 18 : base + 20, :] = coef_ref[f, r]
            wide_ref[base + 22 : base + 24, :] = below_ref[0, f, r]
        for r in range(2):
            wide_ref[at(f, r), :] = rad_below_ref[0, f, r]
            wide_ref[at(f, LV + 2 + r), :] = rad_above_ref[0, f, r]

    def level(r, carry):
        def load(f, d):
            return wide_ref[at(f, r + 1 + d), :]

        center, lap, adv, mag = rates(load, ROWS)
        buoyancy = center[0][19:20]
        for f in range(NF):
            rate = rate_of(f, center[f][18:19], buoyancy, center, lap, adv, mag)
            start = pl.multiple_of((f * (LV + 2) + r) * ROWS, 8)
            first_ref[pl.ds(start, ROWS), :] = center[f] + step_size * rate
        return carry

    lax.fori_loop(0, LV + 2, level, 0)

    rad, ang = where_ref[1], where_ref[2]
    n_rad, n_ang = where_ref[3], where_ref[4]

    @pl.when(rad == 0)
    def _():
        for f in range(NF):
            first_ref[f * (LV + 2) * ROWS : (f * (LV + 2) + 1) * ROWS, :] = jnp.zeros((ROWS, LAT), F32)

    @pl.when(rad == n_rad - 1)
    def _():
        for f in range(NF):
            start = (f * (LV + 2) + LV + 1) * ROWS
            first_ref[start : start + ROWS, :] = jnp.zeros((ROWS, LAT), F32)

    def blank(row):
        for i in range(NF * (LV + 2)):
            first_ref[i * ROWS + row : i * ROWS + row + 1, :] = jnp.zeros((1, LAT), F32)

    @pl.when(ang == 0)
    def _():
        blank(ROWS - 1)

    @pl.when(ang == n_ang - 1)
    def _():
        blank(CP)

    def rows_of(j):
        return jnp.concatenate(
            [first_ref[pl.ds((f * (LV + 2) + 1) * ROWS + j, LV, ROWS), :] for f in range(NF)], axis=0
        )

    send(send_ref, interpolate(weights_ref, rows_of))


def received(place_ref, recv_ref):
    return lax.dot_general(
        place_ref[...], recv_ref[...], (((0,), (0,)), ((), ())), precision=HIGHEST, preferred_element_type=F32
    )


def with_rows(own, values, point, lane):
    low = jnp.broadcast_to(values[0:CP, point : point + 1], (CP, LAT))
    high = jnp.broadcast_to(values[CP : 2 * CP, point : point + 1], (CP, LAT))
    return jnp.where(lane == 0, low, jnp.where(lane == LAT - 1, high, own))


def second_kernel(state_ref, first_ref, coef_ref, recv_ref, place_ref, weights_ref, next_ref, send_ref, work_ref):
    values = received(place_ref, recv_ref)
    lane = lax.broadcasted_iota(jnp.int32, (CP, LAT), 1)
    for f in range(NF):
        for r in range(LV + 2):
            base = (f * (LV + 2) + r) * ROWS
            if 1 <= r <= LV:
                work_ref[base : base + CP, :] = with_rows(
                    first_ref[base : base + CP, :], values, f * LV + r - 1, lane
                )
                work_ref[base + CP : base + ROWS, :] = first_ref[base + CP : base + ROWS, :]
            else:
                work_ref[base : base + ROWS, :] = first_ref[base : base + ROWS, :]

    def level(r, carry):
        def load(f, d):
            start = (f * (LV + 2) + r + 1 + d) * ROWS
            return work_ref[pl.ds(pl.multiple_of(start, 8), ROWS), :]

        center, lap, adv, mag = rates(load, CP)
        buoyancy = coef_ref[0, r, 1:2, :]
        for f in range(NF):
            rate = rate_of(f, coef_ref[f, r, 0:1, :], buoyancy, center, lap, adv, mag)
            start = pl.multiple_of((f * LV + r) * CP, 8)
            next_ref[pl.ds(start, CP), :] = 0.5 * (state_ref[0, f, r] + center[f] + step_size * rate)
        return carry

    lax.fori_loop(0, LV, level, 0)
    send(send_ref, interpolate(weights_ref, lambda j: next_ref[pl.ds(j, NPTS, CP), :]))


def last_kernel(next_ref, recv_ref, place_ref, out_ref):
    values = received(place_ref, recv_ref)
    lane = lax.broadcasted_iota(jnp.int32, (CP, LAT), 1)
    for f in range(NF):
        for r in range(LV):
            base = (f * LV + r) * CP
            out_ref[0, f, r] = with_rows(next_ref[base : base + CP, :], values, f * LV + r, lane)


def shift(value, axis, step):
    count = lax.axis_size(axis)
    pairs = [(i, i + step) for i in range(count) if 0 <= i + step < count]
    return lax.ppermute(value, axis, pairs)


def exchange(values):
    n = values.shape[0] // 2
    got = lax.all_to_all(values.reshape(n, 2, 128), ("panel", "ang"), 0, 0, tiled=True)
    return got.reshape(2 * n, 128)


def body(state, kappa, buoyancy, donor_lon, donor_lat, fractions):
    where = jnp.stack(
        [lax.axis_index(a) for a in ("panel", "rad", "ang")] + [lax.axis_size(a) for a in ("rad", "ang")]
    ).astype(jnp.int32)

    below = shift(state[:, :, :, CP - 2 :], "ang", 1)
    above = shift(state[:, :, :, :2], "ang", -1)
    coef = jnp.stack(
        [
            jnp.broadcast_to(kappa[:, :, None], (NF, LV, LAT)),
            jnp.broadcast_to(buoyancy[None, :, None], (NF, LV, LAT)),
        ],
        axis=2,
    )

    def levels(low):
        part = slice(low, low + 2)
        return jnp.concatenate(
            [
                state[:, :, part],
                above[:, :, part],
                coef[None, :, part],
                jnp.zeros((1, NF, 2, 2, LAT), F32),
                below[:, :, part],
            ],
            axis=3,
        )

    rad_below = shift(levels(LV - 2), "rad", 1)
    rad_above = shift(levels(0), "rad", -1)
    weights, place = tables(where, donor_lon, donor_lat, fractions)
    n_send = 2 * weights.shape[0]
    smem = pl.BlockSpec(memory_space=pltpu.SMEM)

    first, out = pl.pallas_call(
        first_kernel,
        out_shape=(
            jax.ShapeDtypeStruct((NF * (LV + 2) * ROWS, LAT), F32),
            jax.ShapeDtypeStruct((n_send, 128), F32),
        ),
        in_specs=[smem] + [VMEM] * 7,
        out_specs=(VMEM, VMEM),
        scratch_shapes=[pltpu.VMEM((NF * (LV + 4) * ROWS, LAT), F32)],
        compiler_params=params(),
        name="first",
    )(where, state, below, above, coef, rad_below, rad_above, weights)
    got = exchange(out)
    following, out = pl.pallas_call(
        second_kernel,
        out_shape=(
            jax.ShapeDtypeStruct((NPTS * CP, LAT), F32),
            jax.ShapeDtypeStruct((n_send, 128), F32),
        ),
        in_specs=[VMEM] * 6,
        out_specs=(VMEM, VMEM),
        scratch_shapes=[pltpu.VMEM((NF * (LV + 2) * ROWS, LAT), F32)],
        compiler_params=params(),
        name="second",
    )(state, first, coef, got, place, weights)
    got = exchange(out)
    return pl.pallas_call(
        last_kernel,
        out_shape=jax.ShapeDtypeStruct(state.shape, F32),
        in_specs=[VMEM] * 3,
        out_specs=VMEM,
        compiler_params=params(),
        name="last",
    )(following, got, place)


def solution(mesh):
    return jax.shard_map(
        body,
        mesh=mesh,
        in_specs=(P("panel", None, "rad", "ang", None), P(None, "rad"), P("rad"), P(), P(), P()),
        out_specs=P("panel", None, "rad", "ang", None),
        check_vma=False,
    )
```

```python
import jax
import jax.numpy as jnp
from jax import lax
from jax.experimental import pallas as pl
from jax.experimental.pallas import tpu as pltpu
from jax.sharding import PartitionSpec as P

step_size = 0.1
HIGHEST = lax.Precision.HIGHEST
VMEM = pl.BlockSpec(memory_space=pltpu.VMEM)
SMEM = pl.BlockSpec(memory_space=pltpu.SMEM)
F32 = jnp.float32

NF = 7
LV = 16
CP = 16
LAT = 128
TILE = LV * CP
BLOCK = 24
MESSAGE = 40


def params():
    return pltpu.CompilerParams(vmem_limit_bytes=40 * 1024 * 1024)


def cost(flops):
    return pl.CostEstimate(flops=flops, bytes_accessed=2_000_000, transcendentals=0)


def shape(*dims):
    return jax.ShapeDtypeStruct(dims, F32)


def picks(match, kid, slot):
    low = jnp.min(jnp.where(match, kid, 4096.0), axis=1, keepdims=True)
    high = jnp.max(jnp.where(match, kid, -1.0), axis=1, keepdims=True)
    low_or_none = jnp.where(low < 4096.0, low, -8.0)
    high_or_none = jnp.where(high > low, high, -8.0)
    return jnp.where(slot == 0, low_or_none, high_or_none)


def tables_kernel(where_ref, lon_ref, lat_ref, frac_ref, lat_weight_ref, lon_weight_ref, place_ref):
    nlon = lon_ref.shape[1]
    half = 2 * nlon // CP
    points = 2 * nlon
    panel = where_ref[0]
    tile = where_ref[2]

    def flat(low, high):
        return jnp.concatenate([low, high], axis=1)

    lon_k = flat(lon_ref[0:1, :], lon_ref[1:2, :])
    owner_k = lon_k >> 4
    off_k = (lon_k & 15).astype(F32)
    lat_k = flat(lat_ref[0:1, :], lat_ref[1:2, :]).astype(F32)
    fx_k = flat(frac_ref[0, 0:1, :], frac_ref[0, 1:2, :])
    fy_k = flat(frac_ref[1, 0:1, :], frac_ref[1, 1:2, :])

    kid = lax.broadcasted_iota(jnp.int32, (1, points), 1)
    dest_k = (kid & (nlon - 1)) >> 4
    kid = kid.astype(F32)

    row = lax.broadcasted_iota(jnp.int32, (half, 1), 0)
    match = (dest_k == (row >> 1)) & (owner_k == tile)
    pick = picks(match, kid, row & 1)
    chosen = kid == pick

    def of(value):
        return jnp.sum(jnp.where(chosen, value, 0.0), axis=1, keepdims=True)

    off, lat, fx, fy = of(off_k), of(lat_k), of(fx_k), of(fy_k)
    lane = lax.broadcasted_iota(jnp.int32, (half, LAT), 1).astype(F32)
    lat_weight = jnp.where(lane == lat, 1.0 - fy, 0.0) + jnp.where(lane == lat + 1.0, fy, 0.0)
    lat_weight = jnp.where(pick >= 0.0, lat_weight, 0.0)
    lon_weight = jnp.where(lane == off, 1.0 - fx, 0.0) + jnp.where(lane == off + 1.0, fx, 0.0)
    lat_weight_ref[...] = jnp.transpose(jnp.concatenate([lat_weight, lat_weight], axis=0))
    lon_weight_ref[...] = jnp.transpose(jnp.concatenate([lon_weight, lon_weight], axis=0))[0:CP]

    row = lax.broadcasted_iota(jnp.int32, (half, 1), 0)
    match = (owner_k == (row >> 1)) & (dest_k == tile)
    pick = picks(match, kid, row & 1).astype(jnp.int32)
    target = ((pick >> (nlon.bit_length() - 1)) << 4) + (pick & 15)
    target = jnp.where(pick >= 0, target, -1)
    lane = lax.broadcasted_iota(jnp.int32, (half, 128), 1)
    place = jnp.where(lane == target, 1.0, 0.0)
    place_ref[0:half, :] = place * panel.astype(F32)
    place_ref[half : 2 * half, :] = place * (1 - panel).astype(F32)


def increments(center, neighbours, kappa, buoyancy, scale):
    u = [(0.5 * scale) * center[d] for d in range(3)]
    b = [(0.5 * scale) * center[3 + d] for d in range(3)]
    lap, adv, mag = [], [], []
    for f in range(NF):
        up, down, east, west = neighbours(f)
        north = pltpu.roll(center[f], LAT - 1, 1)
        south = pltpu.roll(center[f], 1, 1)
        diffs = [up - down, east - west, north - south]
        lap.append((scale * kappa(f)) * ((up + down) + (east + west) + (north + south) - 6.0 * center[f]))
        adv.append(u[0] * diffs[0] + u[1] * diffs[1] + u[2] * diffs[2])
        if f < 6:
            mag.append(b[0] * diffs[0] + b[1] * diffs[1] + b[2] * diffs[2])
    rates = [lap[f] - adv[f] + mag[(f + 3) % 6] for f in range(6)] + [lap[6] - adv[6]]
    rates[0] = rates[0] + (scale * buoyancy) * center[6]
    return rates


def interpolate(rows, lat_weight_ref, lon_weight_ref):
    along = jnp.dot(rows, lat_weight_ref[...], precision=HIGHEST, preferred_element_type=F32)
    n = rows.shape[0] // CP
    return jnp.sum(along.reshape(n, CP, along.shape[1]) * lon_weight_ref[...][None], axis=1)


def pack_kernel(state_ref, below_ref, above_ref, coef_ref, up_ref, down_ref):
    for ref, near, far in ((up_ref, LV - 1, LV - 2), (down_ref, 0, 1)):
        for f in range(NF):
            start = f * TILE
            ref[f, 0:CP, :] = state_ref[start + near * CP : start + (near + 1) * CP, :]
            ref[f, CP : 2 * CP, :] = state_ref[start + far * CP : start + (far + 1) * CP, :]
            ref[f, 32:33, :] = above_ref[0, f, near : near + 1, :]
            ref[f, 33:34, :] = below_ref[1, f, near : near + 1, :]
            ref[f, 34:35, :] = coef_ref[f, near : near + 1, :]
            ref[f, 35:36, :] = coef_ref[NF, near : near + 1, :]
            ref[f, 36:40, :] = jnp.zeros((4, LAT), F32)


def first_a_kernel(
    state_ref, below_ref, above_ref, coef_ref, lat_weight_ref, lon_weight_ref, inner_ref, values_ref, line_ref
):
    for f in range(NF):
        for r in range(LV):
            base = (f * LV + r) * BLOCK + 8
            line_ref[base : base + CP, :] = state_ref[f * TILE + r * CP : f * TILE + (r + 1) * CP, :]
        line_ref[pl.ds(f * LV * BLOCK + 7, LV, BLOCK), :] = below_ref[1, f]
        line_ref[pl.ds(f * LV * BLOCK + 24, LV, BLOCK), :] = above_ref[0, f]
        for r in (0, LV - 1):
            inner_ref[f * TILE + r * CP : f * TILE + (r + 1) * CP, :] = jnp.zeros((CP, LAT), F32)
    for r in range(1, LV - 1):
        for t in range(2):

            def row(f, level=r):
                return f * TILE + level * CP + 8 * t

            def neighbours(f):
                line = (f * LV + r) * BLOCK + 8 + 8 * t
                return (
                    state_ref[row(f, r + 1) : row(f, r + 1) + 8, :],
                    state_ref[row(f, r - 1) : row(f, r - 1) + 8, :],
                    line_ref[line + 1 : line + 9, :],
                    line_ref[line - 1 : line + 7, :],
                )

            center = [state_ref[row(f) : row(f) + 8, :] for f in range(NF)]
            rates = increments(
                center, neighbours, lambda f: coef_ref[f, r : r + 1, :], coef_ref[NF, r : r + 1, :], step_size
            )
            for f in range(NF):
                inner_ref[row(f) : row(f) + 8, :] = center[f] + rates[f]
    values_ref[...] = interpolate(inner_ref[...], lat_weight_ref, lon_weight_ref)


def first_b_kernel(
    where_ref, state_ref, below_ref, above_ref, coef_ref, rad_below_ref, rad_above_ref, lat_weight_ref,
    lon_weight_ref, values_ref, edge_ref, ring_ref, send_ref, line_ref, column_ref,
):
    rad, ang, n_rad, n_ang = where_ref[1], where_ref[2], where_ref[3], where_ref[4]
    keep_rad = [jnp.where(rad == 0, 0.0, 1.0), jnp.where(rad == n_rad - 1, 0.0, 1.0)]
    keep_ang = [jnp.where(ang == 0, 0.0, 1.0), jnp.where(ang == n_ang - 1, 0.0, 1.0)]
    radial = (rad_below_ref, rad_above_ref)

    for f in range(NF):
        for e, r in ((1, 0), (2, LV - 1)):
            base = (e * NF + f) * BLOCK + 8
            line_ref[base : base + CP, :] = state_ref[f * TILE + r * CP : f * TILE + (r + 1) * CP, :]
            line_ref[base - 1 : base, :] = below_ref[1, f, r : r + 1, :]
            line_ref[base + CP : base + CP + 1, :] = above_ref[0, f, r : r + 1, :]
        for e, ref in ((0, rad_below_ref), (3, rad_above_ref)):
            base = (e * NF + f) * BLOCK + 8
            line_ref[base : base + CP, :] = ref[f, 0:CP, :]
            line_ref[base - 1 : base, :] = ref[f, 33:34, :]
            line_ref[base + CP : base + CP + 1, :] = ref[f, 32:33, :]
        for side, ref in ((0, below_ref.at[1]), (1, above_ref.at[0])):
            base = (side * NF + f) * BLOCK + 8
            column_ref[base : base + LV, :] = ref[f]
            column_ref[base - 1 : base, :] = rad_below_ref[f, 33 - side : 34 - side, :]
            column_ref[base + LV : base + LV + 1, :] = rad_above_ref[f, 33 - side : 34 - side, :]

    for e in range(4):
        for t in range(2):
            part = slice(8 * t, 8 * t + 8)

            def own(f, r):
                return state_ref[f * TILE + r * CP + 8 * t : f * TILE + r * CP + 8 * t + 8, :]

            def neighbours(f):
                line = (e * NF + f) * BLOCK + 8 + 8 * t
                if e == 0:
                    up, down = own(f, 0), rad_below_ref[f, CP + 8 * t : CP + 8 * t + 8, :]
                elif e == 1:
                    up, down = own(f, 1), rad_below_ref[f, part, :]
                elif e == 2:
                    up, down = rad_above_ref[f, part, :], own(f, LV - 2)
                else:
                    up, down = rad_above_ref[f, CP + 8 * t : CP + 8 * t + 8, :], own(f, LV - 1)
                return up, down, line_ref[line + 1 : line + 9, :], line_ref[line - 1 : line + 7, :]

            center = [line_ref[(e * NF + f) * BLOCK + 8 + 8 * t : (e * NF + f) * BLOCK + 16 + 8 * t, :] for f in range(NF)]
            if e in (0, 3):
                source = radial[e // 3]
                rates = increments(center, neighbours, lambda f: source[f, 34:35, :], source[0, 35:36, :], step_size)
            else:
                r = (e - 1) * (LV - 1)
                rates = increments(
                    center, neighbours, lambda f: coef_ref[f, r : r + 1, :], coef_ref[NF, r : r + 1, :], step_size
                )
            for f in range(NF):
                value = center[f] + rates[f]
                if e in (0, 3):
                    value = keep_rad[e // 3] * value
                base = (e * 8 + f) * CP + 8 * t
                edge_ref[base : base + 8, :] = value
        edge_ref[(e * 8 + NF) * CP : (e * 8 + 8) * CP, :] = jnp.zeros((CP, LAT), F32)

    for side in range(2):
        for t in range(2):
            part = slice(8 * t, 8 * t + 8)

            def neighbours(f):
                column = (side * NF + f) * BLOCK + 8 + 8 * t
                near = state_ref[pl.ds(f * TILE + 8 * t * CP + side * (CP - 1), 8, CP), :]
                if side == 0:
                    east, west = near, below_ref[0, f, part, :]
                else:
                    east, west = above_ref[1, f, part, :], near
                return column_ref[column + 1 : column + 9, :], column_ref[column - 1 : column + 7, :], east, west

            center = [(below_ref[1, f, part, :] if side == 0 else above_ref[0, f, part, :]) for f in range(NF)]
            rates = increments(center, neighbours, lambda f: coef_ref[f, part, :], coef_ref[NF, part, :], step_size)
            for f in range(NF):
                ring_ref[side, f, part, :] = keep_ang[side] * (center[f] + rates[f])

    edges = interpolate(edge_ref[8 * CP : 24 * CP, :], lat_weight_ref, lon_weight_ref)
    send_ref[...] = jnp.transpose(jnp.concatenate([values_ref[...], edges], axis=0))


def received(place_ref, recv_ref):
    values = lax.dot_general(
        place_ref[...], recv_ref[...], (((0,), (0,)), ((), ())), precision=HIGHEST, preferred_element_type=F32
    )
    low, high = values[0:CP], pltpu.roll(values[CP : 2 * CP], LAT - 1, 1)
    even = (lax.broadcasted_iota(jnp.int32, (CP, LAT), 1) & 1) == 0
    return jnp.where(even, low, high), jnp.where(even, high, low)


def with_rows(own, values, point, ends):
    rows = values[point % 2]
    if point:
        rows = pltpu.roll(rows, LAT - point, 1)
    return jnp.where(ends, rows, own)


def ends_of():
    lane = lax.broadcasted_iota(jnp.int32, (CP, LAT), 1)
    return (lane == 0) | (lane == LAT - 1)


def second_kernel(
    state_ref, inner_ref, edge_ref, ring_ref, coef_ref, recv_ref, place_ref, lat_weight_ref, lon_weight_ref,
    next_ref, send_ref, line_ref,
):
    values = received(place_ref, recv_ref)
    ends = ends_of()
    for f in range(NF):
        for r in range(-1, LV + 1):
            base = (f * (LV + 2) + r + 1) * BLOCK + 8
            if 1 <= r <= LV - 2:
                own = inner_ref[f * TILE + r * CP : f * TILE + (r + 1) * CP, :]
                point = f * LV + r
            else:
                e = {-1: 0, 0: 1, LV - 1: 2, LV: 3}[r]
                own = edge_ref[(e * 8 + f) * CP : (e * 8 + f + 1) * CP, :]
                point = NF * LV + (e - 1) * 8 + f
            if 0 <= r <= LV - 1:
                own = with_rows(own, values, point, ends)
            line_ref[base : base + CP, :] = own
        start = (f * (LV + 2) + 1) * BLOCK
        line_ref[pl.ds(start + 7, LV, BLOCK), :] = ring_ref[0, f]
        line_ref[pl.ds(start + 24, LV, BLOCK), :] = ring_ref[1, f]

    for r in range(LV):
        for t in range(2):

            def line(f, level=r):
                return (f * (LV + 2) + level + 1) * BLOCK + 8 + 8 * t

            def neighbours(f):
                return (
                    line_ref[line(f, r + 1) : line(f, r + 1) + 8, :],
                    line_ref[line(f, r - 1) : line(f, r - 1) + 8, :],
                    line_ref[line(f) + 1 : line(f) + 9, :],
                    line_ref[line(f) - 1 : line(f) + 7, :],
                )

            center = [line_ref[line(f) : line(f) + 8, :] for f in range(NF)]
            rates = increments(
                center, neighbours, lambda f: coef_ref[f, r : r + 1, :], coef_ref[NF, r : r + 1, :], 0.5 * step_size
            )
            for f in range(NF):
                row = f * TILE + r * CP + 8 * t
                next_ref[row : row + 8, :] = 0.5 * (state_ref[row : row + 8, :] + center[f]) + rates[f]
    donors = interpolate(next_ref[...], lat_weight_ref, lon_weight_ref)
    send_ref[...] = jnp.transpose(jnp.concatenate([donors, jnp.zeros((128 - NF * LV, 128), F32)], axis=0))


def last_kernel(next_ref, recv_ref, place_ref, out_ref, done_ref, sems):
    values = received(place_ref, recv_ref)
    ends = ends_of()
    copies = []
    for f in range(NF):
        for r in range(LV):
            row = f * TILE + r * CP
            done_ref[row : row + CP, :] = with_rows(next_ref[row : row + CP, :], values, f * LV + r, ends)
        part = pl.ds(f * TILE, TILE)
        copies.append(pltpu.make_async_copy(done_ref.at[part, :], out_ref.at[part, :], sems.at[f]))
        copies[-1].start()
    for copy in copies:
        copy.wait()


def shift(value, axis, step):
    count = lax.axis_size(axis)
    pairs = [(i, i + step) for i in range(count) if 0 <= i + step < count]
    return lax.ppermute(value, axis, pairs)


def exchange(values):
    n = values.shape[0] // 2
    got = lax.all_to_all(values.reshape(n, 2, 128), ("panel", "ang"), 0, 0, tiled=True)
    return got.reshape(2 * n, 128)


def body(state, kappa, buoyancy, donor_lon, donor_lat, fractions):
    where = jnp.stack(
        [lax.axis_index(a) for a in ("panel", "rad", "ang")] + [lax.axis_size(a) for a in ("rad", "ang")]
    ).astype(jnp.int32)

    below = shift(jnp.stack([state[0, :, :, CP - 2], state[0, :, :, CP - 1]]), "ang", 1)
    above = shift(jnp.stack([state[0, :, :, 0], state[0, :, :, 1]]), "ang", -1)
    own = state.reshape(NF * TILE, LAT)

    coef = jnp.broadcast_to(jnp.concatenate([kappa, buoyancy[None]])[:, :, None], (NF + 1, LV, LAT))
    n_send = 4 * donor_lon.shape[1] // CP
    lat_weight, lon_weight, place = pl.pallas_call(
        tables_kernel,
        out_shape=(shape(LAT, n_send), shape(CP, n_send), shape(n_send, 128)),
        in_specs=[SMEM] + [VMEM] * 3,
        out_specs=(VMEM,) * 3,
        compiler_params=params(),
        cost_estimate=cost(4_000_000),
        name="tables",
    )(where, donor_lon, donor_lat, fractions)
    coef, lat_weight = lax.optimization_barrier((coef, lat_weight))

    up, down = pl.pallas_call(
        pack_kernel,
        out_shape=(shape(NF, MESSAGE, LAT),) * 2,
        in_specs=[VMEM] * 4,
        out_specs=(VMEM,) * 2,
        compiler_params=params(),
        name="pack",
    )(own, below, above, coef)
    rad_below = shift(up, "rad", 1)
    rad_above = shift(down, "rad", -1)

    inner, inner_values = pl.pallas_call(
        first_a_kernel,
        out_shape=(shape(NF * TILE, LAT), shape(NF * LV, n_send)),
        in_specs=[VMEM] * 6,
        out_specs=(VMEM,) * 2,
        scratch_shapes=[pltpu.VMEM((NF * LV * BLOCK + 8, LAT), F32)],
        compiler_params=params(),
        cost_estimate=cost(60_000_000),
        name="first_a",
    )(own, below, above, coef, lat_weight, lon_weight)
    edge, ring, out = pl.pallas_call(
        first_b_kernel,
        out_shape=(shape(4 * 8 * CP, LAT), shape(2, NF, LV, LAT), shape(n_send, 128)),
        in_specs=[SMEM] + [VMEM] * 9,
        out_specs=(VMEM,) * 3,
        scratch_shapes=[
            pltpu.VMEM((4 * NF * BLOCK + 8, LAT), F32),
            pltpu.VMEM((2 * NF * BLOCK + 8, LAT), F32),
        ],
        compiler_params=params(),
        name="first_b",
    )(where, own, below, above, coef, rad_below, rad_above, lat_weight, lon_weight, inner_values)
    got = exchange(out)
    following, out = pl.pallas_call(
        second_kernel,
        out_shape=(shape(NF * TILE, LAT), shape(n_send, 128)),
        in_specs=[VMEM] * 9,
        out_specs=(VMEM,) * 2,
        scratch_shapes=[pltpu.VMEM((NF * (LV + 2) * BLOCK + 8, LAT), F32)],
        compiler_params=params(),
        name="second",
    )(own, inner, edge, ring, coef, got, place, lat_weight, lon_weight)
    got = exchange(out)
    result = pl.pallas_call(
        last_kernel,
        out_shape=shape(NF * TILE, LAT),
        in_specs=[VMEM] * 3,
        out_specs=pl.BlockSpec(memory_space=pl.ANY),
        scratch_shapes=[pltpu.VMEM((NF * TILE, LAT), F32), pltpu.SemaphoreType.DMA((NF,))],
        compiler_params=params(),
        name="last",
    )(following, got, place)
    return result.reshape(state.shape)


def solution(mesh):
    return jax.shard_map(
        body,
        mesh=mesh,
        in_specs=(P("panel", None, "rad", "ang", None), P(None, "rad"), P("rad"), P(), P(), P()),
        out_specs=P("panel", None, "rad", "ang", None),
        check_vma=False,
    )
```

```python
import jax
import jax.numpy as jnp
from jax import lax
from jax.experimental import pallas as pl
from jax.experimental.pallas import tpu as pltpu
from jax.sharding import PartitionSpec as P

step_size = 0.1
HIGHEST = lax.Precision.HIGHEST
VMEM = pl.BlockSpec(memory_space=pltpu.VMEM)
SMEM = pl.BlockSpec(memory_space=pltpu.SMEM)
F32 = jnp.float32

NF = 7
LV = 16
CP = 16
LAT = 128
TILE = LV * CP
BLOCK = 24
MESSAGE = 40


def params():
    return pltpu.CompilerParams(vmem_limit_bytes=40 * 1024 * 1024)


def cost(flops):
    return pl.CostEstimate(flops=flops, bytes_accessed=2_000_000, transcendentals=0)


def shape(*dims):
    return jax.ShapeDtypeStruct(dims, F32)


def picks(match, kid, slot):
    low = jnp.min(jnp.where(match, kid, 4096.0), axis=1, keepdims=True)
    high = jnp.max(jnp.where(match, kid, -1.0), axis=1, keepdims=True)
    low_or_none = jnp.where(low < 4096.0, low, -8.0)
    high_or_none = jnp.where(high > low, high, -8.0)
    return jnp.where(slot == 0, low_or_none, high_or_none)


def tables_kernel(where_ref, lon_ref, lat_ref, frac_ref, lat_weight_ref, lon_weight_ref, place_ref):
    nlon = lon_ref.shape[1]
    half = 2 * nlon // CP
    points = 2 * nlon
    panel = where_ref[0]
    tile = where_ref[2]

    def flat(low, high):
        return jnp.concatenate([low, high], axis=1)

    lon_k = flat(lon_ref[0:1, :], lon_ref[1:2, :])
    owner_k = lon_k >> 4
    off_k = (lon_k & 15).astype(F32)
    lat_k = flat(lat_ref[0:1, :], lat_ref[1:2, :]).astype(F32)
    fx_k = flat(frac_ref[0, 0:1, :], frac_ref[0, 1:2, :])
    fy_k = flat(frac_ref[1, 0:1, :], frac_ref[1, 1:2, :])

    kid = lax.broadcasted_iota(jnp.int32, (1, points), 1)
    dest_k = (kid & (nlon - 1)) >> 4
    kid = kid.astype(F32)

    row = lax.broadcasted_iota(jnp.int32, (half, 1), 0)
    match = (dest_k == (row >> 1)) & (owner_k == tile)
    pick = picks(match, kid, row & 1)
    chosen = kid == pick

    def of(value):
        return jnp.sum(jnp.where(chosen, value, 0.0), axis=1, keepdims=True)

    off, lat, fx, fy = of(off_k), of(lat_k), of(fx_k), of(fy_k)
    lane = lax.broadcasted_iota(jnp.int32, (half, LAT), 1).astype(F32)
    lat_weight = jnp.where(lane == lat, 1.0 - fy, 0.0) + jnp.where(lane == lat + 1.0, fy, 0.0)
    lat_weight = jnp.where(pick >= 0.0, lat_weight, 0.0)
    lon_weight = jnp.where(lane == off, 1.0 - fx, 0.0) + jnp.where(lane == off + 1.0, fx, 0.0)
    lat_weight_ref[...] = jnp.transpose(jnp.concatenate([lat_weight, lat_weight], axis=0))
    lon_weight_ref[...] = jnp.transpose(jnp.concatenate([lon_weight, lon_weight], axis=0))[0:CP]

    row = lax.broadcasted_iota(jnp.int32, (half, 1), 0)
    match = (owner_k == (row >> 1)) & (dest_k == tile)
    pick = picks(match, kid, row & 1).astype(jnp.int32)
    target = ((pick >> (nlon.bit_length() - 1)) << 4) + (pick & 15)
    target = jnp.where(pick >= 0, target, -1)
    lane = lax.broadcasted_iota(jnp.int32, (half, 128), 1)
    place = jnp.where(lane == target, 1.0, 0.0)
    place_ref[0:half, :] = place * panel.astype(F32)
    place_ref[half : 2 * half, :] = place * (1 - panel).astype(F32)


def increments(center, neighbours, kappa, buoyancy, scale):
    u = [(0.5 * scale) * center[d] for d in range(3)]
    b = [(0.5 * scale) * center[3 + d] for d in range(3)]
    lap, adv, mag = [], [], []
    for f in range(NF):
        up, down, east, west = neighbours(f)
        north = pltpu.roll(center[f], LAT - 1, 1)
        south = pltpu.roll(center[f], 1, 1)
        diffs = [up - down, east - west, north - south]
        lap.append((scale * kappa(f)) * ((up + down) + (east + west) + (north + south) - 6.0 * center[f]))
        adv.append(u[0] * diffs[0] + u[1] * diffs[1] + u[2] * diffs[2])
        if f < 6:
            mag.append(b[0] * diffs[0] + b[1] * diffs[1] + b[2] * diffs[2])
    rates = [lap[f] - adv[f] + mag[(f + 3) % 6] for f in range(6)] + [lap[6] - adv[6]]
    rates[0] = rates[0] + (scale * buoyancy) * center[6]
    return rates


def interpolate(rows, lat_weight_ref, lon_weight_ref):
    along = jnp.dot(rows, lat_weight_ref[...], precision=HIGHEST, preferred_element_type=F32)
    n = rows.shape[0] // CP
    return jnp.sum(along.reshape(n, CP, along.shape[1]) * lon_weight_ref[...][None], axis=1)


def cut_kernel(where_ref, state_ref, outer_ref, inner_ref):
    odd = where_ref[2] % 2 == 1
    for f in range(NF):
        for i in range(2):
            low = state_ref[pl.ds(f * TILE + i, LV, CP), :]
            high = state_ref[pl.ds(f * TILE + CP - 1 - i, LV, CP), :]
            outer_ref[i, f] = jnp.where(odd, high, low)
            inner_ref[i, f] = jnp.where(odd, low, high)


def pack_kernel(
    where_ref, state_ref, outer_ref, inner_ref, coef_ref, up_ref, down_ref, below_ref, above_ref
):
    odd = where_ref[2] % 2 == 1
    for i in range(2):
        for f in range(NF):
            above_ref[i, f] = jnp.where(odd, outer_ref[i, f], inner_ref[i, f])
            below_ref[i, f] = jnp.where(odd, inner_ref[i, f], outer_ref[i, f])
    for ref, near, far in ((up_ref, LV - 1, LV - 2), (down_ref, 0, 1)):
        for f in range(NF):
            start = f * TILE
            ref[f, 0:CP, :] = state_ref[start + near * CP : start + (near + 1) * CP, :]
            ref[f, CP : 2 * CP, :] = state_ref[start + far * CP : start + (far + 1) * CP, :]
            ref[f, 32:33, :] = above_ref[0, f, near : near + 1, :]
            ref[f, 33:34, :] = below_ref[0, f, near : near + 1, :]
            ref[f, 34:35, :] = coef_ref[f, near : near + 1, :]
            ref[f, 35:36, :] = coef_ref[NF, near : near + 1, :]
            ref[f, 36:40, :] = jnp.zeros((4, LAT), F32)


def first_a_kernel(
    state_ref, below_ref, above_ref, coef_ref, lat_weight_ref, lon_weight_ref, inner_ref, values_ref, line_ref
):
    for f in range(NF):
        for r in range(LV):
            base = (f * LV + r) * BLOCK + 8
            line_ref[base : base + CP, :] = state_ref[f * TILE + r * CP : f * TILE + (r + 1) * CP, :]
        line_ref[pl.ds(f * LV * BLOCK + 7, LV, BLOCK), :] = below_ref[0, f]
        line_ref[pl.ds(f * LV * BLOCK + 24, LV, BLOCK), :] = above_ref[0, f]
        for r in (0, LV - 1):
            inner_ref[f * TILE + r * CP : f * TILE + (r + 1) * CP, :] = jnp.zeros((CP, LAT), F32)
    for r in range(1, LV - 1):
        for t in range(2):

            def row(f, level=r):
                return f * TILE + level * CP + 8 * t

            def neighbours(f):
                line = (f * LV + r) * BLOCK + 8 + 8 * t
                return (
                    state_ref[row(f, r + 1) : row(f, r + 1) + 8, :],
                    state_ref[row(f, r - 1) : row(f, r - 1) + 8, :],
                    line_ref[line + 1 : line + 9, :],
                    line_ref[line - 1 : line + 7, :],
                )

            center = [state_ref[row(f) : row(f) + 8, :] for f in range(NF)]
            rates = increments(
                center, neighbours, lambda f: coef_ref[f, r : r + 1, :], coef_ref[NF, r : r + 1, :], step_size
            )
            for f in range(NF):
                inner_ref[row(f) : row(f) + 8, :] = center[f] + rates[f]
    values_ref[...] = interpolate(inner_ref[...], lat_weight_ref, lon_weight_ref)


def first_b_kernel(
    where_ref, state_ref, below_ref, above_ref, coef_ref, rad_below_ref, rad_above_ref, lat_weight_ref,
    lon_weight_ref, values_ref, edge_ref, ring_ref, send_ref, line_ref, column_ref,
):
    rad, ang, n_rad, n_ang = where_ref[1], where_ref[2], where_ref[3], where_ref[4]
    keep_rad = [jnp.where(rad == 0, 0.0, 1.0), jnp.where(rad == n_rad - 1, 0.0, 1.0)]
    keep_ang = [jnp.where(ang == 0, 0.0, 1.0), jnp.where(ang == n_ang - 1, 0.0, 1.0)]
    radial = (rad_below_ref, rad_above_ref)

    for f in range(NF):
        for e, r in ((1, 0), (2, LV - 1)):
            base = (e * NF + f) * BLOCK + 8
            line_ref[base : base + CP, :] = state_ref[f * TILE + r * CP : f * TILE + (r + 1) * CP, :]
            line_ref[base - 1 : base, :] = below_ref[0, f, r : r + 1, :]
            line_ref[base + CP : base + CP + 1, :] = above_ref[0, f, r : r + 1, :]
        for e, ref in ((0, rad_below_ref), (3, rad_above_ref)):
            base = (e * NF + f) * BLOCK + 8
            line_ref[base : base + CP, :] = ref[f, 0:CP, :]
            line_ref[base - 1 : base, :] = ref[f, 33:34, :]
            line_ref[base + CP : base + CP + 1, :] = ref[f, 32:33, :]
        for side, ref in ((0, below_ref.at[0]), (1, above_ref.at[0])):
            base = (side * NF + f) * BLOCK + 8
            column_ref[base : base + LV, :] = ref[f]
            column_ref[base - 1 : base, :] = rad_below_ref[f, 33 - side : 34 - side, :]
            column_ref[base + LV : base + LV + 1, :] = rad_above_ref[f, 33 - side : 34 - side, :]

    for e in range(4):
        for t in range(2):
            part = slice(8 * t, 8 * t + 8)

            def own(f, r):
                return state_ref[f * TILE + r * CP + 8 * t : f * TILE + r * CP + 8 * t + 8, :]

            def neighbours(f):
                line = (e * NF + f) * BLOCK + 8 + 8 * t
                if e == 0:
                    up, down = own(f, 0), rad_below_ref[f, CP + 8 * t : CP + 8 * t + 8, :]
                elif e == 1:
                    up, down = own(f, 1), rad_below_ref[f, part, :]
                elif e == 2:
                    up, down = rad_above_ref[f, part, :], own(f, LV - 2)
                else:
                    up, down = rad_above_ref[f, CP + 8 * t : CP + 8 * t + 8, :], own(f, LV - 1)
                return up, down, line_ref[line + 1 : line + 9, :], line_ref[line - 1 : line + 7, :]

            center = [line_ref[(e * NF + f) * BLOCK + 8 + 8 * t : (e * NF + f) * BLOCK + 16 + 8 * t, :] for f in range(NF)]
            if e in (0, 3):
                source = radial[e // 3]
                rates = increments(center, neighbours, lambda f: source[f, 34:35, :], source[0, 35:36, :], step_size)
            else:
                r = (e - 1) * (LV - 1)
                rates = increments(
                    center, neighbours, lambda f: coef_ref[f, r : r + 1, :], coef_ref[NF, r : r + 1, :], step_size
                )
            for f in range(NF):
                value = center[f] + rates[f]
                if e in (0, 3):
                    value = keep_rad[e // 3] * value
                base = (e * 8 + f) * CP + 8 * t
                edge_ref[base : base + 8, :] = value
        edge_ref[(e * 8 + NF) * CP : (e * 8 + 8) * CP, :] = jnp.zeros((CP, LAT), F32)

    for side in range(2):
        for t in range(2):
            part = slice(8 * t, 8 * t + 8)

            def neighbours(f):
                column = (side * NF + f) * BLOCK + 8 + 8 * t
                near = state_ref[pl.ds(f * TILE + 8 * t * CP + side * (CP - 1), 8, CP), :]
                if side == 0:
                    east, west = near, below_ref[1, f, part, :]
                else:
                    east, west = above_ref[1, f, part, :], near
                return column_ref[column + 1 : column + 9, :], column_ref[column - 1 : column + 7, :], east, west

            center = [(below_ref[0, f, part, :] if side == 0 else above_ref[0, f, part, :]) for f in range(NF)]
            rates = increments(center, neighbours, lambda f: coef_ref[f, part, :], coef_ref[NF, part, :], step_size)
            for f in range(NF):
                ring_ref[side, f, part, :] = keep_ang[side] * (center[f] + rates[f])

    edges = interpolate(edge_ref[8 * CP : 24 * CP, :], lat_weight_ref, lon_weight_ref)
    send_ref[...] = jnp.transpose(jnp.concatenate([values_ref[...], edges], axis=0))


def received(place_ref, recv_ref):
    values = lax.dot_general(
        place_ref[...], recv_ref[...], (((0,), (0,)), ((), ())), precision=HIGHEST, preferred_element_type=F32
    )
    low, high = values[0:CP], pltpu.roll(values[CP : 2 * CP], LAT - 1, 1)
    even = (lax.broadcasted_iota(jnp.int32, (CP, LAT), 1) & 1) == 0
    return jnp.where(even, low, high), jnp.where(even, high, low)


def with_rows(own, values, point, ends):
    rows = values[point % 2]
    if point:
        rows = pltpu.roll(rows, LAT - point, 1)
    return jnp.where(ends, rows, own)


def ends_of():
    lane = lax.broadcasted_iota(jnp.int32, (CP, LAT), 1)
    return (lane == 0) | (lane == LAT - 1)


def second_kernel(
    state_ref, inner_ref, edge_ref, ring_ref, coef_ref, recv_ref, place_ref, lat_weight_ref, lon_weight_ref,
    next_ref, send_ref, line_ref,
):
    values = received(place_ref, recv_ref)
    ends = ends_of()
    for f in range(NF):
        for r in range(-1, LV + 1):
            base = (f * (LV + 2) + r + 1) * BLOCK + 8
            if 1 <= r <= LV - 2:
                own = inner_ref[f * TILE + r * CP : f * TILE + (r + 1) * CP, :]
                point = f * LV + r
            else:
                e = {-1: 0, 0: 1, LV - 1: 2, LV: 3}[r]
                own = edge_ref[(e * 8 + f) * CP : (e * 8 + f + 1) * CP, :]
                point = NF * LV + (e - 1) * 8 + f
            if 0 <= r <= LV - 1:
                own = with_rows(own, values, point, ends)
            line_ref[base : base + CP, :] = own
        start = (f * (LV + 2) + 1) * BLOCK
        line_ref[pl.ds(start + 7, LV, BLOCK), :] = ring_ref[0, f]
        line_ref[pl.ds(start + 24, LV, BLOCK), :] = ring_ref[1, f]

    for r in range(LV):
        for t in range(2):

            def line(f, level=r):
                return (f * (LV + 2) + level + 1) * BLOCK + 8 + 8 * t

            def neighbours(f):
                return (
                    line_ref[line(f, r + 1) : line(f, r + 1) + 8, :],
                    line_ref[line(f, r - 1) : line(f, r - 1) + 8, :],
                    line_ref[line(f) + 1 : line(f) + 9, :],
                    line_ref[line(f) - 1 : line(f) + 7, :],
                )

            center = [line_ref[line(f) : line(f) + 8, :] for f in range(NF)]
            rates = increments(
                center, neighbours, lambda f: coef_ref[f, r : r + 1, :], coef_ref[NF, r : r + 1, :], 0.5 * step_size
            )
            for f in range(NF):
                row = f * TILE + r * CP + 8 * t
                next_ref[row : row + 8, :] = 0.5 * (state_ref[row : row + 8, :] + center[f]) + rates[f]
    donors = interpolate(next_ref[...], lat_weight_ref, lon_weight_ref)
    send_ref[...] = jnp.transpose(jnp.concatenate([donors, jnp.zeros((128 - NF * LV, 128), F32)], axis=0))


def last_kernel(next_ref, recv_ref, place_ref, out_ref, done_ref, sems):
    values = received(place_ref, recv_ref)
    ends = ends_of()
    copies = []
    for f in range(NF):
        for r in range(LV):
            row = f * TILE + r * CP
            done_ref[row : row + CP, :] = with_rows(next_ref[row : row + CP, :], values, f * LV + r, ends)
        part = pl.ds(f * TILE, TILE)
        copies.append(pltpu.make_async_copy(done_ref.at[part, :], out_ref.at[part, :], sems.at[f]))
        copies[-1].start()
    for copy in copies:
        copy.wait()


def shift(value, axis, step):
    count = lax.axis_size(axis)
    pairs = [(i, i + step) for i in range(count) if 0 <= i + step < count]
    return lax.ppermute(value, axis, pairs)


def swap(value, axis, first):
    count = lax.axis_size(axis)
    low = range(first, count - 1, 2)
    return lax.ppermute(value, axis, [(i, i + 1) for i in low] + [(i + 1, i) for i in low])


def exchange(values):
    n = values.shape[0] // 2
    got = lax.all_to_all(values.reshape(n, 2, 128), ("panel", "ang"), 0, 0, tiled=True)
    return got.reshape(2 * n, 128)


def body(state, kappa, buoyancy, donor_lon, donor_lat, fractions):
    where = jnp.stack(
        [lax.axis_index(a) for a in ("panel", "rad", "ang")] + [lax.axis_size(a) for a in ("rad", "ang")]
    ).astype(jnp.int32)

    own = state.reshape(NF * TILE, LAT)
    outer, inner = pl.pallas_call(
        cut_kernel,
        out_shape=(shape(2, NF, LV, LAT),) * 2,
        in_specs=[SMEM, VMEM],
        out_specs=(VMEM,) * 2,
        compiler_params=params(),
        name="cut",
    )(where, own)
    outer = swap(outer, "ang", 1)
    inner = swap(inner, "ang", 0)

    coef = jnp.broadcast_to(jnp.concatenate([kappa, buoyancy[None]])[:, :, None], (NF + 1, LV, LAT))
    n_send = 4 * donor_lon.shape[1] // CP
    lat_weight, lon_weight, place = pl.pallas_call(
        tables_kernel,
        out_shape=(shape(LAT, n_send), shape(CP, n_send), shape(n_send, 128)),
        in_specs=[SMEM] + [VMEM] * 3,
        out_specs=(VMEM,) * 3,
        compiler_params=params(),
        cost_estimate=cost(4_000_000),
        name="tables",
    )(where, donor_lon, donor_lat, fractions)
    coef, lat_weight = lax.optimization_barrier((coef, lat_weight))

    up, down, below, above = pl.pallas_call(
        pack_kernel,
        out_shape=(shape(NF, MESSAGE, LAT),) * 2 + (shape(2, NF, LV, LAT),) * 2,
        in_specs=[SMEM] + [VMEM] * 4,
        out_specs=(VMEM,) * 4,
        compiler_params=params(),
        name="pack",
    )(where, own, outer, inner, coef)
    rad_below = shift(up, "rad", 1)
    rad_above = shift(down, "rad", -1)

    middle, middle_values = pl.pallas_call(
        first_a_kernel,
        out_shape=(shape(NF * TILE, LAT), shape(NF * LV, n_send)),
        in_specs=[VMEM] * 6,
        out_specs=(VMEM,) * 2,
        scratch_shapes=[pltpu.VMEM((NF * LV * BLOCK + 8, LAT), F32)],
        compiler_params=params(),
        cost_estimate=cost(60_000_000),
        name="first_a",
    )(own, below, above, coef, lat_weight, lon_weight)
    edge, ring, out = pl.pallas_call(
        first_b_kernel,
        out_shape=(shape(4 * 8 * CP, LAT), shape(2, NF, LV, LAT), shape(n_send, 128)),
        in_specs=[SMEM] + [VMEM] * 9,
        out_specs=(VMEM,) * 3,
        scratch_shapes=[
            pltpu.VMEM((4 * NF * BLOCK + 8, LAT), F32),
            pltpu.VMEM((2 * NF * BLOCK + 8, LAT), F32),
        ],
        compiler_params=params(),
        name="first_b",
    )(where, own, below, above, coef, rad_below, rad_above, lat_weight, lon_weight, middle_values)
    got = exchange(out)
    following, out = pl.pallas_call(
        second_kernel,
        out_shape=(shape(NF * TILE, LAT), shape(n_send, 128)),
        in_specs=[VMEM] * 9,
        out_specs=(VMEM,) * 2,
        scratch_shapes=[pltpu.VMEM((NF * (LV + 2) * BLOCK + 8, LAT), F32)],
        compiler_params=params(),
        name="second",
    )(own, middle, edge, ring, coef, got, place, lat_weight, lon_weight)
    got = exchange(out)
    result = pl.pallas_call(
        last_kernel,
        out_shape=shape(NF * TILE, LAT),
        in_specs=[VMEM] * 3,
        out_specs=pl.BlockSpec(memory_space=pl.ANY),
        scratch_shapes=[pltpu.VMEM((NF * TILE, LAT), F32), pltpu.SemaphoreType.DMA((NF,))],
        compiler_params=params(),
        name="last",
    )(following, got, place)
    return result.reshape(state.shape)


def solution(mesh):
    return jax.shard_map(
        body,
        mesh=mesh,
        in_specs=(P("panel", None, "rad", "ang", None), P(None, "rad"), P("rad"), P(), P(), P()),
        out_specs=P("panel", None, "rad", "ang", None),
        check_vma=False,
    )
```

```python
import jax
import jax.numpy as jnp
from jax import lax
from jax.experimental import pallas as pl
from jax.experimental.pallas import tpu as pltpu
from jax.sharding import PartitionSpec as P

step_size = 0.1
HIGHEST = lax.Precision.HIGHEST
VMEM = pl.BlockSpec(memory_space=pltpu.VMEM)
F32 = jnp.float32

NF = 7
LV = 16
CP = 16
LAT = 128
TILE = LV * CP
BLOCK = 24
LATE = 24


def params():
    return pltpu.CompilerParams(vmem_limit_bytes=40 * 1024 * 1024)


def cost(flops):
    return pl.CostEstimate(flops=flops, bytes_accessed=2_000_000, transcendentals=0)


def shape(*dims):
    return jax.ShapeDtypeStruct(dims, F32)


def picks(match, kid, slot):
    low = jnp.min(jnp.where(match, kid, 4096.0), axis=1, keepdims=True)
    high = jnp.max(jnp.where(match, kid, -1.0), axis=1, keepdims=True)
    low_or_none = jnp.where(low < 4096.0, low, -8.0)
    high_or_none = jnp.where(high > low, high, -8.0)
    return jnp.where(slot == 0, low_or_none, high_or_none)


def tables_kernel(lon_ref, lat_ref, frac_ref, lat_weight_ref, lon_weight_ref, place_ref):
    nlon = lon_ref.shape[1]
    half = 2 * nlon // CP
    points = 2 * nlon
    panel = lax.axis_index("panel")
    tile = lax.axis_index("ang")

    def flat(low, high):
        return jnp.concatenate([low, high], axis=1)

    lon_k = flat(lon_ref[0:1, :], lon_ref[1:2, :])
    owner_k = lon_k >> 4
    off_k = (lon_k & 15).astype(F32)
    lat_k = flat(lat_ref[0:1, :], lat_ref[1:2, :]).astype(F32)
    fx_k = flat(frac_ref[0, 0:1, :], frac_ref[0, 1:2, :])
    fy_k = flat(frac_ref[1, 0:1, :], frac_ref[1, 1:2, :])

    kid = lax.broadcasted_iota(jnp.int32, (1, points), 1)
    dest_k = (kid & (nlon - 1)) >> 4
    kid = kid.astype(F32)

    row = lax.broadcasted_iota(jnp.int32, (half, 1), 0)
    match = (dest_k == (row >> 1)) & (owner_k == tile)
    pick = picks(match, kid, row & 1)
    chosen = kid == pick

    def of(value):
        return jnp.sum(jnp.where(chosen, value, 0.0), axis=1, keepdims=True)

    off, lat, fx, fy = of(off_k), of(lat_k), of(fx_k), of(fy_k)
    lane = lax.broadcasted_iota(jnp.int32, (half, LAT), 1).astype(F32)
    lat_weight = jnp.where(lane == lat, 1.0 - fy, 0.0) + jnp.where(lane == lat + 1.0, fy, 0.0)
    lat_weight = jnp.where(pick >= 0.0, lat_weight, 0.0)
    lon_weight = jnp.where(lane == off, 1.0 - fx, 0.0) + jnp.where(lane == off + 1.0, fx, 0.0)
    lat_weight_ref[...] = jnp.transpose(jnp.concatenate([lat_weight, lat_weight], axis=0))
    lon_weight_ref[...] = jnp.transpose(jnp.concatenate([lon_weight, lon_weight], axis=0))[0:CP]

    row = lax.broadcasted_iota(jnp.int32, (half, 1), 0)
    match = (owner_k == (row >> 1)) & (dest_k == tile)
    pick = picks(match, kid, row & 1).astype(jnp.int32)
    target = ((pick >> (nlon.bit_length() - 1)) << 4) + (pick & 15)
    target = jnp.where(pick >= 0, target, -1)
    lane = lax.broadcasted_iota(jnp.int32, (half, 128), 1)
    place = jnp.where(lane == target, 1.0, 0.0)
    place_ref[0:half, :] = place * panel.astype(F32)
    place_ref[half : 2 * half, :] = place * (1 - panel).astype(F32)


def increments(center, neighbours, kappa, buoyancy, scale):
    u = [(0.5 * scale) * center[d] for d in range(3)]
    b = [(0.5 * scale) * center[3 + d] for d in range(3)]
    lap, adv, mag = [], [], []
    for f in range(NF):
        up, down, east, west = neighbours(f)
        north = pltpu.roll(center[f], LAT - 1, 1)
        south = pltpu.roll(center[f], 1, 1)
        diffs = [up - down, east - west, north - south]
        lap.append((scale * kappa(f)) * ((up + down) + (east + west) + (north + south) - 6.0 * center[f]))
        adv.append(u[0] * diffs[0] + u[1] * diffs[1] + u[2] * diffs[2])
        if f < 6:
            mag.append(b[0] * diffs[0] + b[1] * diffs[1] + b[2] * diffs[2])
    rates = [lap[f] - adv[f] + mag[(f + 3) % 6] for f in range(6)] + [lap[6] - adv[6]]
    rates[0] = rates[0] + (scale * buoyancy) * center[6]
    return rates


def interpolate(rows, lat_weight_ref, lon_weight_ref):
    along = jnp.dot(rows, lat_weight_ref[...], precision=HIGHEST, preferred_element_type=F32)
    n = rows.shape[0] // CP
    return jnp.sum(along.reshape(n, CP, along.shape[1]) * lon_weight_ref[...][None], axis=1)


def cut_kernel(state_ref, outer_ref, inner_ref, up_ref, down_ref):
    odd = lax.axis_index("ang") % 2 == 1
    for f in range(NF):
        for i in range(2):
            low = state_ref[pl.ds(f * TILE + i, LV, CP), :]
            high = state_ref[pl.ds(f * TILE + CP - 1 - i, LV, CP), :]
            outer_ref[i, f] = jnp.where(odd, high, low)
            inner_ref[i, f] = jnp.where(odd, low, high)
        up_ref[f] = state_ref[(f + 1) * TILE - CP : (f + 1) * TILE, :]
        down_ref[f] = state_ref[f * TILE : f * TILE + CP, :]


def pack_kernel(state_ref, outer_ref, inner_ref, coef_ref, up_ref, down_ref, below_ref, above_ref):
    odd = lax.axis_index("ang") % 2 == 1
    for i in range(2):
        for f in range(NF):
            above_ref[i, f] = jnp.where(odd, outer_ref[i, f], inner_ref[i, f])
            below_ref[i, f] = jnp.where(odd, inner_ref[i, f], outer_ref[i, f])
    for ref, near, far in ((up_ref, LV - 1, LV - 2), (down_ref, 0, 1)):
        for f in range(NF):
            start = f * TILE
            ref[f, 0:CP, :] = state_ref[start + far * CP : start + (far + 1) * CP, :]
            ref[f, 16:17, :] = above_ref[0, f, near : near + 1, :]
            ref[f, 17:18, :] = below_ref[0, f, near : near + 1, :]
            ref[f, 18:19, :] = coef_ref[f, near : near + 1, :]
            ref[f, 19:20, :] = coef_ref[NF, near : near + 1, :]
            ref[f, 20:24, :] = jnp.zeros((4, LAT), F32)


def first_a_kernel(
    state_ref, below_ref, above_ref, coef_ref, lat_weight_ref, lon_weight_ref, inner_ref, values_ref, line_ref
):
    for f in range(NF):
        for r in range(LV):
            base = (f * LV + r) * BLOCK + 8
            line_ref[base : base + CP, :] = state_ref[f * TILE + r * CP : f * TILE + (r + 1) * CP, :]
        line_ref[pl.ds(f * LV * BLOCK + 7, LV, BLOCK), :] = below_ref[0, f]
        line_ref[pl.ds(f * LV * BLOCK + 24, LV, BLOCK), :] = above_ref[0, f]
        for r in (0, LV - 1):
            inner_ref[f * TILE + r * CP : f * TILE + (r + 1) * CP, :] = jnp.zeros((CP, LAT), F32)
    for r in range(1, LV - 1):
        for t in range(2):

            def row(f, level=r):
                return f * TILE + level * CP + 8 * t

            def neighbours(f):
                line = (f * LV + r) * BLOCK + 8 + 8 * t
                return (
                    state_ref[row(f, r + 1) : row(f, r + 1) + 8, :],
                    state_ref[row(f, r - 1) : row(f, r - 1) + 8, :],
                    line_ref[line + 1 : line + 9, :],
                    line_ref[line - 1 : line + 7, :],
                )

            center = [state_ref[row(f) : row(f) + 8, :] for f in range(NF)]
            rates = increments(
                center, neighbours, lambda f: coef_ref[f, r : r + 1, :], coef_ref[NF, r : r + 1, :], step_size
            )
            for f in range(NF):
                inner_ref[row(f) : row(f) + 8, :] = center[f] + rates[f]
    values_ref[...] = interpolate(inner_ref[...], lat_weight_ref, lon_weight_ref)


def first_b_kernel(
    state_ref, below_ref, above_ref, coef_ref, near_below_ref, near_above_ref, lat_weight_ref, lon_weight_ref,
    values_ref, edge_ref, send_ref, line_ref,
):
    for e, r in enumerate((0, LV - 1)):
        for f in range(NF):
            base = (e * NF + f) * BLOCK + 8
            line_ref[base : base + CP, :] = state_ref[f * TILE + r * CP : f * TILE + (r + 1) * CP, :]
            line_ref[base - 1 : base, :] = below_ref[0, f, r : r + 1, :]
            line_ref[base + CP : base + CP + 1, :] = above_ref[0, f, r : r + 1, :]
    for e, r in enumerate((0, LV - 1)):
        for t in range(2):

            def own(f, level):
                return state_ref[f * TILE + level * CP + 8 * t : f * TILE + level * CP + 8 * t + 8, :]

            def neighbours(f):
                line = (e * NF + f) * BLOCK + 8 + 8 * t
                if e == 0:
                    up, down = own(f, 1), near_below_ref[f, 8 * t : 8 * t + 8, :]
                else:
                    up, down = near_above_ref[f, 8 * t : 8 * t + 8, :], own(f, LV - 2)
                return up, down, line_ref[line + 1 : line + 9, :], line_ref[line - 1 : line + 7, :]

            center = [own(f, r) for f in range(NF)]
            rates = increments(
                center, neighbours, lambda f: coef_ref[f, r : r + 1, :], coef_ref[NF, r : r + 1, :], step_size
            )
            for f in range(NF):
                base = (e * 8 + f) * CP + 8 * t
                edge_ref[base : base + 8, :] = center[f] + rates[f]
        edge_ref[(e * 8 + NF) * CP : (e * 8 + 8) * CP, :] = jnp.zeros((CP, LAT), F32)
    edges = interpolate(edge_ref[...], lat_weight_ref, lon_weight_ref)
    send_ref[...] = jnp.transpose(jnp.concatenate([values_ref[...], edges], axis=0))


def surround(
    state_ref, below_ref, above_ref, coef_ref, near_refs, late_refs, work_ref, column_ref, line_ref
):
    rad, ang = lax.axis_index("rad"), lax.axis_index("ang")
    keep_rad = [jnp.where(rad == 0, 0.0, 1.0), jnp.where(rad == lax.axis_size("rad") - 1, 0.0, 1.0)]
    keep_ang = [jnp.where(ang == 0, 0.0, 1.0), jnp.where(ang == lax.axis_size("ang") - 1, 0.0, 1.0)]
    for e in range(2):
        late = late_refs[e]
        for f in range(NF):
            base = (e * NF + f) * BLOCK + 8
            work_ref[base : base + CP, :] = near_refs[e][f]
            work_ref[base - 1 : base, :] = late[f, 17:18, :]
            work_ref[base + CP : base + CP + 1, :] = late[f, 16:17, :]
    for side, ref in ((0, below_ref), (1, above_ref)):
        for f in range(NF):
            base = (side * NF + f) * BLOCK + 8
            column_ref[base : base + LV, :] = ref[0, f]
            column_ref[base - 1 : base, :] = late_refs[0][f, 17 - side : 18 - side, :]
            column_ref[base + LV : base + LV + 1, :] = late_refs[1][f, 17 - side : 18 - side, :]

    for e in range(2):
        late = late_refs[e]
        for t in range(2):
            part = slice(8 * t, 8 * t + 8)

            def neighbours(f):
                line = (e * NF + f) * BLOCK + 8 + 8 * t
                start = f * TILE + e * (LV - 1) * CP + 8 * t
                inside, outside = state_ref[start : start + 8, :], late[f, part, :]
                up, down = (inside, outside) if e == 0 else (outside, inside)
                return up, down, work_ref[line + 1 : line + 9, :], work_ref[line - 1 : line + 7, :]

            center = [near_refs[e][f, part, :] for f in range(NF)]
            rates = increments(center, neighbours, lambda f: late[f, 18:19, :], late[0, 19:20, :], step_size)
            for f in range(NF):
                base = (f * (LV + 2) + e * (LV + 1)) * BLOCK + 8 + 8 * t
                line_ref[base : base + 8, :] = keep_rad[e] * (center[f] + rates[f])

    for side, ref in ((0, below_ref), (1, above_ref)):
        for t in range(2):
            part = slice(8 * t, 8 * t + 8)

            def neighbours(f):
                column = (side * NF + f) * BLOCK + 8 + 8 * t
                inside = state_ref[pl.ds(f * TILE + 8 * t * CP + side * (CP - 1), 8, CP), :]
                outside = ref[1, f, part, :]
                east, west = (inside, outside) if side == 0 else (outside, inside)
                return column_ref[column + 1 : column + 9, :], column_ref[column - 1 : column + 7, :], east, west

            center = [ref[0, f, part, :] for f in range(NF)]
            rates = increments(center, neighbours, lambda f: coef_ref[f, part, :], coef_ref[NF, part, :], step_size)
            for f in range(NF):
                start = (f * (LV + 2) + 1 + 8 * t) * BLOCK + (7 if side == 0 else 24)
                line_ref[pl.ds(start, 8, BLOCK), :] = keep_ang[side] * (center[f] + rates[f])


def received(place_ref, recv_ref):
    values = lax.dot_general(
        place_ref[...], recv_ref[...], (((0,), (0,)), ((), ())), precision=HIGHEST, preferred_element_type=F32
    )
    low, high = values[0:CP], pltpu.roll(values[CP : 2 * CP], LAT - 1, 1)
    even = (lax.broadcasted_iota(jnp.int32, (CP, LAT), 1) & 1) == 0
    return jnp.where(even, low, high), jnp.where(even, high, low)


def with_rows(own, values, point, ends):
    rows = values[point % 2]
    if point:
        rows = pltpu.roll(rows, LAT - point, 1)
    return jnp.where(ends, rows, own)


def ends_of():
    lane = lax.broadcasted_iota(jnp.int32, (CP, LAT), 1)
    return (lane == 0) | (lane == LAT - 1)


def second_kernel(
    state_ref, below_ref, above_ref, coef_ref, near_below_ref, near_above_ref, late_below_ref, late_above_ref,
    inner_ref, edge_ref, recv_ref, place_ref, lat_weight_ref, lon_weight_ref, next_ref, send_ref,
    line_ref, work_ref, column_ref,
):
    values = received(place_ref, recv_ref)
    ends = ends_of()
    for f in range(NF):
        for r in range(LV):
            base = (f * (LV + 2) + r + 1) * BLOCK + 8
            if 1 <= r <= LV - 2:
                own = inner_ref[f * TILE + r * CP : f * TILE + (r + 1) * CP, :]
                point = f * LV + r
            else:
                e = r // (LV - 1)
                own = edge_ref[(e * 8 + f) * CP : (e * 8 + f + 1) * CP, :]
                point = NF * LV + e * 8 + f
            line_ref[base : base + CP, :] = with_rows(own, values, point, ends)
    surround(
        state_ref, below_ref, above_ref, coef_ref, (near_below_ref, near_above_ref), (late_below_ref, late_above_ref),
        work_ref, column_ref, line_ref,
    )

    for r in range(LV):
        for t in range(2):

            def line(f, level=r):
                return (f * (LV + 2) + level + 1) * BLOCK + 8 + 8 * t

            def neighbours(f):
                return (
                    line_ref[line(f, r + 1) : line(f, r + 1) + 8, :],
                    line_ref[line(f, r - 1) : line(f, r - 1) + 8, :],
                    line_ref[line(f) + 1 : line(f) + 9, :],
                    line_ref[line(f) - 1 : line(f) + 7, :],
                )

            center = [line_ref[line(f) : line(f) + 8, :] for f in range(NF)]
            rates = increments(
                center, neighbours, lambda f: coef_ref[f, r : r + 1, :], coef_ref[NF, r : r + 1, :], 0.5 * step_size
            )
            for f in range(NF):
                row = f * TILE + r * CP + 8 * t
                next_ref[row : row + 8, :] = 0.5 * (state_ref[row : row + 8, :] + center[f]) + rates[f]
    donors = interpolate(next_ref[...], lat_weight_ref, lon_weight_ref)
    send_ref[...] = jnp.transpose(jnp.concatenate([donors, jnp.zeros((128 - NF * LV, 128), F32)], axis=0))


def last_kernel(next_ref, recv_ref, place_ref, out_ref, done_ref, sems):
    values = received(place_ref, recv_ref)
    ends = ends_of()
    copies = []
    for f in range(NF):
        for r in range(LV):
            row = f * TILE + r * CP
            done_ref[row : row + CP, :] = with_rows(next_ref[row : row + CP, :], values, f * LV + r, ends)
        part = pl.ds(f * TILE, TILE)
        copies.append(pltpu.make_async_copy(done_ref.at[part, :], out_ref.at[part, :], sems.at[f]))
        copies[-1].start()
    for copy in copies:
        copy.wait()


def shift(value, axis, step):
    count = lax.axis_size(axis)
    pairs = [(i, i + step) for i in range(count) if 0 <= i + step < count]
    return lax.ppermute(value, axis, pairs)


def swap(value, axis, first):
    count = lax.axis_size(axis)
    low = range(first, count - 1, 2)
    return lax.ppermute(value, axis, [(i, i + 1) for i in low] + [(i + 1, i) for i in low])


def exchange(values):
    n = values.shape[0] // 2
    got = lax.all_to_all(values.reshape(n, 2, 128), ("panel", "ang"), 0, 0, tiled=True)
    return got.reshape(2 * n, 128)


def call(kernel, name, outs, scratch, flops, *operands):
    return pl.pallas_call(
        kernel,
        out_shape=outs,
        in_specs=[VMEM] * len(operands),
        out_specs=(VMEM,) * len(outs),
        scratch_shapes=scratch,
        compiler_params=params(),
        cost_estimate=cost(flops),
        name=name,
    )(*operands)


def rows(count):
    return pltpu.VMEM((count, LAT), F32)


def body(state, kappa, buoyancy, donor_lon, donor_lat, fractions):
    n_send = 4 * donor_lon.shape[1] // CP
    own = state.reshape(NF * TILE, LAT)
    halo, level, late = shape(2, NF, LV, LAT), shape(NF, CP, LAT), shape(NF, LATE, LAT)

    outer, inner, up, down = call(cut_kernel, "cut", (halo, halo, level, level), [], 100_000, own)
    outer = swap(outer, "ang", 1)
    inner = swap(inner, "ang", 0)
    near_below = shift(up, "rad", 1)
    near_above = shift(down, "rad", -1)

    coef = jnp.broadcast_to(jnp.concatenate([kappa, buoyancy[None]])[:, :, None], (NF + 1, LV, LAT))
    lat_weight, lon_weight, place = call(
        tables_kernel, "tables", (shape(LAT, n_send), shape(CP, n_send), shape(n_send, 128)), [], 4_000_000,
        donor_lon, donor_lat, fractions,
    )
    coef, lat_weight = lax.optimization_barrier((coef, lat_weight))

    up, down, below, above = call(
        pack_kernel, "pack", (late, late, halo, halo), [], 100_000, own, outer, inner, coef
    )
    late_below = shift(up, "rad", 1)
    late_above = shift(down, "rad", -1)
    middle, values = call(
        first_a_kernel, "first_a", (shape(NF * TILE, LAT), shape(NF * LV, n_send)), [rows(NF * LV * BLOCK + 8)],
        60_000_000, own, below, above, coef, lat_weight, lon_weight,
    )
    edge, out = call(
        first_b_kernel, "first_b", (shape(2 * 8 * CP, LAT), shape(n_send, 128)), [rows(2 * NF * BLOCK + 8)],
        10_000_000, own, below, above, coef, near_below, near_above, lat_weight, lon_weight, values,
    )
    got = exchange(out)
    following, out = call(
        second_kernel, "second", (shape(NF * TILE, LAT), shape(n_send, 128)),
        [rows(NF * (LV + 2) * BLOCK + 8), rows(2 * NF * BLOCK + 8), rows(2 * NF * BLOCK + 8)], 60_000_000,
        own, below, above, coef, near_below, near_above, late_below, late_above, middle, edge, got, place,
        lat_weight, lon_weight,
    )
    got = exchange(out)
    result = pl.pallas_call(
        last_kernel,
        out_shape=shape(NF * TILE, LAT),
        in_specs=[VMEM] * 3,
        out_specs=pl.BlockSpec(memory_space=pl.ANY),
        scratch_shapes=[rows(NF * TILE), pltpu.SemaphoreType.DMA((NF,))],
        compiler_params=params(),
        name="last",
    )(following, got, place)
    return result.reshape(state.shape)


def solution(mesh):
    return jax.shard_map(
        body,
        mesh=mesh,
        in_specs=(P("panel", None, "rad", "ang", None), P(None, "rad"), P("rad"), P(), P(), P()),
        out_specs=P("panel", None, "rad", "ang", None),
        check_vma=False,
    )
```

```python
import jax
import jax.numpy as jnp
from jax import lax
from jax.experimental import pallas as pl
from jax.experimental.pallas import tpu as pltpu
from jax.sharding import PartitionSpec as P

step_size = 0.1
HIGHEST = lax.Precision.HIGHEST
VMEM = pl.BlockSpec(memory_space=pltpu.VMEM)
F32 = jnp.float32

NF = 7
LV = 16
CP = 16
LAT = 128
TILE = LV * CP
BLOCK = 24
MESSAGE = 40


def params():
    return pltpu.CompilerParams(vmem_limit_bytes=40 * 1024 * 1024)


def cost(flops):
    return pl.CostEstimate(flops=flops, bytes_accessed=2_000_000, transcendentals=0)


def shape(*dims):
    return jax.ShapeDtypeStruct(dims, F32)


def picks(match, kid, slot):
    low = jnp.min(jnp.where(match, kid, 4096.0), axis=1, keepdims=True)
    high = jnp.max(jnp.where(match, kid, -1.0), axis=1, keepdims=True)
    low_or_none = jnp.where(low < 4096.0, low, -8.0)
    high_or_none = jnp.where(high > low, high, -8.0)
    return jnp.where(slot == 0, low_or_none, high_or_none)


def tables_kernel(lon_ref, lat_ref, frac_ref, lat_weight_ref, lon_weight_ref, place_ref):
    nlon = lon_ref.shape[1]
    half = 2 * nlon // CP
    points = 2 * nlon
    panel = lax.axis_index("panel")
    tile = lax.axis_index("ang")

    def flat(low, high):
        return jnp.concatenate([low, high], axis=1)

    lon_k = flat(lon_ref[0:1, :], lon_ref[1:2, :])
    owner_k = lon_k >> 4
    off_k = (lon_k & 15).astype(F32)
    lat_k = flat(lat_ref[0:1, :], lat_ref[1:2, :]).astype(F32)
    fx_k = flat(frac_ref[0, 0:1, :], frac_ref[0, 1:2, :])
    fy_k = flat(frac_ref[1, 0:1, :], frac_ref[1, 1:2, :])

    kid = lax.broadcasted_iota(jnp.int32, (1, points), 1)
    dest_k = (kid & (nlon - 1)) >> 4
    kid = kid.astype(F32)

    row = lax.broadcasted_iota(jnp.int32, (half, 1), 0)
    match = (dest_k == (row >> 1)) & (owner_k == tile)
    pick = picks(match, kid, row & 1)
    chosen = kid == pick

    def of(value):
        return jnp.sum(jnp.where(chosen, value, 0.0), axis=1, keepdims=True)

    off, lat, fx, fy = of(off_k), of(lat_k), of(fx_k), of(fy_k)
    lane = lax.broadcasted_iota(jnp.int32, (half, LAT), 1).astype(F32)
    lat_weight = jnp.where(lane == lat, 1.0 - fy, 0.0) + jnp.where(lane == lat + 1.0, fy, 0.0)
    lat_weight = jnp.where(pick >= 0.0, lat_weight, 0.0)
    lon_weight = jnp.where(lane == off, 1.0 - fx, 0.0) + jnp.where(lane == off + 1.0, fx, 0.0)
    lat_weight_ref[...] = jnp.transpose(jnp.concatenate([lat_weight, lat_weight], axis=0))
    lon_weight_ref[...] = jnp.transpose(jnp.concatenate([lon_weight, lon_weight], axis=0))[0:CP]

    row = lax.broadcasted_iota(jnp.int32, (half, 1), 0)
    match = (owner_k == (row >> 1)) & (dest_k == tile)
    pick = picks(match, kid, row & 1).astype(jnp.int32)
    target = ((pick >> (nlon.bit_length() - 1)) << 4) + (pick & 15)
    target = jnp.where(pick >= 0, target, -1)
    lane = lax.broadcasted_iota(jnp.int32, (half, 128), 1)
    place = jnp.where(lane == target, 1.0, 0.0)
    place = jnp.concatenate([place * panel.astype(F32), place * (1 - panel).astype(F32)], axis=0)
    place_ref[...] = jnp.transpose(place)[0 : 2 * CP]


def increments(center, neighbours, kappa, buoyancy, scale):
    u = [(0.5 * scale) * center[d] for d in range(3)]
    b = [(0.5 * scale) * center[3 + d] for d in range(3)]
    lap, adv, mag = [], [], []
    for f in range(NF):
        up, down, east, west = neighbours(f)
        north = pltpu.roll(center[f], LAT - 1, 1)
        south = pltpu.roll(center[f], 1, 1)
        diffs = [up - down, east - west, north - south]
        lap.append((scale * kappa(f)) * ((up + down) + (east + west) + (north + south) - 6.0 * center[f]))
        adv.append(u[0] * diffs[0] + u[1] * diffs[1] + u[2] * diffs[2])
        if f < 6:
            mag.append(b[0] * diffs[0] + b[1] * diffs[1] + b[2] * diffs[2])
    rates = [lap[f] - adv[f] + mag[(f + 3) % 6] for f in range(6)] + [lap[6] - adv[6]]
    rates[0] = rates[0] + (scale * buoyancy) * center[6]
    return rates


def interpolate(rows, lat_weight_ref, lon_weight_ref):
    along = jnp.dot(rows, lat_weight_ref[...], precision=HIGHEST, preferred_element_type=F32)
    n = rows.shape[0] // CP
    return jnp.sum(along.reshape(n, CP, along.shape[1]) * lon_weight_ref[...][None], axis=1)


def cut_kernel(state_ref, outer_ref, inner_ref):
    odd = lax.axis_index("ang") % 2 == 1
    for f in range(NF):
        for i in range(2):
            low = state_ref[pl.ds(f * TILE + i, LV, CP), :]
            high = state_ref[pl.ds(f * TILE + CP - 1 - i, LV, CP), :]
            outer_ref[i, f] = jnp.where(odd, high, low)
            inner_ref[i, f] = jnp.where(odd, low, high)


def pack_kernel(state_ref, outer_ref, inner_ref, coef_ref, up_ref, down_ref, below_ref, above_ref):
    odd = lax.axis_index("ang") % 2 == 1
    for i in range(2):
        for f in range(NF):
            above_ref[i, f] = jnp.where(odd, outer_ref[i, f], inner_ref[i, f])
            below_ref[i, f] = jnp.where(odd, inner_ref[i, f], outer_ref[i, f])
    for ref, near, far in ((up_ref, LV - 1, LV - 2), (down_ref, 0, 1)):
        for f in range(NF):
            start = f * TILE
            ref[f, 0:CP, :] = state_ref[start + near * CP : start + (near + 1) * CP, :]
            ref[f, CP : 2 * CP, :] = state_ref[start + far * CP : start + (far + 1) * CP, :]
            ref[f, 32:33, :] = above_ref[0, f, near : near + 1, :]
            ref[f, 33:34, :] = below_ref[0, f, near : near + 1, :]
            ref[f, 34:35, :] = coef_ref[f, near : near + 1, :]
            ref[f, 35:36, :] = coef_ref[NF, near : near + 1, :]
            ref[f, 36:40, :] = jnp.zeros((4, LAT), F32)


def first_a_kernel(
    state_ref, below_ref, above_ref, coef_ref, lat_weight_ref, lon_weight_ref, inner_ref, values_ref, line_ref
):
    for f in range(NF):
        for r in range(LV):
            base = (f * LV + r) * BLOCK + 8
            line_ref[base : base + CP, :] = state_ref[f * TILE + r * CP : f * TILE + (r + 1) * CP, :]
        line_ref[pl.ds(f * LV * BLOCK + 7, LV, BLOCK), :] = below_ref[0, f]
        line_ref[pl.ds(f * LV * BLOCK + 24, LV, BLOCK), :] = above_ref[0, f]
        for r in (0, LV - 1):
            inner_ref[f * TILE + r * CP : f * TILE + (r + 1) * CP, :] = jnp.zeros((CP, LAT), F32)
    for r in range(1, LV - 1):
        for t in range(2):

            def row(f, level=r):
                return f * TILE + level * CP + 8 * t

            def neighbours(f):
                line = (f * LV + r) * BLOCK + 8 + 8 * t
                return (
                    state_ref[row(f, r + 1) : row(f, r + 1) + 8, :],
                    state_ref[row(f, r - 1) : row(f, r - 1) + 8, :],
                    line_ref[line + 1 : line + 9, :],
                    line_ref[line - 1 : line + 7, :],
                )

            center = [state_ref[row(f) : row(f) + 8, :] for f in range(NF)]
            rates = increments(
                center, neighbours, lambda f: coef_ref[f, r : r + 1, :], coef_ref[NF, r : r + 1, :], step_size
            )
            for f in range(NF):
                inner_ref[row(f) : row(f) + 8, :] = center[f] + rates[f]
    values_ref[...] = interpolate(inner_ref[...], lat_weight_ref, lon_weight_ref)


def first_b_kernel(
    state_ref, below_ref, above_ref, coef_ref, rad_below_ref, rad_above_ref, lat_weight_ref, lon_weight_ref,
    values_ref, edge_ref, send_ref, line_ref,
):
    for e, r in enumerate((0, LV - 1)):
        for f in range(NF):
            base = (e * NF + f) * BLOCK + 8
            line_ref[base : base + CP, :] = state_ref[f * TILE + r * CP : f * TILE + (r + 1) * CP, :]
            line_ref[base - 1 : base, :] = below_ref[0, f, r : r + 1, :]
            line_ref[base + CP : base + CP + 1, :] = above_ref[0, f, r : r + 1, :]
    for e, r in enumerate((0, LV - 1)):
        for t in range(2):

            def own(f, level):
                return state_ref[f * TILE + level * CP + 8 * t : f * TILE + level * CP + 8 * t + 8, :]

            def neighbours(f):
                line = (e * NF + f) * BLOCK + 8 + 8 * t
                if e == 0:
                    up, down = own(f, 1), rad_below_ref[f, 8 * t : 8 * t + 8, :]
                else:
                    up, down = rad_above_ref[f, 8 * t : 8 * t + 8, :], own(f, LV - 2)
                return up, down, line_ref[line + 1 : line + 9, :], line_ref[line - 1 : line + 7, :]

            center = [own(f, r) for f in range(NF)]
            rates = increments(
                center, neighbours, lambda f: coef_ref[f, r : r + 1, :], coef_ref[NF, r : r + 1, :], step_size
            )
            for f in range(NF):
                base = (e * 8 + f) * CP + 8 * t
                edge_ref[base : base + 8, :] = center[f] + rates[f]
        edge_ref[(e * 8 + NF) * CP : (e * 8 + 8) * CP, :] = jnp.zeros((CP, LAT), F32)
    edges = interpolate(edge_ref[...], lat_weight_ref, lon_weight_ref)
    send_ref[...] = jnp.transpose(jnp.concatenate([values_ref[...], edges], axis=0))


def surround(
    state_ref, below_ref, above_ref, coef_ref, rad_refs, work_ref, column_ref, line_ref
):
    rad, ang = lax.axis_index("rad"), lax.axis_index("ang")
    keep_rad = [jnp.where(rad == 0, 0.0, 1.0), jnp.where(rad == lax.axis_size("rad") - 1, 0.0, 1.0)]
    keep_ang = [jnp.where(ang == 0, 0.0, 1.0), jnp.where(ang == lax.axis_size("ang") - 1, 0.0, 1.0)]
    for e in range(2):
        source = rad_refs[e]
        for f in range(NF):
            base = (e * NF + f) * BLOCK + 8
            work_ref[base : base + CP, :] = source[f, 0:CP, :]
            work_ref[base - 1 : base, :] = source[f, 33:34, :]
            work_ref[base + CP : base + CP + 1, :] = source[f, 32:33, :]
    for side, ref in ((0, below_ref), (1, above_ref)):
        for f in range(NF):
            base = (side * NF + f) * BLOCK + 8
            column_ref[base : base + LV, :] = ref[0, f]
            column_ref[base - 1 : base, :] = rad_refs[0][f, 33 - side : 34 - side, :]
            column_ref[base + LV : base + LV + 1, :] = rad_refs[1][f, 33 - side : 34 - side, :]

    for e in range(2):
        source = rad_refs[e]
        for t in range(2):
            part = slice(8 * t, 8 * t + 8)

            def neighbours(f):
                line = (e * NF + f) * BLOCK + 8 + 8 * t
                start = f * TILE + e * (LV - 1) * CP + 8 * t
                inside, outside = state_ref[start : start + 8, :], source[f, CP + 8 * t : CP + 8 * t + 8, :]
                up, down = (inside, outside) if e == 0 else (outside, inside)
                return up, down, work_ref[line + 1 : line + 9, :], work_ref[line - 1 : line + 7, :]

            center = [source[f, part, :] for f in range(NF)]
            rates = increments(center, neighbours, lambda f: source[f, 34:35, :], source[0, 35:36, :], step_size)
            for f in range(NF):
                base = (f * (LV + 2) + e * (LV + 1)) * BLOCK + 8 + 8 * t
                line_ref[base : base + 8, :] = keep_rad[e] * (center[f] + rates[f])

    for side, ref in ((0, below_ref), (1, above_ref)):
        for t in range(2):
            part = slice(8 * t, 8 * t + 8)

            def neighbours(f):
                column = (side * NF + f) * BLOCK + 8 + 8 * t
                inside = state_ref[pl.ds(f * TILE + 8 * t * CP + side * (CP - 1), 8, CP), :]
                outside = ref[1, f, part, :]
                east, west = (inside, outside) if side == 0 else (outside, inside)
                return column_ref[column + 1 : column + 9, :], column_ref[column - 1 : column + 7, :], east, west

            center = [ref[0, f, part, :] for f in range(NF)]
            rates = increments(center, neighbours, lambda f: coef_ref[f, part, :], coef_ref[NF, part, :], step_size)
            for f in range(NF):
                start = (f * (LV + 2) + 1 + 8 * t) * BLOCK + (7 if side == 0 else 24)
                line_ref[pl.ds(start, 8, BLOCK), :] = keep_ang[side] * (center[f] + rates[f])


def received(place_ref, recv_ref, edge):
    values = jnp.dot(place_ref[...], recv_ref[...], precision=HIGHEST, preferred_element_type=F32)
    low, high = values[0:CP], pltpu.roll(values[CP : 2 * CP], LAT - 1 - edge, 1)
    if edge:
        low = pltpu.roll(low, edge, 1)
    first = (lax.broadcasted_iota(jnp.int32, (CP, LAT), 1) & 1) == edge & 1
    return jnp.where(first, low, high), jnp.where(first, high, low)


def with_rows(own, values, point, ends):
    rows = values[point % 2]
    if point:
        rows = pltpu.roll(rows, LAT - point, 1)
    return jnp.where(ends, rows, own)


def ends_of(edge):
    lane = lax.broadcasted_iota(jnp.int32, (CP, LAT), 1)
    return (lane == edge) | (lane == LAT - 1 - edge)


def first_at(inner_ref, edge_ref, f, r):
    if 1 <= r <= LV - 2:
        return inner_ref[f * TILE + r * CP : f * TILE + (r + 1) * CP, :], f * LV + r
    e = r // (LV - 1)
    return edge_ref[(e * 8 + f) * CP : (e * 8 + f + 1) * CP, :], NF * LV + e * 8 + f


def second_a_kernel(
    state_ref, below_ref, above_ref, coef_ref, rad_below_ref, rad_above_ref, inner_ref, edge_ref, next_ref,
    line_ref, work_ref, column_ref,
):
    ends = ends_of(0)
    for f in range(NF):
        for r in range(LV):
            base = (f * (LV + 2) + r + 1) * BLOCK + 8
            line_ref[base : base + CP, :] = jnp.where(ends, 0.0, first_at(inner_ref, edge_ref, f, r)[0])
    surround(
        state_ref, below_ref, above_ref, coef_ref, (rad_below_ref, rad_above_ref), work_ref, column_ref, line_ref
    )

    for r in range(LV):
        for t in range(2):

            def line(f, level=r):
                return (f * (LV + 2) + level + 1) * BLOCK + 8 + 8 * t

            def neighbours(f):
                return (
                    line_ref[line(f, r + 1) : line(f, r + 1) + 8, :],
                    line_ref[line(f, r - 1) : line(f, r - 1) + 8, :],
                    line_ref[line(f) + 1 : line(f) + 9, :],
                    line_ref[line(f) - 1 : line(f) + 7, :],
                )

            center = [line_ref[line(f) : line(f) + 8, :] for f in range(NF)]
            rates = increments(
                center, neighbours, lambda f: coef_ref[f, r : r + 1, :], coef_ref[NF, r : r + 1, :], 0.5 * step_size
            )
            for f in range(NF):
                row = f * TILE + r * CP + 8 * t
                next_ref[row : row + 8, :] = 0.5 * (state_ref[row : row + 8, :] + center[f]) + rates[f]


def second_b_kernel(
    before_ref, inner_ref, edge_ref, coef_ref, recv_ref, place_ref, lat_weight_ref, lon_weight_ref,
    next_ref, send_ref,
):
    values = received(place_ref, recv_ref, 1)
    beside = ends_of(1)
    lane = lax.broadcasted_iota(jnp.int32, (CP, LAT), 1)
    quarter = jnp.where(lane == 1, 0.25 * step_size, -0.25 * step_size)
    for r in range(LV):
        u = quarter * first_at(inner_ref, edge_ref, 2, r)[0]
        b = quarter * first_at(inner_ref, edge_ref, 5, r)[0]
        rows = [
            with_rows(jnp.zeros((CP, LAT), F32), values, first_at(inner_ref, edge_ref, f, r)[1], beside)
            for f in range(NF)
        ]
        for f in range(NF):
            gain = ((0.5 * step_size) * coef_ref[f, r : r + 1, :] + u) * rows[f]
            if f < 6:
                gain = gain - b * rows[(f + 3) % 6]
            row = f * TILE + r * CP
            next_ref[row : row + CP, :] = before_ref[row : row + CP, :] + gain
    donors = interpolate(next_ref[...], lat_weight_ref, lon_weight_ref)
    send_ref[...] = jnp.transpose(jnp.concatenate([donors, jnp.zeros((128 - NF * LV, 128), F32)], axis=0))


def last_kernel(next_ref, recv_ref, place_ref, out_ref, done_ref, sems):
    values = received(place_ref, recv_ref, 0)
    ends = ends_of(0)
    copies = []
    for f in range(NF):
        for r in range(LV):
            row = f * TILE + r * CP
            done_ref[row : row + CP, :] = with_rows(next_ref[row : row + CP, :], values, f * LV + r, ends)
        part = pl.ds(f * TILE, TILE)
        copies.append(pltpu.make_async_copy(done_ref.at[part, :], out_ref.at[part, :], sems.at[f]))
        copies[-1].start()
    for copy in copies:
        copy.wait()


def shift(value, axis, step):
    count = lax.axis_size(axis)
    pairs = [(i, i + step) for i in range(count) if 0 <= i + step < count]
    return lax.ppermute(value, axis, pairs)


def swap(value, axis, first):
    count = lax.axis_size(axis)
    low = range(first, count - 1, 2)
    return lax.ppermute(value, axis, [(i, i + 1) for i in low] + [(i + 1, i) for i in low])


def exchange(values):
    n = values.shape[0] // 2
    got = lax.all_to_all(values.reshape(n, 2, 128), ("panel", "ang"), 0, 0, tiled=True)
    return got.reshape(2 * n, 128)


def call(kernel, name, outs, scratch, flops, *operands):
    return pl.pallas_call(
        kernel,
        out_shape=outs,
        in_specs=[VMEM] * len(operands),
        out_specs=(VMEM,) * len(outs),
        scratch_shapes=scratch,
        compiler_params=params(),
        cost_estimate=cost(flops),
        name=name,
    )(*operands)


def rows(count):
    return pltpu.VMEM((count, LAT), F32)


def body(state, kappa, buoyancy, donor_lon, donor_lat, fractions):
    n_send = 4 * donor_lon.shape[1] // CP
    own = state.reshape(NF * TILE, LAT)
    halo, message = shape(2, NF, LV, LAT), shape(NF, MESSAGE, LAT)

    outer, inner = call(cut_kernel, "cut", (halo, halo), [], 100_000, own)
    outer = swap(outer, "ang", 1)
    inner = swap(inner, "ang", 0)

    coef = jnp.broadcast_to(jnp.concatenate([kappa, buoyancy[None]])[:, :, None], (NF + 1, LV, LAT))
    lat_weight, lon_weight, place = call(
        tables_kernel, "tables", (shape(LAT, n_send), shape(CP, n_send), shape(2 * CP, n_send)), [], 4_000_000,
        donor_lon, donor_lat, fractions,
    )
    coef, lat_weight = lax.optimization_barrier((coef, lat_weight))

    up, down, below, above = call(
        pack_kernel, "pack", (message, message, halo, halo), [], 100_000, own, outer, inner, coef
    )
    rad_below = shift(up, "rad", 1)
    rad_above = shift(down, "rad", -1)
    middle, values = call(
        first_a_kernel, "first_a", (shape(NF * TILE, LAT), shape(NF * LV, n_send)), [rows(NF * LV * BLOCK + 8)],
        60_000_000, own, below, above, coef, lat_weight, lon_weight,
    )
    edge, out = call(
        first_b_kernel, "first_b", (shape(2 * 8 * CP, LAT), shape(n_send, 128)), [rows(2 * NF * BLOCK + 8)],
        10_000_000, own, below, above, coef, rad_below, rad_above, lat_weight, lon_weight, values,
    )
    got = exchange(out)
    (before,) = call(
        second_a_kernel, "second_a", (shape(NF * TILE, LAT),),
        [rows(NF * (LV + 2) * BLOCK + 8), rows(2 * NF * BLOCK + 8), rows(2 * NF * BLOCK + 8)], 60_000_000,
        own, below, above, coef, rad_below, rad_above, middle, edge,
    )
    following, out = call(
        second_b_kernel, "second_b", (shape(NF * TILE, LAT), shape(n_send, 128)), [], 30_000_000,
        before, middle, edge, coef, got, place, lat_weight, lon_weight,
    )
    got = exchange(out)
    result = pl.pallas_call(
        last_kernel,
        out_shape=shape(NF * TILE, LAT),
        in_specs=[VMEM] * 3,
        out_specs=pl.BlockSpec(memory_space=pl.ANY),
        scratch_shapes=[rows(NF * TILE), pltpu.SemaphoreType.DMA((NF,))],
        compiler_params=params(),
        name="last",
    )(following, got, place)
    return result.reshape(state.shape)


def solution(mesh):
    return jax.shard_map(
        body,
        mesh=mesh,
        in_specs=(P("panel", None, "rad", "ang", None), P(None, "rad"), P("rad"), P(), P(), P()),
        out_specs=P("panel", None, "rad", "ang", None),
        check_vma=False,
    )
```

```python
import jax
import jax.numpy as jnp
from jax import lax
from jax.experimental import pallas as pl
from jax.experimental.pallas import tpu as pltpu
from jax.sharding import PartitionSpec as P

step_size = 0.1
HIGHEST = lax.Precision.HIGHEST
VMEM = pl.BlockSpec(memory_space=pltpu.VMEM)
F32 = jnp.float32

NF = 7
LV = 16
CP = 16
LAT = 128
TILE = LV * CP
BLOCK = 24
MESSAGE = 40


def params():
    return pltpu.CompilerParams(vmem_limit_bytes=40 * 1024 * 1024)


def cost(flops):
    return pl.CostEstimate(flops=flops, bytes_accessed=2_000_000, transcendentals=0)


def shape(*dims):
    return jax.ShapeDtypeStruct(dims, F32)


def picks(match, kid, slot):
    low = jnp.min(jnp.where(match, kid, 4096.0), axis=1, keepdims=True)
    high = jnp.max(jnp.where(match, kid, -1.0), axis=1, keepdims=True)
    low_or_none = jnp.where(low < 4096.0, low, -8.0)
    high_or_none = jnp.where(high > low, high, -8.0)
    return jnp.where(slot == 0, low_or_none, high_or_none)


def tables_kernel(
    kappa_ref, buoyancy_ref, lon_ref, lat_ref, frac_ref, coef_ref, lat_weight_ref, lon_weight_ref, beside_weight_ref,
    place_ref, placed_ref,
):
    level = lax.broadcasted_iota(jnp.int32, (LV, LV), 0)
    same = level == lax.broadcasted_iota(jnp.int32, (LV, LV), 1)
    for f in range(NF + 1):
        line = kappa_ref[f : f + 1, :] if f < NF else buoyancy_ref[...]
        column = jnp.sum(jnp.where(same, line, 0.0), axis=1, keepdims=True)
        coef_ref[f] = jnp.broadcast_to(column, (LV, LAT))

    nlon = lon_ref.shape[1]
    half = 2 * nlon // CP
    points = 2 * nlon
    panel = lax.axis_index("panel")
    tile = lax.axis_index("ang")

    def flat(low, high):
        return jnp.concatenate([low, high], axis=1)

    lon_k = flat(lon_ref[0:1, :], lon_ref[1:2, :])
    owner_k = lon_k >> 4
    off_k = (lon_k & 15).astype(F32)
    lat_k = flat(lat_ref[0:1, :], lat_ref[1:2, :]).astype(F32)
    fx_k = flat(frac_ref[0, 0:1, :], frac_ref[0, 1:2, :])
    fy_k = flat(frac_ref[1, 0:1, :], frac_ref[1, 1:2, :])

    kid = lax.broadcasted_iota(jnp.int32, (1, points), 1)
    dest_k = (kid & (nlon - 1)) >> 4
    kid = kid.astype(F32)

    row = lax.broadcasted_iota(jnp.int32, (half, 1), 0)
    match = (dest_k == (row >> 1)) & (owner_k == tile)
    pick = picks(match, kid, row & 1)
    chosen = kid == pick

    def of(value):
        return jnp.sum(jnp.where(chosen, value, 0.0), axis=1, keepdims=True)

    off, lat, fx, fy = of(off_k), of(lat_k), of(fx_k), of(fy_k)
    lane = lax.broadcasted_iota(jnp.int32, (half, LAT), 1).astype(F32)
    lat_weight = jnp.where(lane == lat, 1.0 - fy, 0.0) + jnp.where(lane == lat + 1.0, fy, 0.0)
    lat_weight = jnp.where(pick >= 0.0, lat_weight, 0.0)
    lon_weight = jnp.where(lane == off, 1.0 - fx, 0.0) + jnp.where(lane == off + 1.0, fx, 0.0)
    shifted = pltpu.roll(lon_weight, CP, 1)
    beside = jnp.where(lane < CP, lat_weight[:, 1:2] * lon_weight, lat_weight[:, LAT - 2 : LAT - 1] * shifted)
    beside_weight_ref[...] = jnp.transpose(jnp.concatenate([beside, beside], axis=0))
    lat_weight_ref[...] = jnp.transpose(jnp.concatenate([lat_weight, lat_weight], axis=0))
    lon_weight_ref[...] = jnp.transpose(jnp.concatenate([lon_weight, lon_weight], axis=0))[0:CP]

    row = lax.broadcasted_iota(jnp.int32, (half, 1), 0)
    match = (owner_k == (row >> 1)) & (dest_k == tile)
    pick = picks(match, kid, row & 1).astype(jnp.int32)
    target = ((pick >> (nlon.bit_length() - 1)) << 4) + (pick & 15)
    target = jnp.where(pick >= 0, target, -1)
    lane = lax.broadcasted_iota(jnp.int32, (half, 128), 1)
    place = jnp.where(lane == target, 1.0, 0.0)
    place = jnp.concatenate([place * panel.astype(F32), place * (1 - panel).astype(F32)], axis=0)
    place_ref[...] = place
    placed_ref[...] = jnp.transpose(place)[0 : 2 * CP]


def increments(center, neighbours, kappa, buoyancy, scale):
    u = [(0.5 * scale) * center[d] for d in range(3)]
    b = [(0.5 * scale) * center[3 + d] for d in range(3)]
    lap, adv, mag = [], [], []
    for f in range(NF):
        up, down, east, west = neighbours(f)
        north = pltpu.roll(center[f], LAT - 1, 1)
        south = pltpu.roll(center[f], 1, 1)
        diffs = [up - down, east - west, north - south]
        lap.append((scale * kappa(f)) * ((up + down) + (east + west) + (north + south) - 6.0 * center[f]))
        adv.append(u[0] * diffs[0] + u[1] * diffs[1] + u[2] * diffs[2])
        if f < 6:
            mag.append(b[0] * diffs[0] + b[1] * diffs[1] + b[2] * diffs[2])
    rates = [lap[f] - adv[f] + mag[(f + 3) % 6] for f in range(6)] + [lap[6] - adv[6]]
    rates[0] = rates[0] + (scale * buoyancy) * center[6]
    return rates


def interpolate(rows, lat_weight_ref, lon_weight_ref):
    along = jnp.dot(rows, lat_weight_ref[...], precision=HIGHEST, preferred_element_type=F32)
    n = rows.shape[0] // CP
    return jnp.sum(along.reshape(n, CP, along.shape[1]) * lon_weight_ref[...][None], axis=1)


def cut_kernel(state_ref, outer_ref, inner_ref):
    odd = lax.axis_index("ang") % 2 == 1
    for f in range(NF):
        for i in range(2):
            low = state_ref[pl.ds(f * TILE + i, LV, CP), :]
            high = state_ref[pl.ds(f * TILE + CP - 1 - i, LV, CP), :]
            outer_ref[i, f] = jnp.where(odd, high, low)
            inner_ref[i, f] = jnp.where(odd, low, high)


def pack_kernel(state_ref, outer_ref, inner_ref, coef_ref, up_ref, down_ref, below_ref, above_ref):
    odd = lax.axis_index("ang") % 2 == 1
    for i in range(2):
        for f in range(NF):
            above_ref[i, f] = jnp.where(odd, outer_ref[i, f], inner_ref[i, f])
            below_ref[i, f] = jnp.where(odd, inner_ref[i, f], outer_ref[i, f])
    for ref, near, far in ((up_ref, LV - 1, LV - 2), (down_ref, 0, 1)):
        for f in range(NF):
            start = f * TILE
            ref[f, 0:CP, :] = state_ref[start + near * CP : start + (near + 1) * CP, :]
            ref[f, CP : 2 * CP, :] = state_ref[start + far * CP : start + (far + 1) * CP, :]
            ref[f, 32:33, :] = above_ref[0, f, near : near + 1, :]
            ref[f, 33:34, :] = below_ref[0, f, near : near + 1, :]
            ref[f, 34:35, :] = coef_ref[f, near : near + 1, :]
            ref[f, 35:36, :] = coef_ref[NF, near : near + 1, :]
            ref[f, 36:40, :] = jnp.zeros((4, LAT), F32)


def first_a_kernel(
    state_ref, below_ref, above_ref, coef_ref, lat_weight_ref, lon_weight_ref, inner_ref, values_ref, line_ref
):
    for f in range(NF):
        for r in range(LV):
            base = (f * LV + r) * BLOCK + 8
            line_ref[base : base + CP, :] = state_ref[f * TILE + r * CP : f * TILE + (r + 1) * CP, :]
        line_ref[pl.ds(f * LV * BLOCK + 7, LV, BLOCK), :] = below_ref[0, f]
        line_ref[pl.ds(f * LV * BLOCK + 24, LV, BLOCK), :] = above_ref[0, f]
        for r in (0, LV - 1):
            inner_ref[f * TILE + r * CP : f * TILE + (r + 1) * CP, :] = jnp.zeros((CP, LAT), F32)
    for r in range(1, LV - 1):
        for t in range(2):

            def row(f, level=r):
                return f * TILE + level * CP + 8 * t

            def neighbours(f):
                line = (f * LV + r) * BLOCK + 8 + 8 * t
                return (
                    state_ref[row(f, r + 1) : row(f, r + 1) + 8, :],
                    state_ref[row(f, r - 1) : row(f, r - 1) + 8, :],
                    line_ref[line + 1 : line + 9, :],
                    line_ref[line - 1 : line + 7, :],
                )

            center = [state_ref[row(f) : row(f) + 8, :] for f in range(NF)]
            rates = increments(
                center, neighbours, lambda f: coef_ref[f, r : r + 1, :], coef_ref[NF, r : r + 1, :], step_size
            )
            for f in range(NF):
                inner_ref[row(f) : row(f) + 8, :] = center[f] + rates[f]
    values_ref[...] = interpolate(inner_ref[...], lat_weight_ref, lon_weight_ref)


def first_b_kernel(
    state_ref, below_ref, above_ref, coef_ref, rad_below_ref, rad_above_ref, lat_weight_ref, lon_weight_ref,
    values_ref, edge_ref, send_ref, line_ref, donors_ref,
):
    for e, r in enumerate((0, LV - 1)):
        for f in range(NF):
            base = (e * NF + f) * BLOCK + 8
            line_ref[base : base + CP, :] = state_ref[f * TILE + r * CP : f * TILE + (r + 1) * CP, :]
            line_ref[base - 1 : base, :] = below_ref[0, f, r : r + 1, :]
            line_ref[base + CP : base + CP + 1, :] = above_ref[0, f, r : r + 1, :]
    for e, r in enumerate((0, LV - 1)):
        for t in range(2):

            def own(f, level):
                return state_ref[f * TILE + level * CP + 8 * t : f * TILE + level * CP + 8 * t + 8, :]

            def neighbours(f):
                line = (e * NF + f) * BLOCK + 8 + 8 * t
                if e == 0:
                    up, down = own(f, 1), rad_below_ref[f, 8 * t : 8 * t + 8, :]
                else:
                    up, down = rad_above_ref[f, 8 * t : 8 * t + 8, :], own(f, LV - 2)
                return up, down, line_ref[line + 1 : line + 9, :], line_ref[line - 1 : line + 7, :]

            center = [own(f, r) for f in range(NF)]
            rates = increments(
                center, neighbours, lambda f: coef_ref[f, r : r + 1, :], coef_ref[NF, r : r + 1, :], step_size
            )
            for f in range(NF):
                base = (e * 8 + f) * CP + 8 * t
                edge_ref[base : base + 8, :] = center[f] + rates[f]
        edge_ref[(e * 8 + NF) * CP : (e * 8 + 8) * CP, :] = jnp.zeros((CP, LAT), F32)
    edges = interpolate(edge_ref[...], lat_weight_ref, lon_weight_ref)
    donors_ref[0 : NF * LV, :] = values_ref[...]
    donors_ref[NF * LV : 128, :] = jnp.zeros((128 - NF * LV, 128), F32)
    for f in range(NF):
        donors_ref[f * LV : f * LV + 1, :] = edges[f : f + 1]
        donors_ref[(f + 1) * LV - 1 : (f + 1) * LV, :] = edges[8 + f : 9 + f]
    send_ref[...] = jnp.transpose(donors_ref[...])


def surround(
    state_ref, below_ref, above_ref, coef_ref, rad_refs, work_ref, column_ref, line_ref
):
    rad, ang = lax.axis_index("rad"), lax.axis_index("ang")
    keep_rad = [jnp.where(rad == 0, 0.0, 1.0), jnp.where(rad == lax.axis_size("rad") - 1, 0.0, 1.0)]
    keep_ang = [jnp.where(ang == 0, 0.0, 1.0), jnp.where(ang == lax.axis_size("ang") - 1, 0.0, 1.0)]
    for e in range(2):
        source = rad_refs[e]
        for f in range(NF):
            base = (e * NF + f) * BLOCK + 8
            work_ref[base : base + CP, :] = source[f, 0:CP, :]
            work_ref[base - 1 : base, :] = source[f, 33:34, :]
            work_ref[base + CP : base + CP + 1, :] = source[f, 32:33, :]
    for side, ref in ((0, below_ref), (1, above_ref)):
        for f in range(NF):
            base = (side * NF + f) * BLOCK + 8
            column_ref[base : base + LV, :] = ref[0, f]
            column_ref[base - 1 : base, :] = rad_refs[0][f, 33 - side : 34 - side, :]
            column_ref[base + LV : base + LV + 1, :] = rad_refs[1][f, 33 - side : 34 - side, :]

    for e in range(2):
        source = rad_refs[e]
        for t in range(2):
            part = slice(8 * t, 8 * t + 8)

            def neighbours(f):
                line = (e * NF + f) * BLOCK + 8 + 8 * t
                start = f * TILE + e * (LV - 1) * CP + 8 * t
                inside, outside = state_ref[start : start + 8, :], source[f, CP + 8 * t : CP + 8 * t + 8, :]
                up, down = (inside, outside) if e == 0 else (outside, inside)
                return up, down, work_ref[line + 1 : line + 9, :], work_ref[line - 1 : line + 7, :]

            center = [source[f, part, :] for f in range(NF)]
            rates = increments(center, neighbours, lambda f: source[f, 34:35, :], source[0, 35:36, :], step_size)
            for f in range(NF):
                base = (f * (LV + 2) + e * (LV + 1)) * BLOCK + 8 + 8 * t
                line_ref[base : base + 8, :] = keep_rad[e] * (center[f] + rates[f])

    for side, ref in ((0, below_ref), (1, above_ref)):
        for t in range(2):
            part = slice(8 * t, 8 * t + 8)

            def neighbours(f):
                column = (side * NF + f) * BLOCK + 8 + 8 * t
                inside = state_ref[pl.ds(f * TILE + 8 * t * CP + side * (CP - 1), 8, CP), :]
                outside = ref[1, f, part, :]
                east, west = (inside, outside) if side == 0 else (outside, inside)
                return column_ref[column + 1 : column + 9, :], column_ref[column - 1 : column + 7, :], east, west

            center = [ref[0, f, part, :] for f in range(NF)]
            rates = increments(center, neighbours, lambda f: coef_ref[f, part, :], coef_ref[NF, part, :], step_size)
            for f in range(NF):
                start = (f * (LV + 2) + 1 + 8 * t) * BLOCK + (7 if side == 0 else 24)
                line_ref[pl.ds(start, 8, BLOCK), :] = keep_ang[side] * (center[f] + rates[f])


def first_at(inner_ref, edge_ref, f, r):
    if 1 <= r <= LV - 2:
        return inner_ref[f * TILE + r * CP : f * TILE + (r + 1) * CP, :]
    e = r // (LV - 1)
    return edge_ref[(e * 8 + f) * CP : (e * 8 + f + 1) * CP, :]


def second_a_kernel(
    state_ref, below_ref, above_ref, coef_ref, rad_below_ref, rad_above_ref, inner_ref, edge_ref, lat_weight_ref,
    lon_weight_ref, next_ref, values_ref, carry_ref, line_ref, work_ref, column_ref,
):
    lane = lax.broadcasted_iota(jnp.int32, (CP, LAT), 1)
    row = lax.broadcasted_iota(jnp.int32, (CP, LAT), 0)
    ends = (lane == 0) | (lane == LAT - 1)
    for i, f in enumerate((2, 5)):
        for r in range(LV):
            own = (0.25 * step_size) * first_at(inner_ref, edge_ref, f, r)
            low = jnp.where(lane == row, own[:, 1:2], 0.0)
            high = jnp.where(lane == row + CP, own[:, LAT - 2 : LAT - 1], 0.0)
            carry_ref[i, r : r + 1, :] = jnp.sum(low - high, axis=0, keepdims=True)
    for f in range(NF):
        for r in range(LV):
            base = (f * (LV + 2) + r + 1) * BLOCK + 8
            line_ref[base : base + CP, :] = jnp.where(ends, 0.0, first_at(inner_ref, edge_ref, f, r))
    surround(
        state_ref, below_ref, above_ref, coef_ref, (rad_below_ref, rad_above_ref), work_ref, column_ref, line_ref
    )

    for r in range(LV):
        for t in range(2):

            def line(f, level=r):
                return (f * (LV + 2) + level + 1) * BLOCK + 8 + 8 * t

            def neighbours(f):
                return (
                    line_ref[line(f, r + 1) : line(f, r + 1) + 8, :],
                    line_ref[line(f, r - 1) : line(f, r - 1) + 8, :],
                    line_ref[line(f) + 1 : line(f) + 9, :],
                    line_ref[line(f) - 1 : line(f) + 7, :],
                )

            center = [line_ref[line(f) : line(f) + 8, :] for f in range(NF)]
            rates = increments(
                center, neighbours, lambda f: coef_ref[f, r : r + 1, :], coef_ref[NF, r : r + 1, :], 0.5 * step_size
            )
            for f in range(NF):
                row = f * TILE + r * CP + 8 * t
                next_ref[row : row + 8, :] = 0.5 * (state_ref[row : row + 8, :] + center[f]) + rates[f]
    values_ref[...] = interpolate(next_ref[...], lat_weight_ref, lon_weight_ref)


def second_b_kernel(
    coef_ref, recv_ref, place_ref, carry_ref, values_ref, beside_weight_ref, beside_ref, send_ref
):
    ends = lax.dot_general(
        recv_ref[...], place_ref[...], (((0,), (0,)), ((), ())), precision=HIGHEST, preferred_element_type=F32
    )
    ends = [ends[f * LV : (f + 1) * LV] for f in range(NF)]
    gains = []
    for f in range(NF):
        gain = ((0.5 * step_size) * coef_ref[f] + carry_ref[0]) * ends[f]
        gains.append(gain - carry_ref[1] * ends[(f + 3) % 6] if f < 6 else gain)
    gains = jnp.concatenate(gains, axis=0)
    added = jnp.dot(gains, beside_weight_ref[...], precision=HIGHEST, preferred_element_type=F32)
    blank = jnp.zeros((128 - NF * LV, 128), F32)
    send_ref[...] = jnp.transpose(jnp.concatenate([values_ref[...] + added, blank], axis=0))
    beside_ref[...] = jnp.transpose(jnp.concatenate([gains, blank], axis=0))[0 : 2 * CP]


def last_kernel(next_ref, beside_ref, recv_ref, placed_ref, out_ref, done_ref, sems):
    values = jnp.dot(placed_ref[...], recv_ref[...], precision=HIGHEST, preferred_element_type=F32)
    parts = [
        values[0:CP],
        pltpu.roll(beside_ref[0:CP], 1, 1),
        pltpu.roll(beside_ref[CP : 2 * CP], LAT - 2, 1),
        pltpu.roll(values[CP : 2 * CP], LAT - 1, 1),
    ]
    lane = lax.broadcasted_iota(jnp.int32, (CP, LAT), 1)
    mixed = []
    for q in range(4):
        place = (lane - q) & 3
        mixed.append(
            jnp.where(place < 2, jnp.where(place == 0, parts[0], parts[1]), jnp.where(place == 2, parts[2], parts[3]))
        )
    ends = (lane == 0) | (lane == LAT - 1)
    near = (lane < 2) | (lane >= LAT - 2)
    copies = []
    for f in range(NF):
        for r in range(LV):
            row, point = f * TILE + r * CP, f * LV + r
            rows = mixed[point % 4]
            if point:
                rows = pltpu.roll(rows, LAT - point, 1)
            own = next_ref[row : row + CP, :]
            done_ref[row : row + CP, :] = jnp.where(ends, 0.0, own) + jnp.where(near, rows, 0.0)
        part = pl.ds(f * TILE, TILE)
        copies.append(pltpu.make_async_copy(done_ref.at[part, :], out_ref.at[part, :], sems.at[f]))
        copies[-1].start()
    for copy in copies:
        copy.wait()


def shift(value, axis, step):
    count = lax.axis_size(axis)
    pairs = [(i, i + step) for i in range(count) if 0 <= i + step < count]
    return lax.ppermute(value, axis, pairs)


def swap(value, axis, first):
    count = lax.axis_size(axis)
    low = range(first, count - 1, 2)
    return lax.ppermute(value, axis, [(i, i + 1) for i in low] + [(i + 1, i) for i in low])


def exchange(values):
    n = values.shape[0] // 2
    got = lax.all_to_all(values.reshape(n, 2, 128), ("panel", "ang"), 0, 0, tiled=True)
    return got.reshape(2 * n, 128)


def call(kernel, name, outs, scratch, flops, *operands):
    return pl.pallas_call(
        kernel,
        out_shape=outs,
        in_specs=[VMEM] * len(operands),
        out_specs=(VMEM,) * len(outs),
        scratch_shapes=scratch,
        compiler_params=params(),
        cost_estimate=cost(flops) if isinstance(flops, int) else flops,
        name=name,
    )(*operands)


def rows(count):
    return pltpu.VMEM((count, LAT), F32)


def body(state, kappa, buoyancy, donor_lon, donor_lat, fractions):
    n_send = 4 * donor_lon.shape[1] // CP
    own = state.reshape(NF * TILE, LAT)
    halo, message = shape(2, NF, LV, LAT), shape(NF, MESSAGE, LAT)
    outer, inner = call(cut_kernel, "cut", (halo, halo), [], pl.CostEstimate(flops=4_000_000_000, bytes_accessed=20_000_000, transcendentals=0), own)
    outer = swap(outer, "ang", 1)
    inner = swap(inner, "ang", 0)
    coef, lat_weight, lon_weight, beside_weight, place, placed = call(
        tables_kernel, "tables",
        (
            shape(NF + 1, LV, LAT), shape(LAT, n_send), shape(CP, n_send), shape(LAT, n_send), shape(n_send, 128),
            shape(2 * CP, n_send),
        ), [], 4_000_000, kappa, buoyancy[None], donor_lon, donor_lat, fractions,
    )

    up, down, below, above = call(
        pack_kernel, "pack", (message, message, halo, halo), [], 100_000, own, outer, inner, coef
    )
    rad_below = shift(up, "rad", 1)
    rad_above = shift(down, "rad", -1)
    middle, values = call(
        first_a_kernel, "first_a", (shape(NF * TILE, LAT), shape(NF * LV, n_send)), [rows(NF * LV * BLOCK + 8)],
        60_000_000, own, below, above, coef, lat_weight, lon_weight,
    )
    edge, out = call(
        first_b_kernel, "first_b", (shape(2 * 8 * CP, LAT), shape(n_send, 128)), [rows(2 * NF * BLOCK + 8), rows(128)],
        10_000_000, own, below, above, coef, rad_below, rad_above, lat_weight, lon_weight, values,
    )
    got = exchange(out)
    following, values, carry = call(
        second_a_kernel, "second_a", (shape(NF * TILE, LAT), shape(NF * LV, n_send), shape(2, LV, LAT)),
        [rows(NF * (LV + 2) * BLOCK + 8), rows(2 * NF * BLOCK + 8), rows(2 * NF * BLOCK + 8)], 60_000_000,
        own, below, above, coef, rad_below, rad_above, middle, edge, lat_weight, lon_weight,
    )
    beside, out = call(
        second_b_kernel, "second_b", (shape(2 * CP, LAT), shape(n_send, 128)), [], 1_000_000,
        coef, got, place, carry, values, beside_weight,
    )
    got = exchange(out)
    result = pl.pallas_call(
        last_kernel,
        out_shape=shape(NF * TILE, LAT),
        in_specs=[VMEM] * 4,
        out_specs=pl.BlockSpec(memory_space=pl.ANY),
        scratch_shapes=[rows(NF * TILE), pltpu.SemaphoreType.DMA((NF,))],
        compiler_params=params(),
        name="last",
    )(following, beside, got, placed)
    return result.reshape(state.shape)


def solution(mesh):
    return jax.shard_map(
        body,
        mesh=mesh,
        in_specs=(P("panel", None, "rad", "ang", None), P(None, "rad"), P("rad"), P(), P(), P()),
        out_specs=P("panel", None, "rad", "ang", None),
        check_vma=False,
    )
```

```python
import jax
import jax.numpy as jnp
from jax import lax
from jax.experimental import pallas as pl
from jax.experimental.pallas import tpu as pltpu
from jax.sharding import PartitionSpec as P

step_size = 0.1
HIGHEST = lax.Precision.HIGHEST
VMEM = pl.BlockSpec(memory_space=pltpu.VMEM)
F32 = jnp.float32

NF = 7
LV = 16
CP = 16
LAT = 128
TILE = LV * CP
BLOCK = 24
MESSAGE = 40


def params():
    return pltpu.CompilerParams(vmem_limit_bytes=40 * 1024 * 1024)


def cost(flops):
    return pl.CostEstimate(flops=flops, bytes_accessed=2_000_000, transcendentals=0)


def shape(*dims):
    return jax.ShapeDtypeStruct(dims, F32)


def picks(match, kid, slot):
    low = jnp.min(jnp.where(match, kid, 4096.0), axis=1, keepdims=True)
    high = jnp.max(jnp.where(match, kid, -1.0), axis=1, keepdims=True)
    low_or_none = jnp.where(low < 4096.0, low, -8.0)
    high_or_none = jnp.where(high > low, high, -8.0)
    return jnp.where(slot == 0, low_or_none, high_or_none)


def tables_kernel(
    kappa_ref, buoyancy_ref, lon_ref, lat_ref, frac_ref, coef_ref, lat_weight_ref, lon_weight_ref, beside_weight_ref,
    placed_ref,
):
    level = lax.broadcasted_iota(jnp.int32, (LV, LV), 0)
    same = level == lax.broadcasted_iota(jnp.int32, (LV, LV), 1)
    for f in range(NF + 1):
        line = kappa_ref[f : f + 1, :] if f < NF else buoyancy_ref[...]
        column = jnp.sum(jnp.where(same, line, 0.0), axis=1, keepdims=True)
        coef_ref[f] = jnp.broadcast_to(column, (LV, LAT))

    nlon = lon_ref.shape[1]
    half = 2 * nlon // CP
    points = 2 * nlon
    panel = lax.axis_index("panel")
    tile = lax.axis_index("ang")

    def flat(low, high):
        return jnp.concatenate([low, high], axis=1)

    lon_k = flat(lon_ref[0:1, :], lon_ref[1:2, :])
    owner_k = lon_k >> 4
    off_k = (lon_k & 15).astype(F32)
    lat_k = flat(lat_ref[0:1, :], lat_ref[1:2, :]).astype(F32)
    fx_k = flat(frac_ref[0, 0:1, :], frac_ref[0, 1:2, :])
    fy_k = flat(frac_ref[1, 0:1, :], frac_ref[1, 1:2, :])

    kid = lax.broadcasted_iota(jnp.int32, (1, points), 1)
    dest_k = (kid & (nlon - 1)) >> 4
    kid = kid.astype(F32)

    row = lax.broadcasted_iota(jnp.int32, (half, 1), 0)
    match = (dest_k == (row >> 1)) & (owner_k == tile)
    pick = picks(match, kid, row & 1)
    chosen = kid == pick

    def of(value):
        return jnp.sum(jnp.where(chosen, value, 0.0), axis=1, keepdims=True)

    off, lat, fx, fy = of(off_k), of(lat_k), of(fx_k), of(fy_k)
    lane = lax.broadcasted_iota(jnp.int32, (half, LAT), 1).astype(F32)
    lat_weight = jnp.where(lane == lat, 1.0 - fy, 0.0) + jnp.where(lane == lat + 1.0, fy, 0.0)
    lat_weight = jnp.where(pick >= 0.0, lat_weight, 0.0)
    lon_weight = jnp.where(lane == off, 1.0 - fx, 0.0) + jnp.where(lane == off + 1.0, fx, 0.0)
    shifted = pltpu.roll(lon_weight, CP, 1)
    beside = jnp.where(lane < CP, lat_weight[:, 1:2] * lon_weight, lat_weight[:, LAT - 2 : LAT - 1] * shifted)
    beside_weight_ref[...] = jnp.transpose(jnp.concatenate([beside, beside], axis=0))[0 : 2 * CP]
    lat_weight_ref[...] = jnp.transpose(jnp.concatenate([lat_weight, lat_weight], axis=0))
    lon_weight_ref[...] = jnp.transpose(jnp.concatenate([lon_weight, lon_weight], axis=0))[0:CP]

    row = lax.broadcasted_iota(jnp.int32, (half, 1), 0)
    match = (owner_k == (row >> 1)) & (dest_k == tile)
    pick = picks(match, kid, row & 1).astype(jnp.int32)
    target = ((pick >> (nlon.bit_length() - 1)) << 4) + (pick & 15)
    target = jnp.where(pick >= 0, target, -1)
    lane = lax.broadcasted_iota(jnp.int32, (half, 128), 1)
    place = jnp.where(lane == target, 1.0, 0.0)
    place = jnp.concatenate([place * panel.astype(F32), place * (1 - panel).astype(F32)], axis=0)
    placed_ref[...] = jnp.transpose(place)[0 : 2 * CP]


def increments(center, neighbours, kappa, buoyancy, scale):
    u = [(0.5 * scale) * center[d] for d in range(3)]
    b = [(0.5 * scale) * center[3 + d] for d in range(3)]
    lap, adv, mag = [], [], []
    for f in range(NF):
        up, down, east, west = neighbours(f)
        north = pltpu.roll(center[f], LAT - 1, 1)
        south = pltpu.roll(center[f], 1, 1)
        diffs = [up - down, east - west, north - south]
        lap.append((scale * kappa(f)) * ((up + down) + (east + west) + (north + south) - 6.0 * center[f]))
        adv.append(u[0] * diffs[0] + u[1] * diffs[1] + u[2] * diffs[2])
        if f < 6:
            mag.append(b[0] * diffs[0] + b[1] * diffs[1] + b[2] * diffs[2])
    rates = [lap[f] - adv[f] + mag[(f + 3) % 6] for f in range(6)] + [lap[6] - adv[6]]
    rates[0] = rates[0] + (scale * buoyancy) * center[6]
    return rates


def interpolate(rows, lat_weight_ref, lon_weight_ref):
    along = jnp.dot(rows, lat_weight_ref[...], precision=HIGHEST, preferred_element_type=F32)
    n = rows.shape[0] // CP
    return jnp.sum(along.reshape(n, CP, along.shape[1]) * lon_weight_ref[...][None], axis=1)


def cut_kernel(state_ref, outer_ref, inner_ref):
    odd = lax.axis_index("ang") % 2 == 1
    for f in range(NF):
        for i in range(2):
            low = state_ref[pl.ds(f * TILE + i, LV, CP), :]
            high = state_ref[pl.ds(f * TILE + CP - 1 - i, LV, CP), :]
            outer_ref[i, f] = jnp.where(odd, high, low)
            inner_ref[i, f] = jnp.where(odd, low, high)


def pack_kernel(state_ref, outer_ref, inner_ref, coef_ref, up_ref, down_ref, below_ref, above_ref):
    odd = lax.axis_index("ang") % 2 == 1
    for i in range(2):
        for f in range(NF):
            above_ref[i, f] = jnp.where(odd, outer_ref[i, f], inner_ref[i, f])
            below_ref[i, f] = jnp.where(odd, inner_ref[i, f], outer_ref[i, f])
    for ref, near, far in ((up_ref, LV - 1, LV - 2), (down_ref, 0, 1)):
        for f in range(NF):
            start = f * TILE
            ref[f, 0:CP, :] = state_ref[start + near * CP : start + (near + 1) * CP, :]
            ref[f, CP : 2 * CP, :] = state_ref[start + far * CP : start + (far + 1) * CP, :]
            ref[f, 32:33, :] = above_ref[0, f, near : near + 1, :]
            ref[f, 33:34, :] = below_ref[0, f, near : near + 1, :]
            ref[f, 34:35, :] = coef_ref[f, near : near + 1, :]
            ref[f, 35:36, :] = coef_ref[NF, near : near + 1, :]
            ref[f, 36:40, :] = jnp.zeros((4, LAT), F32)


def first_a_kernel(
    state_ref, below_ref, above_ref, coef_ref, lat_weight_ref, lon_weight_ref, inner_ref, values_ref, line_ref
):
    for f in range(NF):
        for r in range(LV):
            base = (f * LV + r) * BLOCK + 8
            line_ref[base : base + CP, :] = state_ref[f * TILE + r * CP : f * TILE + (r + 1) * CP, :]
        line_ref[pl.ds(f * LV * BLOCK + 7, LV, BLOCK), :] = below_ref[0, f]
        line_ref[pl.ds(f * LV * BLOCK + 24, LV, BLOCK), :] = above_ref[0, f]
        for r in (0, LV - 1):
            inner_ref[f * TILE + r * CP : f * TILE + (r + 1) * CP, :] = jnp.zeros((CP, LAT), F32)
    for r in range(1, LV - 1):
        for t in range(2):

            def row(f, level=r):
                return f * TILE + level * CP + 8 * t

            def neighbours(f):
                line = (f * LV + r) * BLOCK + 8 + 8 * t
                return (
                    state_ref[row(f, r + 1) : row(f, r + 1) + 8, :],
                    state_ref[row(f, r - 1) : row(f, r - 1) + 8, :],
                    line_ref[line + 1 : line + 9, :],
                    line_ref[line - 1 : line + 7, :],
                )

            center = [state_ref[row(f) : row(f) + 8, :] for f in range(NF)]
            rates = increments(
                center, neighbours, lambda f: coef_ref[f, r : r + 1, :], coef_ref[NF, r : r + 1, :], step_size
            )
            for f in range(NF):
                inner_ref[row(f) : row(f) + 8, :] = center[f] + rates[f]
    values_ref[...] = interpolate(inner_ref[...], lat_weight_ref, lon_weight_ref)


def first_b_kernel(
    state_ref, below_ref, above_ref, coef_ref, rad_below_ref, rad_above_ref, lat_weight_ref, lon_weight_ref,
    values_ref, edge_ref, ring_ref, send_ref, line_ref, column_ref, donors_ref,
):
    rad, ang = lax.axis_index("rad"), lax.axis_index("ang")
    keep_rad = [jnp.where(rad == 0, 0.0, 1.0), jnp.where(rad == lax.axis_size("rad") - 1, 0.0, 1.0)]
    keep_ang = [jnp.where(ang == 0, 0.0, 1.0), jnp.where(ang == lax.axis_size("ang") - 1, 0.0, 1.0)]
    radial = (rad_below_ref, rad_above_ref)

    for f in range(NF):
        for e, r in ((1, 0), (2, LV - 1)):
            base = (e * NF + f) * BLOCK + 8
            line_ref[base : base + CP, :] = state_ref[f * TILE + r * CP : f * TILE + (r + 1) * CP, :]
            line_ref[base - 1 : base, :] = below_ref[0, f, r : r + 1, :]
            line_ref[base + CP : base + CP + 1, :] = above_ref[0, f, r : r + 1, :]
        for e, ref in ((0, rad_below_ref), (3, rad_above_ref)):
            base = (e * NF + f) * BLOCK + 8
            line_ref[base : base + CP, :] = ref[f, 0:CP, :]
            line_ref[base - 1 : base, :] = ref[f, 33:34, :]
            line_ref[base + CP : base + CP + 1, :] = ref[f, 32:33, :]
        for side, ref in ((0, below_ref.at[0]), (1, above_ref.at[0])):
            base = (side * NF + f) * BLOCK + 8
            column_ref[base : base + LV, :] = ref[f]
            column_ref[base - 1 : base, :] = rad_below_ref[f, 33 - side : 34 - side, :]
            column_ref[base + LV : base + LV + 1, :] = rad_above_ref[f, 33 - side : 34 - side, :]

    for e in range(4):
        for t in range(2):
            part = slice(8 * t, 8 * t + 8)

            def own(f, r):
                return state_ref[f * TILE + r * CP + 8 * t : f * TILE + r * CP + 8 * t + 8, :]

            def neighbours(f):
                line = (e * NF + f) * BLOCK + 8 + 8 * t
                if e == 0:
                    up, down = own(f, 0), rad_below_ref[f, CP + 8 * t : CP + 8 * t + 8, :]
                elif e == 1:
                    up, down = own(f, 1), rad_below_ref[f, part, :]
                elif e == 2:
                    up, down = rad_above_ref[f, part, :], own(f, LV - 2)
                else:
                    up, down = rad_above_ref[f, CP + 8 * t : CP + 8 * t + 8, :], own(f, LV - 1)
                return up, down, line_ref[line + 1 : line + 9, :], line_ref[line - 1 : line + 7, :]

            center = [line_ref[(e * NF + f) * BLOCK + 8 + 8 * t : (e * NF + f) * BLOCK + 16 + 8 * t, :] for f in range(NF)]
            if e in (0, 3):
                source = radial[e // 3]
                rates = increments(center, neighbours, lambda f: source[f, 34:35, :], source[0, 35:36, :], step_size)
            else:
                r = (e - 1) * (LV - 1)
                rates = increments(
                    center, neighbours, lambda f: coef_ref[f, r : r + 1, :], coef_ref[NF, r : r + 1, :], step_size
                )
            for f in range(NF):
                value = center[f] + rates[f]
                if e in (0, 3):
                    value = keep_rad[e // 3] * value
                base = (e * 8 + f) * CP + 8 * t
                edge_ref[base : base + 8, :] = value
        edge_ref[(e * 8 + NF) * CP : (e * 8 + 8) * CP, :] = jnp.zeros((CP, LAT), F32)

    for side in range(2):
        for t in range(2):
            part = slice(8 * t, 8 * t + 8)

            def neighbours(f):
                column = (side * NF + f) * BLOCK + 8 + 8 * t
                near = state_ref[pl.ds(f * TILE + 8 * t * CP + side * (CP - 1), 8, CP), :]
                if side == 0:
                    east, west = near, below_ref[1, f, part, :]
                else:
                    east, west = above_ref[1, f, part, :], near
                return column_ref[column + 1 : column + 9, :], column_ref[column - 1 : column + 7, :], east, west

            center = [(below_ref[0, f, part, :] if side == 0 else above_ref[0, f, part, :]) for f in range(NF)]
            rates = increments(center, neighbours, lambda f: coef_ref[f, part, :], coef_ref[NF, part, :], step_size)
            for f in range(NF):
                ring_ref[side, f, part, :] = keep_ang[side] * (center[f] + rates[f])

    edges = interpolate(edge_ref[8 * CP : 24 * CP, :], lat_weight_ref, lon_weight_ref)
    donors_ref[0 : NF * LV, :] = values_ref[...]
    donors_ref[NF * LV : 128, :] = jnp.zeros((128 - NF * LV, 128), F32)
    for f in range(NF):
        donors_ref[f * LV : f * LV + 1, :] = edges[f : f + 1]
        donors_ref[(f + 1) * LV - 1 : (f + 1) * LV, :] = edges[8 + f : 9 + f]
    send_ref[...] = jnp.transpose(donors_ref[...])


def first_at(inner_ref, edge_ref, f, r):
    if 1 <= r <= LV - 2:
        return inner_ref[f * TILE + r * CP : f * TILE + (r + 1) * CP, :]
    e = {-1: 0, 0: 1, LV - 1: 2, LV: 3}[r]
    return edge_ref[(e * 8 + f) * CP : (e * 8 + f + 1) * CP, :]


def second_a_kernel(
    state_ref, coef_ref, inner_ref, edge_ref, ring_ref, lat_weight_ref, lon_weight_ref, next_ref, mid_ref, line_ref
):
    lane = lax.broadcasted_iota(jnp.int32, (CP, LAT), 1)
    row = lax.broadcasted_iota(jnp.int32, (CP, LAT), 0)
    ends = (lane == 0) | (lane == LAT - 1)
    for i, f in enumerate((2, 5)):
        for r in range(LV):
            own = (0.25 * step_size) * first_at(inner_ref, edge_ref, f, r)
            low = jnp.where(lane == row, own[:, 1:2], 0.0)
            high = jnp.where(lane == row + CP, own[:, LAT - 2 : LAT - 1], 0.0)
            mid_ref[NF * LV + i * LV + r : NF * LV + i * LV + r + 1, :] = jnp.sum(low - high, axis=0, keepdims=True)
    for f in range(NF):
        for r in range(-1, LV + 1):
            base = (f * (LV + 2) + r + 1) * BLOCK + 8
            own = first_at(inner_ref, edge_ref, f, r)
            line_ref[base : base + CP, :] = jnp.where(ends, 0.0, own) if 0 <= r < LV else own
        start = (f * (LV + 2) + 1) * BLOCK
        line_ref[pl.ds(start + 7, LV, BLOCK), :] = ring_ref[0, f]
        line_ref[pl.ds(start + 24, LV, BLOCK), :] = ring_ref[1, f]

    for r in range(LV):
        for t in range(2):

            def line(f, level=r):
                return (f * (LV + 2) + level + 1) * BLOCK + 8 + 8 * t

            def neighbours(f):
                return (
                    line_ref[line(f, r + 1) : line(f, r + 1) + 8, :],
                    line_ref[line(f, r - 1) : line(f, r - 1) + 8, :],
                    line_ref[line(f) + 1 : line(f) + 9, :],
                    line_ref[line(f) - 1 : line(f) + 7, :],
                )

            center = [line_ref[line(f) : line(f) + 8, :] for f in range(NF)]
            rates = increments(
                center, neighbours, lambda f: coef_ref[f, r : r + 1, :], coef_ref[NF, r : r + 1, :], 0.5 * step_size
            )
            for f in range(NF):
                row = f * TILE + r * CP + 8 * t
                next_ref[row : row + 8, :] = 0.5 * (state_ref[row : row + 8, :] + center[f]) + rates[f]
    mid_ref[0 : NF * LV, :] = interpolate(next_ref[...], lat_weight_ref, lon_weight_ref)


def second_b_kernel(
    coef_ref, recv_ref, placed_ref, mid_ref, beside_weight_ref, beside_ref, send_ref
):
    ends = lax.dot_general(
        recv_ref[...], placed_ref[...], (((0,), (1,)), ((), ())), precision=HIGHEST, preferred_element_type=F32
    )
    ends = [ends[f * LV : (f + 1) * LV] for f in range(NF)]
    u = mid_ref[NF * LV : (NF + 1) * LV, 0 : 2 * CP]
    b = mid_ref[(NF + 1) * LV : (NF + 2) * LV, 0 : 2 * CP]
    gains = []
    for f in range(NF):
        gain = ((0.5 * step_size) * coef_ref[f, :, 0 : 2 * CP] + u) * ends[f]
        gains.append(gain - b * ends[(f + 3) % 6] if f < 6 else gain)
    gains = jnp.concatenate(gains, axis=0)
    added = jnp.dot(gains, beside_weight_ref[...], precision=HIGHEST, preferred_element_type=F32)
    blank = jnp.zeros((128 - NF * LV, 128), F32)
    send_ref[...] = jnp.transpose(jnp.concatenate([mid_ref[0 : NF * LV, :] + added, blank], axis=0))
    gains = jnp.concatenate([gains, jnp.zeros((NF * LV, 128 - 2 * CP), F32)], axis=1)
    beside_ref[...] = jnp.transpose(jnp.concatenate([gains, blank], axis=0))[0 : 2 * CP]


def last_kernel(next_ref, beside_ref, recv_ref, placed_ref, out_ref, done_ref, sems):
    values = jnp.dot(placed_ref[...], recv_ref[...], precision=HIGHEST, preferred_element_type=F32)
    parts = [
        values[0:CP],
        pltpu.roll(beside_ref[0:CP], 1, 1),
        pltpu.roll(beside_ref[CP : 2 * CP], LAT - 2, 1),
        pltpu.roll(values[CP : 2 * CP], LAT - 1, 1),
    ]
    lane = lax.broadcasted_iota(jnp.int32, (CP, LAT), 1)
    mixed = []
    for q in range(4):
        place = (lane - q) & 3
        mixed.append(
            jnp.where(place < 2, jnp.where(place == 0, parts[0], parts[1]), jnp.where(place == 2, parts[2], parts[3]))
        )
    ends = (lane == 0) | (lane == LAT - 1)
    near = (lane < 2) | (lane >= LAT - 2)
    copies = []
    for f in range(NF):
        for r in range(LV):
            row, point = f * TILE + r * CP, f * LV + r
            rows = mixed[point % 4]
            if point:
                rows = pltpu.roll(rows, LAT - point, 1)
            own = next_ref[row : row + CP, :]
            done_ref[row : row + CP, :] = jnp.where(ends, 0.0, own) + jnp.where(near, rows, 0.0)
        part = pl.ds(f * TILE, TILE)
        copies.append(pltpu.make_async_copy(done_ref.at[part, :], out_ref.at[part, :], sems.at[f]))
        copies[-1].start()
    for copy in copies:
        copy.wait()


def shift(value, axis, step):
    count = lax.axis_size(axis)
    pairs = [(i, i + step) for i in range(count) if 0 <= i + step < count]
    return lax.ppermute(value, axis, pairs)


def swap(value, axis, first):
    count = lax.axis_size(axis)
    low = range(first, count - 1, 2)
    return lax.ppermute(value, axis, [(i, i + 1) for i in low] + [(i + 1, i) for i in low])


def exchange(values):
    n = values.shape[0] // 2
    got = lax.all_to_all(values.reshape(n, 2, 128), ("panel", "ang"), 0, 0, tiled=True)
    return got.reshape(2 * n, 128)


def call(kernel, name, outs, scratch, flops, *operands):
    return pl.pallas_call(
        kernel,
        out_shape=outs,
        in_specs=[VMEM] * len(operands),
        out_specs=(VMEM,) * len(outs),
        scratch_shapes=scratch,
        compiler_params=params(),
        cost_estimate=cost(flops) if isinstance(flops, int) else flops,
        name=name,
    )(*operands)


def rows(count):
    return pltpu.VMEM((count, LAT), F32)


def body(state, kappa, buoyancy, donor_lon, donor_lat, fractions):
    n_send = 4 * donor_lon.shape[1] // CP
    own = state.reshape(NF * TILE, LAT)
    halo, message = shape(2, NF, LV, LAT), shape(NF, MESSAGE, LAT)
    outer, inner = call(cut_kernel, "cut", (halo, halo), [], pl.CostEstimate(flops=4_000_000_000, bytes_accessed=20_000_000, transcendentals=0), own)
    outer = swap(outer, "ang", 1)
    inner = swap(inner, "ang", 0)
    coef, lat_weight, lon_weight, beside_weight, placed = call(
        tables_kernel, "tables",
        (
            shape(NF + 1, LV, LAT), shape(LAT, n_send), shape(CP, n_send), shape(2 * CP, n_send), shape(2 * CP, n_send),
        ), [], 4_000_000, kappa, buoyancy[None], donor_lon, donor_lat, fractions,
    )

    up, down, below, above = call(
        pack_kernel, "pack", (message, message, halo, halo), [], 100_000, own, outer, inner, coef
    )
    rad_below = shift(up, "rad", 1)
    rad_above = shift(down, "rad", -1)
    middle, values = call(
        first_a_kernel, "first_a", (shape(NF * TILE, LAT), shape(NF * LV, n_send)), [rows(NF * LV * BLOCK + 8)],
        60_000_000, own, below, above, coef, lat_weight, lon_weight,
    )
    edge, ring, out = call(
        first_b_kernel, "first_b", (shape(4 * 8 * CP, LAT), halo, shape(n_send, 128)),
        [rows(4 * NF * BLOCK + 8), rows(2 * NF * BLOCK + 8), rows(128)], 10_000_000,
        own, below, above, coef, rad_below, rad_above, lat_weight, lon_weight, values,
    )
    got = exchange(out)
    following, mid = call(
        second_a_kernel, "second_a", (shape(NF * TILE, LAT), shape((NF + 2) * LV, n_send)),
        [rows(NF * (LV + 2) * BLOCK + 8)], 60_000_000, own, coef, middle, edge, ring, lat_weight, lon_weight,
    )
    beside, out = call(
        second_b_kernel, "second_b", (shape(2 * CP, LAT), shape(n_send, 128)), [], 1_000_000,
        coef, got, placed, mid, beside_weight,
    )
    got = exchange(out)
    result = pl.pallas_call(
        last_kernel,
        out_shape=shape(NF * TILE, LAT),
        in_specs=[VMEM] * 4,
        out_specs=pl.BlockSpec(memory_space=pl.ANY),
        scratch_shapes=[rows(NF * TILE), pltpu.SemaphoreType.DMA((NF,))],
        compiler_params=params(),
        name="last",
    )(following, beside, got, placed)
    return result.reshape(state.shape)


def solution(mesh):
    return jax.shard_map(
        body,
        mesh=mesh,
        in_specs=(P("panel", None, "rad", "ang", None), P(None, "rad"), P("rad"), P(), P(), P()),
        out_specs=P("panel", None, "rad", "ang", None),
        check_vma=False,
    )
```

```python
import jax
import jax.numpy as jnp
from jax import lax
from jax.experimental import pallas as pl
from jax.experimental.pallas import tpu as pltpu
from jax.sharding import PartitionSpec as P

step_size = 0.1
HIGHEST = lax.Precision.HIGHEST
VMEM = pl.BlockSpec(memory_space=pltpu.VMEM)
F32 = jnp.float32

NF = 7
LV = 16
CP = 16
LAT = 128
TILE = LV * CP
BLOCK = 24
MESSAGE = 40


def params():
    return pltpu.CompilerParams(vmem_limit_bytes=40 * 1024 * 1024)


def cost(flops):
    return pl.CostEstimate(flops=flops, bytes_accessed=2_000_000, transcendentals=0)


def shape(*dims):
    return jax.ShapeDtypeStruct(dims, F32)


def picks(match, kid, slot):
    low = jnp.min(jnp.where(match, kid, 4096.0), axis=1, keepdims=True)
    high = jnp.max(jnp.where(match, kid, -1.0), axis=1, keepdims=True)
    low_or_none = jnp.where(low < 4096.0, low, -8.0)
    high_or_none = jnp.where(high > low, high, -8.0)
    return jnp.where(slot == 0, low_or_none, high_or_none)


def tables_kernel(
    kappa_ref, buoyancy_ref, lon_ref, lat_ref, frac_ref, coef_ref, lat_weight_ref, lon_weight_ref, beside_weight_ref,
    placed_ref,
):
    level = lax.broadcasted_iota(jnp.int32, (LV, LV), 0)
    same = level == lax.broadcasted_iota(jnp.int32, (LV, LV), 1)
    for f in range(NF + 1):
        line = kappa_ref[f : f + 1, :] if f < NF else buoyancy_ref[...]
        column = jnp.sum(jnp.where(same, line, 0.0), axis=1, keepdims=True)
        coef_ref[f] = jnp.broadcast_to(column, (LV, LAT))

    nlon = lon_ref.shape[1]
    half = 2 * nlon // CP
    points = 2 * nlon
    panel = lax.axis_index("panel")
    tile = lax.axis_index("ang")

    def flat(low, high):
        return jnp.concatenate([low, high], axis=1)

    lon_k = flat(lon_ref[0:1, :], lon_ref[1:2, :])
    owner_k = lon_k >> 4
    off_k = (lon_k & 15).astype(F32)
    lat_k = flat(lat_ref[0:1, :], lat_ref[1:2, :]).astype(F32)
    fx_k = flat(frac_ref[0, 0:1, :], frac_ref[0, 1:2, :])
    fy_k = flat(frac_ref[1, 0:1, :], frac_ref[1, 1:2, :])

    kid = lax.broadcasted_iota(jnp.int32, (1, points), 1)
    dest_k = (kid & (nlon - 1)) >> 4
    kid = kid.astype(F32)

    row = lax.broadcasted_iota(jnp.int32, (half, 1), 0)
    match = (dest_k == (row >> 1)) & (owner_k == tile)
    pick = picks(match, kid, row & 1)
    chosen = kid == pick

    def of(value):
        return jnp.sum(jnp.where(chosen, value, 0.0), axis=1, keepdims=True)

    off, lat, fx, fy = of(off_k), of(lat_k), of(fx_k), of(fy_k)
    lane = lax.broadcasted_iota(jnp.int32, (half, LAT), 1).astype(F32)
    lat_weight = jnp.where(lane == lat, 1.0 - fy, 0.0) + jnp.where(lane == lat + 1.0, fy, 0.0)
    lat_weight = jnp.where(pick >= 0.0, lat_weight, 0.0)
    lon_weight = jnp.where(lane == off, 1.0 - fx, 0.0) + jnp.where(lane == off + 1.0, fx, 0.0)
    shifted = pltpu.roll(lon_weight, CP, 1)
    beside = jnp.where(lane < CP, lat_weight[:, 1:2] * lon_weight, lat_weight[:, LAT - 2 : LAT - 1] * shifted)
    beside_weight_ref[...] = jnp.transpose(jnp.concatenate([beside, beside], axis=0))[0 : 2 * CP]
    lat_weight_ref[...] = jnp.transpose(jnp.concatenate([lat_weight, lat_weight], axis=0))
    lon_weight_ref[...] = jnp.transpose(jnp.concatenate([lon_weight, lon_weight], axis=0))[0:CP]

    row = lax.broadcasted_iota(jnp.int32, (half, 1), 0)
    match = (owner_k == (row >> 1)) & (dest_k == tile)
    pick = picks(match, kid, row & 1).astype(jnp.int32)
    target = ((pick >> (nlon.bit_length() - 1)) << 4) + (pick & 15)
    target = jnp.where(pick >= 0, target, -1)
    lane = lax.broadcasted_iota(jnp.int32, (half, 128), 1)
    place = jnp.where(lane == target, 1.0, 0.0)
    place = jnp.concatenate([place * panel.astype(F32), place * (1 - panel).astype(F32)], axis=0)
    placed_ref[...] = jnp.transpose(place)[0 : 2 * CP]


def increments(center, neighbours, kappa, buoyancy, scale):
    u = [(0.5 * scale) * center[d] for d in range(3)]
    b = [(0.5 * scale) * center[3 + d] for d in range(3)]
    lap, adv, mag = [], [], []
    for f in range(NF):
        up, down, east, west = neighbours(f)
        north = pltpu.roll(center[f], LAT - 1, 1)
        south = pltpu.roll(center[f], 1, 1)
        diffs = [up - down, east - west, north - south]
        lap.append((scale * kappa(f)) * ((up + down) + (east + west) + (north + south) - 6.0 * center[f]))
        adv.append(u[0] * diffs[0] + u[1] * diffs[1] + u[2] * diffs[2])
        if f < 6:
            mag.append(b[0] * diffs[0] + b[1] * diffs[1] + b[2] * diffs[2])
    rates = [lap[f] - adv[f] + mag[(f + 3) % 6] for f in range(6)] + [lap[6] - adv[6]]
    rates[0] = rates[0] + (scale * buoyancy) * center[6]
    return rates


def interpolate(rows, lat_weight_ref, lon_weight_ref):
    along = jnp.dot(rows, lat_weight_ref[...], precision=HIGHEST, preferred_element_type=F32)
    n = rows.shape[0] // CP
    return jnp.sum(along.reshape(n, CP, along.shape[1]) * lon_weight_ref[...][None], axis=1)


def cut_kernel(state_ref, outer_ref, inner_ref, own_ref, sems):
    parts = [pl.ds(f * TILE, TILE) for f in range(NF)]
    copies = [
        pltpu.make_async_copy(state_ref.at[part, :], own_ref.at[part, :], sems.at[f]) for f, part in enumerate(parts)
    ]
    for copy in copies:
        copy.start()
    odd = lax.axis_index("ang") % 2 == 1
    for f in range(NF):
        copies[f].wait()
        for i in range(2):
            low = own_ref[pl.ds(f * TILE + i, LV, CP), :]
            high = own_ref[pl.ds(f * TILE + CP - 1 - i, LV, CP), :]
            outer_ref[i, f] = jnp.where(odd, high, low)
            inner_ref[i, f] = jnp.where(odd, low, high)


def pack_kernel(state_ref, outer_ref, inner_ref, coef_ref, up_ref, down_ref, below_ref, above_ref):
    odd = lax.axis_index("ang") % 2 == 1
    for i in range(2):
        for f in range(NF):
            above_ref[i, f] = jnp.where(odd, outer_ref[i, f], inner_ref[i, f])
            below_ref[i, f] = jnp.where(odd, inner_ref[i, f], outer_ref[i, f])
    for ref, near, far in ((up_ref, LV - 1, LV - 2), (down_ref, 0, 1)):
        for f in range(NF):
            start = f * TILE
            ref[f, 0:CP, :] = state_ref[start + near * CP : start + (near + 1) * CP, :]
            ref[f, CP : 2 * CP, :] = state_ref[start + far * CP : start + (far + 1) * CP, :]
            ref[f, 32:33, :] = above_ref[0, f, near : near + 1, :]
            ref[f, 33:34, :] = below_ref[0, f, near : near + 1, :]
            ref[f, 34:35, :] = coef_ref[f, near : near + 1, :]
            ref[f, 35:36, :] = coef_ref[NF, near : near + 1, :]
            ref[f, 36:40, :] = jnp.zeros((4, LAT), F32)


def first_a_kernel(
    state_ref, below_ref, above_ref, coef_ref, lat_weight_ref, lon_weight_ref, inner_ref, values_ref, line_ref
):
    for f in range(NF):
        for r in range(LV):
            base = (f * LV + r) * BLOCK + 8
            line_ref[base : base + CP, :] = state_ref[f * TILE + r * CP : f * TILE + (r + 1) * CP, :]
        line_ref[pl.ds(f * LV * BLOCK + 7, LV, BLOCK), :] = below_ref[0, f]
        line_ref[pl.ds(f * LV * BLOCK + 24, LV, BLOCK), :] = above_ref[0, f]
    zero = jnp.zeros((8, LAT), F32)
    for r in range(LV):
        for t in range(2):

            def row(f, level=r):
                return f * TILE + level * CP + 8 * t

            def neighbours(f):
                line = (f * LV + r) * BLOCK + 8 + 8 * t
                return (
                    state_ref[row(f, r + 1) : row(f, r + 1) + 8, :] if r < LV - 1 else zero,
                    state_ref[row(f, r - 1) : row(f, r - 1) + 8, :] if r else zero,
                    line_ref[line + 1 : line + 9, :],
                    line_ref[line - 1 : line + 7, :],
                )

            center = [state_ref[row(f) : row(f) + 8, :] for f in range(NF)]
            rates = increments(
                center, neighbours, lambda f: coef_ref[f, r : r + 1, :], coef_ref[NF, r : r + 1, :], step_size
            )
            for f in range(NF):
                inner_ref[row(f) : row(f) + 8, :] = center[f] + rates[f]
    values_ref[...] = interpolate(inner_ref[...], lat_weight_ref, lon_weight_ref)


def first_b_kernel(
    state_ref, below_ref, above_ref, coef_ref, rad_below_ref, rad_above_ref, lat_weight_ref, lon_weight_ref,
    inner_ref, values_ref, edge_ref, ring_ref, send_ref, line_ref, column_ref, outside_ref, donors_ref,
):
    rad, ang = lax.axis_index("rad"), lax.axis_index("ang")
    keep_rad = [jnp.where(rad == 0, 0.0, 1.0), jnp.where(rad == lax.axis_size("rad") - 1, 0.0, 1.0)]
    keep_ang = [jnp.where(ang == 0, 0.0, 1.0), jnp.where(ang == lax.axis_size("ang") - 1, 0.0, 1.0)]
    radial = (rad_below_ref, rad_above_ref)

    for e, ref in enumerate(radial):
        level = e * (LV - 1) * CP
        sign = (0.5 - e) * step_size
        u = sign * state_ref[level : level + CP, :]
        b = sign * state_ref[3 * TILE + level : 3 * TILE + level + CP, :]
        near = [ref[f, 0:CP, :] for f in range(NF)]
        for f in range(NF):
            row = f * TILE + level
            gain = (step_size * coef_ref[f, e * (LV - 1) : e * (LV - 1) + 1, :] + u) * near[f]
            if f < 6:
                gain = gain - b * near[(f + 3) % 6]
            outside_ref[(e * 8 + f) * CP : (e * 8 + f + 1) * CP, :] = gain
            edge_ref[((e + 1) * 8 + f) * CP : ((e + 1) * 8 + f + 1) * CP, :] = inner_ref[row : row + CP, :] + gain
        outside_ref[(e * 8 + NF) * CP : (e * 8 + 8) * CP, :] = jnp.zeros((CP, LAT), F32)
    edges = interpolate(outside_ref[...], lat_weight_ref, lon_weight_ref)
    donors_ref[0 : NF * LV, :] = values_ref[...]
    donors_ref[NF * LV : 128, :] = jnp.zeros((128 - NF * LV, 128), F32)
    for f in range(NF):
        for e in range(2):
            row = f * LV + e * (LV - 1)
            donors_ref[row : row + 1, :] = values_ref[row : row + 1, :] + edges[e * 8 + f : e * 8 + f + 1]
    send_ref[...] = jnp.transpose(donors_ref[...])

    for f in range(NF):
        for e, ref in enumerate(radial):
            base = (e * NF + f) * BLOCK + 8
            line_ref[base : base + CP, :] = ref[f, 0:CP, :]
            line_ref[base - 1 : base, :] = ref[f, 33:34, :]
            line_ref[base + CP : base + CP + 1, :] = ref[f, 32:33, :]
        for side, ref in ((0, below_ref.at[0]), (1, above_ref.at[0])):
            base = (side * NF + f) * BLOCK + 8
            column_ref[base : base + LV, :] = ref[f]
            column_ref[base - 1 : base, :] = rad_below_ref[f, 33 - side : 34 - side, :]
            column_ref[base + LV : base + LV + 1, :] = rad_above_ref[f, 33 - side : 34 - side, :]

    for e, source in enumerate(radial):
        for t in range(2):
            part = slice(8 * t, 8 * t + 8)

            def neighbours(f):
                line = (e * NF + f) * BLOCK + 8 + 8 * t
                start = f * TILE + e * (LV - 1) * CP + 8 * t
                inside, outside = state_ref[start : start + 8, :], source[f, CP + 8 * t : CP + 8 * t + 8, :]
                up, down = (inside, outside) if e == 0 else (outside, inside)
                return up, down, line_ref[line + 1 : line + 9, :], line_ref[line - 1 : line + 7, :]

            center = [source[f, part, :] for f in range(NF)]
            rates = increments(center, neighbours, lambda f: source[f, 34:35, :], source[0, 35:36, :], step_size)
            for f in range(NF):
                base = (e * 24 + f) * CP + 8 * t
                edge_ref[base : base + 8, :] = keep_rad[e] * (center[f] + rates[f])

    for side in range(2):
        for t in range(2):
            part = slice(8 * t, 8 * t + 8)

            def neighbours(f):
                column = (side * NF + f) * BLOCK + 8 + 8 * t
                near = state_ref[pl.ds(f * TILE + 8 * t * CP + side * (CP - 1), 8, CP), :]
                if side == 0:
                    east, west = near, below_ref[1, f, part, :]
                else:
                    east, west = above_ref[1, f, part, :], near
                return column_ref[column + 1 : column + 9, :], column_ref[column - 1 : column + 7, :], east, west

            center = [(below_ref[0, f, part, :] if side == 0 else above_ref[0, f, part, :]) for f in range(NF)]
            rates = increments(center, neighbours, lambda f: coef_ref[f, part, :], coef_ref[NF, part, :], step_size)
            for f in range(NF):
                ring_ref[side, f, part, :] = keep_ang[side] * (center[f] + rates[f])


def first_at(inner_ref, edge_ref, f, r):
    if 1 <= r <= LV - 2:
        return inner_ref[f * TILE + r * CP : f * TILE + (r + 1) * CP, :]
    e = {-1: 0, 0: 1, LV - 1: 2, LV: 3}[r]
    return edge_ref[(e * 8 + f) * CP : (e * 8 + f + 1) * CP, :]


def second_a_kernel(
    state_ref, coef_ref, inner_ref, edge_ref, ring_ref, lat_weight_ref, lon_weight_ref, next_ref, mid_ref, line_ref
):
    lane = lax.broadcasted_iota(jnp.int32, (CP, LAT), 1)
    row = lax.broadcasted_iota(jnp.int32, (CP, LAT), 0)
    ends = (lane == 0) | (lane == LAT - 1)
    for i, f in enumerate((2, 5)):
        for r in range(LV):
            own = (0.25 * step_size) * first_at(inner_ref, edge_ref, f, r)
            low = jnp.where(lane == row, own[:, 1:2], 0.0)
            high = jnp.where(lane == row + CP, own[:, LAT - 2 : LAT - 1], 0.0)
            mid_ref[NF * LV + i * LV + r : NF * LV + i * LV + r + 1, :] = jnp.sum(low - high, axis=0, keepdims=True)
    for f in range(NF):
        for r in range(-1, LV + 1):
            base = (f * (LV + 2) + r + 1) * BLOCK + 8
            own = first_at(inner_ref, edge_ref, f, r)
            line_ref[base : base + CP, :] = jnp.where(ends, 0.0, own) if 0 <= r < LV else own
        start = (f * (LV + 2) + 1) * BLOCK
        line_ref[pl.ds(start + 7, LV, BLOCK), :] = ring_ref[0, f]
        line_ref[pl.ds(start + 24, LV, BLOCK), :] = ring_ref[1, f]

    for r in range(LV):
        for t in range(2):

            def line(f, level=r):
                return (f * (LV + 2) + level + 1) * BLOCK + 8 + 8 * t

            def neighbours(f):
                return (
                    line_ref[line(f, r + 1) : line(f, r + 1) + 8, :],
                    line_ref[line(f, r - 1) : line(f, r - 1) + 8, :],
                    line_ref[line(f) + 1 : line(f) + 9, :],
                    line_ref[line(f) - 1 : line(f) + 7, :],
                )

            center = [line_ref[line(f) : line(f) + 8, :] for f in range(NF)]
            rates = increments(
                center, neighbours, lambda f: coef_ref[f, r : r + 1, :], coef_ref[NF, r : r + 1, :], 0.5 * step_size
            )
            for f in range(NF):
                row = f * TILE + r * CP + 8 * t
                next_ref[row : row + 8, :] = 0.5 * (state_ref[row : row + 8, :] + center[f]) + rates[f]
    mid_ref[0 : NF * LV, :] = interpolate(next_ref[...], lat_weight_ref, lon_weight_ref)


def second_b_kernel(
    coef_ref, recv_ref, placed_ref, mid_ref, beside_weight_ref, beside_ref, send_ref
):
    ends = lax.dot_general(
        recv_ref[...], placed_ref[...], (((0,), (1,)), ((), ())), precision=HIGHEST, preferred_element_type=F32
    )
    ends = [ends[f * LV : (f + 1) * LV] for f in range(NF)]
    u = mid_ref[NF * LV : (NF + 1) * LV, 0 : 2 * CP]
    b = mid_ref[(NF + 1) * LV : (NF + 2) * LV, 0 : 2 * CP]
    gains = []
    for f in range(NF):
        gain = ((0.5 * step_size) * coef_ref[f, :, 0 : 2 * CP] + u) * ends[f]
        gains.append(gain - b * ends[(f + 3) % 6] if f < 6 else gain)
    gains = jnp.concatenate(gains, axis=0)
    added = jnp.dot(gains, beside_weight_ref[...], precision=HIGHEST, preferred_element_type=F32)
    blank = jnp.zeros((128 - NF * LV, 128), F32)
    send_ref[...] = jnp.transpose(jnp.concatenate([mid_ref[0 : NF * LV, :] + added, blank], axis=0))
    gains = jnp.concatenate([gains, jnp.zeros((NF * LV, 128 - 2 * CP), F32)], axis=1)
    beside_ref[...] = jnp.transpose(jnp.concatenate([gains, blank], axis=0))[0 : 2 * CP]


def last_kernel(next_ref, beside_ref, recv_ref, placed_ref, out_ref, done_ref, sems):
    values = jnp.dot(placed_ref[...], recv_ref[...], precision=HIGHEST, preferred_element_type=F32)
    parts = [
        values[0:CP],
        pltpu.roll(beside_ref[0:CP], 1, 1),
        pltpu.roll(beside_ref[CP : 2 * CP], LAT - 2, 1),
        pltpu.roll(values[CP : 2 * CP], LAT - 1, 1),
    ]
    lane = lax.broadcasted_iota(jnp.int32, (CP, LAT), 1)
    mixed = []
    for q in range(4):
        place = (lane - q) & 3
        mixed.append(
            jnp.where(place < 2, jnp.where(place == 0, parts[0], parts[1]), jnp.where(place == 2, parts[2], parts[3]))
        )
    ends = (lane == 0) | (lane == LAT - 1)
    near = (lane < 2) | (lane >= LAT - 2)
    copies = []
    for f in range(NF):
        for r in range(LV):
            row, point = f * TILE + r * CP, f * LV + r
            rows = mixed[point % 4]
            if point:
                rows = pltpu.roll(rows, LAT - point, 1)
            own = next_ref[row : row + CP, :]
            done_ref[row : row + CP, :] = jnp.where(ends, 0.0, own) + jnp.where(near, rows, 0.0)
        part = pl.ds(f * TILE, TILE)
        copies.append(pltpu.make_async_copy(done_ref.at[part, :], out_ref.at[part, :], sems.at[f]))
        copies[-1].start()
    for copy in copies:
        copy.wait()


def shift(value, axis, step):
    count = lax.axis_size(axis)
    pairs = [(i, i + step) for i in range(count) if 0 <= i + step < count]
    return lax.ppermute(value, axis, pairs)


def swap(value, axis, first):
    count = lax.axis_size(axis)
    low = range(first, count - 1, 2)
    return lax.ppermute(value, axis, [(i, i + 1) for i in low] + [(i + 1, i) for i in low])


def exchange(values):
    n = values.shape[0] // 2
    got = lax.all_to_all(values.reshape(n, 2, 128), ("panel", "ang"), 0, 0, tiled=True)
    return got.reshape(2 * n, 128)


def call(kernel, name, outs, scratch, flops, *operands):
    return pl.pallas_call(
        kernel,
        out_shape=outs,
        in_specs=[VMEM] * len(operands),
        out_specs=(VMEM,) * len(outs),
        scratch_shapes=scratch,
        compiler_params=params(),
        cost_estimate=cost(flops) if isinstance(flops, int) else flops,
        name=name,
    )(*operands)


def rows(count):
    return pltpu.VMEM((count, LAT), F32)


def body(state, kappa, buoyancy, donor_lon, donor_lat, fractions):
    n_send = 4 * donor_lon.shape[1] // CP
    own = state.reshape(NF * TILE, LAT)
    halo, message = shape(2, NF, LV, LAT), shape(NF, MESSAGE, LAT)
    outer, inner = pl.pallas_call(
        cut_kernel,
        out_shape=(halo, halo),
        in_specs=[pl.BlockSpec(memory_space=pl.ANY)],
        out_specs=(VMEM, VMEM),
        scratch_shapes=[rows(NF * TILE), pltpu.SemaphoreType.DMA((NF,))],
        compiler_params=pltpu.CompilerParams(vmem_limit_bytes=62 * 1024 * 1024),
        cost_estimate=pl.CostEstimate(flops=4_000_000_000, bytes_accessed=20_000_000, transcendentals=0),
        name="cut",
    )(own)
    outer = swap(outer, "ang", 1)
    inner = swap(inner, "ang", 0)
    coef, lat_weight, lon_weight, beside_weight, placed = call(
        tables_kernel, "tables",
        (
            shape(NF + 1, LV, LAT), shape(LAT, n_send), shape(CP, n_send), shape(2 * CP, n_send), shape(2 * CP, n_send),
        ), [], 4_000_000, kappa, buoyancy[None], donor_lon, donor_lat, fractions,
    )

    up, down, below, above = call(
        pack_kernel, "pack", (message, message, halo, halo), [], 100_000, own, outer, inner, coef
    )
    rad_below = shift(up, "rad", 1)
    rad_above = shift(down, "rad", -1)
    middle, values = call(
        first_a_kernel, "first_a", (shape(NF * TILE, LAT), shape(NF * LV, n_send)), [rows(NF * LV * BLOCK + 8)],
        60_000_000, own, below, above, coef, lat_weight, lon_weight,
    )
    edge, ring, out = call(
        first_b_kernel, "first_b", (shape(4 * 8 * CP, LAT), halo, shape(n_send, 128)),
        [rows(2 * NF * BLOCK + 8), rows(2 * NF * BLOCK + 8), rows(2 * 8 * CP), rows(128)], 10_000_000,
        own, below, above, coef, rad_below, rad_above, lat_weight, lon_weight, middle, values,
    )
    got = exchange(out)
    following, mid = call(
        second_a_kernel, "second_a", (shape(NF * TILE, LAT), shape((NF + 2) * LV, n_send)),
        [rows(NF * (LV + 2) * BLOCK + 8)], 60_000_000, own, coef, middle, edge, ring, lat_weight, lon_weight,
    )
    beside, out = call(
        second_b_kernel, "second_b", (shape(2 * CP, LAT), shape(n_send, 128)), [], 1_000_000,
        coef, got, placed, mid, beside_weight,
    )
    got = exchange(out)
    result = pl.pallas_call(
        last_kernel,
        out_shape=shape(NF * TILE, LAT),
        in_specs=[VMEM] * 4,
        out_specs=pl.BlockSpec(memory_space=pl.ANY),
        scratch_shapes=[rows(NF * TILE), pltpu.SemaphoreType.DMA((NF,))],
        compiler_params=params(),
        name="last",
    )(following, beside, got, placed)
    return result.reshape(state.shape)


def solution(mesh):
    return jax.shard_map(
        body,
        mesh=mesh,
        in_specs=(P("panel", None, "rad", "ang", None), P(None, "rad"), P("rad"), P(), P(), P()),
        out_specs=P("panel", None, "rad", "ang", None),
        check_vma=False,
    )
```

```python
import jax
import jax.numpy as jnp
from jax import lax
from jax.experimental import pallas as pl
from jax.experimental.pallas import tpu as pltpu
from jax.sharding import PartitionSpec as P

step_size = 0.1
HIGHEST = lax.Precision.HIGHEST
VMEM = pl.BlockSpec(memory_space=pltpu.VMEM)
F32 = jnp.float32

NF = 7
LV = 16
CP = 16
LAT = 128
TILE = LV * CP
BLOCK = 24
MESSAGE = 40


def params():
    return pltpu.CompilerParams(vmem_limit_bytes=40 * 1024 * 1024)


def cost(flops):
    return pl.CostEstimate(flops=flops, bytes_accessed=2_000_000, transcendentals=0)


def shape(*dims):
    return jax.ShapeDtypeStruct(dims, F32)


def picks(match, kid, slot):
    low = jnp.min(jnp.where(match, kid, 4096.0), axis=1, keepdims=True)
    high = jnp.max(jnp.where(match, kid, -1.0), axis=1, keepdims=True)
    low_or_none = jnp.where(low < 4096.0, low, -8.0)
    high_or_none = jnp.where(high > low, high, -8.0)
    return jnp.where(slot == 0, low_or_none, high_or_none)


def tables_kernel(
    kappa_ref, buoyancy_ref, lon_ref, lat_ref, frac_ref, coef_ref, lat_weight_ref, lon_weight_ref, beside_weight_ref,
    placed_ref,
):
    level = lax.broadcasted_iota(jnp.int32, (LV, LV), 0)
    same = level == lax.broadcasted_iota(jnp.int32, (LV, LV), 1)
    for f in range(NF + 1):
        line = kappa_ref[f : f + 1, :] if f < NF else buoyancy_ref[...]
        column = jnp.sum(jnp.where(same, line, 0.0), axis=1, keepdims=True)
        coef_ref[f] = jnp.broadcast_to(column, (LV, LAT))

    nlon = lon_ref.shape[1]
    half = 2 * nlon // CP
    points = 2 * nlon
    panel = lax.axis_index("panel")
    tile = lax.axis_index("ang")

    def flat(low, high):
        return jnp.concatenate([low, high], axis=1)

    lon_k = flat(lon_ref[0:1, :], lon_ref[1:2, :])
    owner_k = lon_k >> 4
    off_k = (lon_k & 15).astype(F32)
    lat_k = flat(lat_ref[0:1, :], lat_ref[1:2, :]).astype(F32)
    fx_k = flat(frac_ref[0, 0:1, :], frac_ref[0, 1:2, :])
    fy_k = flat(frac_ref[1, 0:1, :], frac_ref[1, 1:2, :])

    kid = lax.broadcasted_iota(jnp.int32, (1, points), 1)
    dest_k = (kid & (nlon - 1)) >> 4
    kid = kid.astype(F32)

    row = lax.broadcasted_iota(jnp.int32, (half, 1), 0)
    match = (dest_k == (row >> 1)) & (owner_k == tile)
    pick = picks(match, kid, row & 1)
    chosen = kid == pick

    def of(value):
        return jnp.sum(jnp.where(chosen, value, 0.0), axis=1, keepdims=True)

    off, lat, fx, fy = of(off_k), of(lat_k), of(fx_k), of(fy_k)
    lane = lax.broadcasted_iota(jnp.int32, (half, LAT), 1).astype(F32)
    lat_weight = jnp.where(lane == lat, 1.0 - fy, 0.0) + jnp.where(lane == lat + 1.0, fy, 0.0)
    lat_weight = jnp.where(pick >= 0.0, lat_weight, 0.0)
    lon_weight = jnp.where(lane == off, 1.0 - fx, 0.0) + jnp.where(lane == off + 1.0, fx, 0.0)
    shifted = pltpu.roll(lon_weight, CP, 1)
    beside = jnp.where(lane < CP, lat_weight[:, 1:2] * lon_weight, lat_weight[:, LAT - 2 : LAT - 1] * shifted)
    beside_weight_ref[...] = jnp.transpose(jnp.concatenate([beside, beside], axis=0))[0 : 2 * CP]
    lat_weight_ref[...] = jnp.transpose(jnp.concatenate([lat_weight, lat_weight], axis=0))
    lon_weight_ref[...] = jnp.transpose(jnp.concatenate([lon_weight, lon_weight], axis=0))[0:CP]

    row = lax.broadcasted_iota(jnp.int32, (half, 1), 0)
    match = (owner_k == (row >> 1)) & (dest_k == tile)
    pick = picks(match, kid, row & 1).astype(jnp.int32)
    target = ((pick >> (nlon.bit_length() - 1)) << 4) + (pick & 15)
    target = jnp.where(pick >= 0, target, -1)
    lane = lax.broadcasted_iota(jnp.int32, (half, 128), 1)
    place = jnp.where(lane == target, 1.0, 0.0)
    place = jnp.concatenate([place * panel.astype(F32), place * (1 - panel).astype(F32)], axis=0)
    placed_ref[...] = jnp.transpose(place)[0 : 2 * CP]


def increments(center, neighbours, kappa, buoyancy, scale):
    u = [(0.5 * scale) * center[d] for d in range(3)]
    b = [(0.5 * scale) * center[3 + d] for d in range(3)]
    lap, adv, mag = [], [], []
    for f in range(NF):
        up, down, east, west = neighbours(f)
        north = pltpu.roll(center[f], LAT - 1, 1)
        south = pltpu.roll(center[f], 1, 1)
        diffs = [up - down, east - west, north - south]
        lap.append((scale * kappa(f)) * ((up + down) + (east + west) + (north + south) - 6.0 * center[f]))
        adv.append(u[0] * diffs[0] + u[1] * diffs[1] + u[2] * diffs[2])
        if f < 6:
            mag.append(b[0] * diffs[0] + b[1] * diffs[1] + b[2] * diffs[2])
    rates = [lap[f] - adv[f] + mag[(f + 3) % 6] for f in range(6)] + [lap[6] - adv[6]]
    rates[0] = rates[0] + (scale * buoyancy) * center[6]
    return rates


def interpolate(rows, lat_weight_ref, lon_weight_ref):
    along = jnp.dot(rows, lat_weight_ref[...], precision=HIGHEST, preferred_element_type=F32)
    n = rows.shape[0] // CP
    return jnp.sum(along.reshape(n, CP, along.shape[1]) * lon_weight_ref[...][None], axis=1)


def cut_kernel(state_ref, own_ref, outer_ref, inner_ref, sems):
    parts = [pl.ds(f * TILE, TILE) for f in range(NF)]
    copies = [
        pltpu.make_async_copy(state_ref.at[part, :], own_ref.at[part, :], sems.at[f]) for f, part in enumerate(parts)
    ]
    for copy in copies:
        copy.start()
    odd = lax.axis_index("ang") % 2 == 1
    for f in range(NF):
        copies[f].wait()
        for i in range(2):
            low = own_ref[pl.ds(f * TILE + i, LV, CP), :]
            high = own_ref[pl.ds(f * TILE + CP - 1 - i, LV, CP), :]
            outer_ref[i, f] = jnp.where(odd, high, low)
            inner_ref[i, f] = jnp.where(odd, low, high)


def pack_kernel(state_ref, outer_ref, inner_ref, coef_ref, up_ref, down_ref, below_ref, above_ref):
    odd = lax.axis_index("ang") % 2 == 1
    for i in range(2):
        for f in range(NF):
            above_ref[i, f] = jnp.where(odd, outer_ref[i, f], inner_ref[i, f])
            below_ref[i, f] = jnp.where(odd, inner_ref[i, f], outer_ref[i, f])
    for ref, near, far in ((up_ref, LV - 1, LV - 2), (down_ref, 0, 1)):
        for f in range(NF):
            start = f * TILE
            ref[f, 0:CP, :] = state_ref[start + near * CP : start + (near + 1) * CP, :]
            ref[f, CP : 2 * CP, :] = state_ref[start + far * CP : start + (far + 1) * CP, :]
            ref[f, 32:33, :] = above_ref[0, f, near : near + 1, :]
            ref[f, 33:34, :] = below_ref[0, f, near : near + 1, :]
            ref[f, 34:35, :] = coef_ref[f, near : near + 1, :]
            ref[f, 35:36, :] = coef_ref[NF, near : near + 1, :]
            ref[f, 36:40, :] = jnp.zeros((4, LAT), F32)


def first_a_kernel(
    state_ref, below_ref, above_ref, coef_ref, lat_weight_ref, lon_weight_ref, inner_ref, values_ref, line_ref
):
    for f in range(NF):
        for r in range(LV):
            base = (f * LV + r) * BLOCK + 8
            line_ref[base : base + CP, :] = state_ref[f * TILE + r * CP : f * TILE + (r + 1) * CP, :]
        line_ref[pl.ds(f * LV * BLOCK + 7, LV, BLOCK), :] = below_ref[0, f]
        line_ref[pl.ds(f * LV * BLOCK + 24, LV, BLOCK), :] = above_ref[0, f]
    zero = jnp.zeros((8, LAT), F32)
    for r in range(LV):
        for t in range(2):

            def row(f, level=r):
                return f * TILE + level * CP + 8 * t

            def neighbours(f):
                line = (f * LV + r) * BLOCK + 8 + 8 * t
                return (
                    state_ref[row(f, r + 1) : row(f, r + 1) + 8, :] if r < LV - 1 else zero,
                    state_ref[row(f, r - 1) : row(f, r - 1) + 8, :] if r else zero,
                    line_ref[line + 1 : line + 9, :],
                    line_ref[line - 1 : line + 7, :],
                )

            center = [state_ref[row(f) : row(f) + 8, :] for f in range(NF)]
            rates = increments(
                center, neighbours, lambda f: coef_ref[f, r : r + 1, :], coef_ref[NF, r : r + 1, :], step_size
            )
            for f in range(NF):
                inner_ref[row(f) : row(f) + 8, :] = center[f] + rates[f]
    values_ref[...] = interpolate(inner_ref[...], lat_weight_ref, lon_weight_ref)


def first_b_kernel(
    state_ref, below_ref, above_ref, coef_ref, rad_below_ref, rad_above_ref, lat_weight_ref, lon_weight_ref,
    inner_ref, values_ref, edge_ref, ring_ref, send_ref, line_ref, column_ref, outside_ref, donors_ref,
):
    rad, ang = lax.axis_index("rad"), lax.axis_index("ang")
    keep_rad = [jnp.where(rad == 0, 0.0, 1.0), jnp.where(rad == lax.axis_size("rad") - 1, 0.0, 1.0)]
    keep_ang = [jnp.where(ang == 0, 0.0, 1.0), jnp.where(ang == lax.axis_size("ang") - 1, 0.0, 1.0)]
    radial = (rad_below_ref, rad_above_ref)

    for e, ref in enumerate(radial):
        level = e * (LV - 1) * CP
        sign = (0.5 - e) * step_size
        u = sign * state_ref[level : level + CP, :]
        b = sign * state_ref[3 * TILE + level : 3 * TILE + level + CP, :]
        near = [ref[f, 0:CP, :] for f in range(NF)]
        for f in range(NF):
            row = f * TILE + level
            gain = (step_size * coef_ref[f, e * (LV - 1) : e * (LV - 1) + 1, :] + u) * near[f]
            if f < 6:
                gain = gain - b * near[(f + 3) % 6]
            outside_ref[(e * 8 + f) * CP : (e * 8 + f + 1) * CP, :] = gain
            edge_ref[((e + 1) * 8 + f) * CP : ((e + 1) * 8 + f + 1) * CP, :] = inner_ref[row : row + CP, :] + gain
        outside_ref[(e * 8 + NF) * CP : (e * 8 + 8) * CP, :] = jnp.zeros((CP, LAT), F32)
    edges = interpolate(outside_ref[...], lat_weight_ref, lon_weight_ref)
    donors_ref[0 : NF * LV, :] = values_ref[...]
    donors_ref[NF * LV : 128, :] = jnp.zeros((128 - NF * LV, 128), F32)
    for f in range(NF):
        for e in range(2):
            row = f * LV + e * (LV - 1)
            donors_ref[row : row + 1, :] = values_ref[row : row + 1, :] + edges[e * 8 + f : e * 8 + f + 1]
    send_ref[...] = jnp.transpose(donors_ref[...])

    for f in range(NF):
        for e, ref in enumerate(radial):
            base = (e * NF + f) * BLOCK + 8
            line_ref[base : base + CP, :] = ref[f, 0:CP, :]
            line_ref[base - 1 : base, :] = ref[f, 33:34, :]
            line_ref[base + CP : base + CP + 1, :] = ref[f, 32:33, :]
        for side, ref in ((0, below_ref.at[0]), (1, above_ref.at[0])):
            base = (side * NF + f) * BLOCK + 8
            column_ref[base : base + LV, :] = ref[f]
            column_ref[base - 1 : base, :] = rad_below_ref[f, 33 - side : 34 - side, :]
            column_ref[base + LV : base + LV + 1, :] = rad_above_ref[f, 33 - side : 34 - side, :]

    for e, source in enumerate(radial):
        for t in range(2):
            part = slice(8 * t, 8 * t + 8)

            def neighbours(f):
                line = (e * NF + f) * BLOCK + 8 + 8 * t
                start = f * TILE + e * (LV - 1) * CP + 8 * t
                inside, outside = state_ref[start : start + 8, :], source[f, CP + 8 * t : CP + 8 * t + 8, :]
                up, down = (inside, outside) if e == 0 else (outside, inside)
                return up, down, line_ref[line + 1 : line + 9, :], line_ref[line - 1 : line + 7, :]

            center = [source[f, part, :] for f in range(NF)]
            rates = increments(center, neighbours, lambda f: source[f, 34:35, :], source[0, 35:36, :], step_size)
            for f in range(NF):
                base = (e * 24 + f) * CP + 8 * t
                edge_ref[base : base + 8, :] = keep_rad[e] * (center[f] + rates[f])

    for side in range(2):
        for t in range(2):
            part = slice(8 * t, 8 * t + 8)

            def neighbours(f):
                column = (side * NF + f) * BLOCK + 8 + 8 * t
                near = state_ref[pl.ds(f * TILE + 8 * t * CP + side * (CP - 1), 8, CP), :]
                if side == 0:
                    east, west = near, below_ref[1, f, part, :]
                else:
                    east, west = above_ref[1, f, part, :], near
                return column_ref[column + 1 : column + 9, :], column_ref[column - 1 : column + 7, :], east, west

            center = [(below_ref[0, f, part, :] if side == 0 else above_ref[0, f, part, :]) for f in range(NF)]
            rates = increments(center, neighbours, lambda f: coef_ref[f, part, :], coef_ref[NF, part, :], step_size)
            for f in range(NF):
                ring_ref[side, f, part, :] = keep_ang[side] * (center[f] + rates[f])


def first_at(inner_ref, edge_ref, f, r):
    if 1 <= r <= LV - 2:
        return inner_ref[f * TILE + r * CP : f * TILE + (r + 1) * CP, :]
    e = {-1: 0, 0: 1, LV - 1: 2, LV: 3}[r]
    return edge_ref[(e * 8 + f) * CP : (e * 8 + f + 1) * CP, :]


def second_a_kernel(
    state_ref, coef_ref, inner_ref, edge_ref, ring_ref, lat_weight_ref, lon_weight_ref, next_ref, mid_ref, line_ref
):
    lane = lax.broadcasted_iota(jnp.int32, (CP, LAT), 1)
    row = lax.broadcasted_iota(jnp.int32, (CP, LAT), 0)
    ends = (lane == 0) | (lane == LAT - 1)
    for i, f in enumerate((2, 5)):
        for r in range(LV):
            own = (0.25 * step_size) * first_at(inner_ref, edge_ref, f, r)
            low = jnp.where(lane == row, own[:, 1:2], 0.0)
            high = jnp.where(lane == row + CP, own[:, LAT - 2 : LAT - 1], 0.0)
            mid_ref[NF * LV + i * LV + r : NF * LV + i * LV + r + 1, :] = jnp.sum(low - high, axis=0, keepdims=True)
    for f in range(NF):
        for r in range(-1, LV + 1):
            base = (f * (LV + 2) + r + 1) * BLOCK + 8
            own = first_at(inner_ref, edge_ref, f, r)
            line_ref[base : base + CP, :] = jnp.where(ends, 0.0, own) if 0 <= r < LV else own
        start = (f * (LV + 2) + 1) * BLOCK
        line_ref[pl.ds(start + 7, LV, BLOCK), :] = ring_ref[0, f]
        line_ref[pl.ds(start + 24, LV, BLOCK), :] = ring_ref[1, f]

    for r in range(LV):
        for t in range(2):

            def line(f, level=r):
                return (f * (LV + 2) + level + 1) * BLOCK + 8 + 8 * t

            def neighbours(f):
                return (
                    line_ref[line(f, r + 1) : line(f, r + 1) + 8, :],
                    line_ref[line(f, r - 1) : line(f, r - 1) + 8, :],
                    line_ref[line(f) + 1 : line(f) + 9, :],
                    line_ref[line(f) - 1 : line(f) + 7, :],
                )

            center = [line_ref[line(f) : line(f) + 8, :] for f in range(NF)]
            rates = increments(
                center, neighbours, lambda f: coef_ref[f, r : r + 1, :], coef_ref[NF, r : r + 1, :], 0.5 * step_size
            )
            for f in range(NF):
                row = f * TILE + r * CP + 8 * t
                next_ref[row : row + 8, :] = 0.5 * (state_ref[row : row + 8, :] + center[f]) + rates[f]
    mid_ref[0 : NF * LV, :] = interpolate(next_ref[...], lat_weight_ref, lon_weight_ref)


def second_b_kernel(
    coef_ref, recv_ref, placed_ref, mid_ref, beside_weight_ref, beside_ref, send_ref
):
    ends = lax.dot_general(
        recv_ref[...], placed_ref[...], (((0,), (1,)), ((), ())), precision=HIGHEST, preferred_element_type=F32
    )
    ends = [ends[f * LV : (f + 1) * LV] for f in range(NF)]
    u = mid_ref[NF * LV : (NF + 1) * LV, 0 : 2 * CP]
    b = mid_ref[(NF + 1) * LV : (NF + 2) * LV, 0 : 2 * CP]
    gains = []
    for f in range(NF):
        gain = ((0.5 * step_size) * coef_ref[f, :, 0 : 2 * CP] + u) * ends[f]
        gains.append(gain - b * ends[(f + 3) % 6] if f < 6 else gain)
    gains = jnp.concatenate(gains, axis=0)
    added = jnp.dot(gains, beside_weight_ref[...], precision=HIGHEST, preferred_element_type=F32)
    blank = jnp.zeros((128 - NF * LV, 128), F32)
    send_ref[...] = jnp.transpose(jnp.concatenate([mid_ref[0 : NF * LV, :] + added, blank], axis=0))
    gains = jnp.concatenate([gains, jnp.zeros((NF * LV, 128 - 2 * CP), F32)], axis=1)
    beside_ref[...] = jnp.transpose(jnp.concatenate([gains, blank], axis=0))[0 : 2 * CP]


def last_kernel(next_ref, beside_ref, recv_ref, placed_ref, out_ref, done_ref, sems):
    values = jnp.dot(placed_ref[...], recv_ref[...], precision=HIGHEST, preferred_element_type=F32)
    parts = [
        values[0:CP],
        pltpu.roll(beside_ref[0:CP], 1, 1),
        pltpu.roll(beside_ref[CP : 2 * CP], LAT - 2, 1),
        pltpu.roll(values[CP : 2 * CP], LAT - 1, 1),
    ]
    lane = lax.broadcasted_iota(jnp.int32, (CP, LAT), 1)
    mixed = []
    for q in range(4):
        place = (lane - q) & 3
        mixed.append(
            jnp.where(place < 2, jnp.where(place == 0, parts[0], parts[1]), jnp.where(place == 2, parts[2], parts[3]))
        )
    ends = (lane == 0) | (lane == LAT - 1)
    near = (lane < 2) | (lane >= LAT - 2)
    copies = []
    for f in range(NF):
        for r in range(LV):
            row, point = f * TILE + r * CP, f * LV + r
            rows = mixed[point % 4]
            if point:
                rows = pltpu.roll(rows, LAT - point, 1)
            own = next_ref[row : row + CP, :]
            done_ref[row : row + CP, :] = jnp.where(ends, 0.0, own) + jnp.where(near, rows, 0.0)
        part = pl.ds(f * TILE, TILE)
        copies.append(pltpu.make_async_copy(done_ref.at[part, :], out_ref.at[part, :], sems.at[f]))
        copies[-1].start()
    for copy in copies:
        copy.wait()


def shift(value, axis, step):
    count = lax.axis_size(axis)
    pairs = [(i, i + step) for i in range(count) if 0 <= i + step < count]
    return lax.ppermute(value, axis, pairs)


def swap(value, axis, first):
    count = lax.axis_size(axis)
    low = range(first, count - 1, 2)
    return lax.ppermute(value, axis, [(i, i + 1) for i in low] + [(i + 1, i) for i in low])


def exchange(values):
    n = values.shape[0] // 2
    got = lax.all_to_all(values.reshape(n, 2, 128), ("panel", "ang"), 0, 0, tiled=True)
    return got.reshape(2 * n, 128)


def call(kernel, name, outs, scratch, flops, *operands):
    return pl.pallas_call(
        kernel,
        out_shape=outs,
        in_specs=[VMEM] * len(operands),
        out_specs=(VMEM,) * len(outs),
        scratch_shapes=scratch,
        compiler_params=params(),
        cost_estimate=cost(flops) if isinstance(flops, int) else flops,
        name=name,
    )(*operands)


def rows(count):
    return pltpu.VMEM((count, LAT), F32)


def body(state, kappa, buoyancy, donor_lon, donor_lat, fractions):
    n_send = 4 * donor_lon.shape[1] // CP
    halo, message = shape(2, NF, LV, LAT), shape(NF, MESSAGE, LAT)
    own, outer, inner = pl.pallas_call(
        cut_kernel,
        out_shape=(shape(NF * TILE, LAT), halo, halo),
        in_specs=[pl.BlockSpec(memory_space=pl.ANY)],
        out_specs=(VMEM,) * 3,
        scratch_shapes=[pltpu.SemaphoreType.DMA((NF,))],
        compiler_params=pltpu.CompilerParams(vmem_limit_bytes=52 * 1024 * 1024),
        cost_estimate=pl.CostEstimate(flops=4_000_000_000, bytes_accessed=20_000_000, transcendentals=0),
        name="cut",
    )(state.reshape(NF * TILE, LAT))
    outer = swap(outer, "ang", 1)
    inner = swap(inner, "ang", 0)
    coef, lat_weight, lon_weight, beside_weight, placed = call(
        tables_kernel, "tables",
        (
            shape(NF + 1, LV, LAT), shape(LAT, n_send), shape(CP, n_send), shape(2 * CP, n_send), shape(2 * CP, n_send),
        ), [], 4_000_000, kappa, buoyancy[None], donor_lon, donor_lat, fractions,
    )

    up, down, below, above = call(
        pack_kernel, "pack", (message, message, halo, halo), [], 100_000, own, outer, inner, coef
    )
    rad_below = shift(up, "rad", 1)
    rad_above = shift(down, "rad", -1)
    middle, values = call(
        first_a_kernel, "first_a", (shape(NF * TILE, LAT), shape(NF * LV, n_send)), [rows(NF * LV * BLOCK + 8)],
        60_000_000, own, below, above, coef, lat_weight, lon_weight,
    )
    edge, ring, out = call(
        first_b_kernel, "first_b", (shape(4 * 8 * CP, LAT), halo, shape(n_send, 128)),
        [rows(2 * NF * BLOCK + 8), rows(2 * NF * BLOCK + 8), rows(2 * 8 * CP), rows(128)], 10_000_000,
        own, below, above, coef, rad_below, rad_above, lat_weight, lon_weight, middle, values,
    )
    got = exchange(out)
    following, mid = call(
        second_a_kernel, "second_a", (shape(NF * TILE, LAT), shape((NF + 2) * LV, n_send)),
        [rows(NF * (LV + 2) * BLOCK + 8)], 60_000_000, own, coef, middle, edge, ring, lat_weight, lon_weight,
    )
    beside, out = call(
        second_b_kernel, "second_b", (shape(2 * CP, LAT), shape(n_send, 128)), [], 1_000_000,
        coef, got, placed, mid, beside_weight,
    )
    got = exchange(out)
    result = pl.pallas_call(
        last_kernel,
        out_shape=shape(NF * TILE, LAT),
        in_specs=[VMEM] * 4,
        out_specs=pl.BlockSpec(memory_space=pl.ANY),
        scratch_shapes=[rows(NF * TILE), pltpu.SemaphoreType.DMA((NF,))],
        compiler_params=params(),
        name="last",
    )(following, beside, got, placed)
    return result.reshape(state.shape)


def solution(mesh):
    return jax.shard_map(
        body,
        mesh=mesh,
        in_specs=(P("panel", None, "rad", "ang", None), P(None, "rad"), P("rad"), P(), P(), P()),
        out_specs=P("panel", None, "rad", "ang", None),
        check_vma=False,
    )
```

```python
import jax
import jax.numpy as jnp
from jax import lax
from jax.experimental import pallas as pl
from jax.experimental.pallas import tpu as pltpu
from jax.sharding import PartitionSpec as P

step_size = 0.1
HIGHEST = lax.Precision.HIGHEST
VMEM = pl.BlockSpec(memory_space=pltpu.VMEM)
F32 = jnp.float32

NF = 7
LV = 16
CP = 16
LAT = 128
TILE = LV * CP
BLOCK = 24
MESSAGE = 40


def params():
    return pltpu.CompilerParams(vmem_limit_bytes=40 * 1024 * 1024)


def cost(flops):
    return pl.CostEstimate(flops=flops, bytes_accessed=2_000_000, transcendentals=0)


def shape(*dims):
    return jax.ShapeDtypeStruct(dims, F32)


def picks(match, kid, slot):
    low = jnp.min(jnp.where(match, kid, 4096.0), axis=1, keepdims=True)
    high = jnp.max(jnp.where(match, kid, -1.0), axis=1, keepdims=True)
    low_or_none = jnp.where(low < 4096.0, low, -8.0)
    high_or_none = jnp.where(high > low, high, -8.0)
    return jnp.where(slot == 0, low_or_none, high_or_none)


def tables_kernel(
    kappa_ref, buoyancy_ref, lon_ref, lat_ref, frac_ref, coef_ref, lat_weight_ref, lon_weight_ref, beside_weight_ref,
    placed_ref,
):
    level = lax.broadcasted_iota(jnp.int32, (LV, LV), 0)
    same = level == lax.broadcasted_iota(jnp.int32, (LV, LV), 1)
    for f in range(NF + 1):
        line = kappa_ref[f : f + 1, :] if f < NF else buoyancy_ref[...]
        column = jnp.sum(jnp.where(same, line, 0.0), axis=1, keepdims=True)
        coef_ref[f] = jnp.broadcast_to(column, (LV, LAT))

    nlon = lon_ref.shape[1]
    half = 2 * nlon // CP
    points = 2 * nlon
    panel = lax.axis_index("panel")
    tile = lax.axis_index("ang")

    def flat(low, high):
        return jnp.concatenate([low, high], axis=1)

    lon_k = flat(lon_ref[0:1, :], lon_ref[1:2, :])
    owner_k = lon_k >> 4
    off_k = (lon_k & 15).astype(F32)
    lat_k = flat(lat_ref[0:1, :], lat_ref[1:2, :]).astype(F32)
    fx_k = flat(frac_ref[0, 0:1, :], frac_ref[0, 1:2, :])
    fy_k = flat(frac_ref[1, 0:1, :], frac_ref[1, 1:2, :])

    kid = lax.broadcasted_iota(jnp.int32, (1, points), 1)
    dest_k = (kid & (nlon - 1)) >> 4
    kid = kid.astype(F32)

    row = lax.broadcasted_iota(jnp.int32, (half, 1), 0)
    match = (dest_k == (row >> 1)) & (owner_k == tile)
    pick = picks(match, kid, row & 1)
    chosen = kid == pick

    def of(value):
        return jnp.sum(jnp.where(chosen, value, 0.0), axis=1, keepdims=True)

    off, lat, fx, fy = of(off_k), of(lat_k), of(fx_k), of(fy_k)
    lane = lax.broadcasted_iota(jnp.int32, (half, LAT), 1).astype(F32)
    lat_weight = jnp.where(lane == lat, 1.0 - fy, 0.0) + jnp.where(lane == lat + 1.0, fy, 0.0)
    lat_weight = jnp.where(pick >= 0.0, lat_weight, 0.0)
    lon_weight = jnp.where(lane == off, 1.0 - fx, 0.0) + jnp.where(lane == off + 1.0, fx, 0.0)
    shifted = pltpu.roll(lon_weight, CP, 1)
    beside = jnp.where(lane < CP, lat_weight[:, 1:2] * lon_weight, lat_weight[:, LAT - 2 : LAT - 1] * shifted)
    beside_weight_ref[...] = jnp.transpose(jnp.concatenate([beside, beside], axis=0))[0 : 2 * CP]
    lat_weight_ref[...] = jnp.transpose(jnp.concatenate([lat_weight, lat_weight], axis=0))
    lon_weight_ref[...] = jnp.transpose(jnp.concatenate([lon_weight, lon_weight], axis=0))[0:CP]

    row = lax.broadcasted_iota(jnp.int32, (half, 1), 0)
    match = (owner_k == (row >> 1)) & (dest_k == tile)
    pick = picks(match, kid, row & 1).astype(jnp.int32)
    target = ((pick >> (nlon.bit_length() - 1)) << 4) + (pick & 15)
    target = jnp.where(pick >= 0, target, -1)
    lane = lax.broadcasted_iota(jnp.int32, (half, 128), 1)
    place = jnp.where(lane == target, 1.0, 0.0)
    place = jnp.concatenate([place * panel.astype(F32), place * (1 - panel).astype(F32)], axis=0)
    placed_ref[...] = jnp.transpose(place)[0 : 2 * CP]


def increments(center, neighbours, kappa, buoyancy, scale):
    u = [(0.5 * scale) * center[d] for d in range(3)]
    b = [(0.5 * scale) * center[3 + d] for d in range(3)]
    lap, adv, mag = [], [], []
    for f in range(NF):
        up, down, east, west = neighbours(f)
        north = pltpu.roll(center[f], LAT - 1, 1)
        south = pltpu.roll(center[f], 1, 1)
        diffs = [up - down, east - west, north - south]
        lap.append((scale * kappa(f)) * ((up + down) + (east + west) + (north + south) - 6.0 * center[f]))
        adv.append(u[0] * diffs[0] + u[1] * diffs[1] + u[2] * diffs[2])
        if f < 6:
            mag.append(b[0] * diffs[0] + b[1] * diffs[1] + b[2] * diffs[2])
    rates = [lap[f] - adv[f] + mag[(f + 3) % 6] for f in range(6)] + [lap[6] - adv[6]]
    rates[0] = rates[0] + (scale * buoyancy) * center[6]
    return rates


def interpolate(rows, lat_weight_ref, lon_weight_ref):
    along = jnp.dot(rows, lat_weight_ref[...], precision=HIGHEST, preferred_element_type=F32)
    n = rows.shape[0] // CP
    return jnp.sum(along.reshape(n, CP, along.shape[1]) * lon_weight_ref[...][None], axis=1)


def cut_kernel(state_ref, own_ref, outer_ref, inner_ref, sems):
    parts = [pl.ds(f * TILE, TILE) for f in range(NF)]
    copies = [
        pltpu.make_async_copy(state_ref.at[part, :], own_ref.at[part, :], sems.at[f]) for f, part in enumerate(parts)
    ]
    for copy in copies:
        copy.start()
    odd = lax.axis_index("ang") % 2 == 1
    for f in range(NF):
        copies[f].wait()
        for i in range(2):
            low = own_ref[pl.ds(f * TILE + i, LV, CP), :]
            high = own_ref[pl.ds(f * TILE + CP - 1 - i, LV, CP), :]
            outer_ref[i, f] = jnp.where(odd, high, low)
            inner_ref[i, f] = jnp.where(odd, low, high)


def pack_kernel(state_ref, outer_ref, inner_ref, coef_ref, up_ref, down_ref, below_ref, above_ref):
    odd = lax.axis_index("ang") % 2 == 1
    for i in range(2):
        for f in range(NF):
            above_ref[i, f] = jnp.where(odd, outer_ref[i, f], inner_ref[i, f])
            below_ref[i, f] = jnp.where(odd, inner_ref[i, f], outer_ref[i, f])
    for ref, near, far in ((up_ref, LV - 1, LV - 2), (down_ref, 0, 1)):
        for f in range(NF):
            start = f * TILE
            ref[f, 0:CP, :] = state_ref[start + near * CP : start + (near + 1) * CP, :]
            ref[f, CP : 2 * CP, :] = state_ref[start + far * CP : start + (far + 1) * CP, :]
            ref[f, 32:33, :] = above_ref[0, f, near : near + 1, :]
            ref[f, 33:34, :] = below_ref[0, f, near : near + 1, :]
            ref[f, 34:35, :] = coef_ref[f, near : near + 1, :]
            ref[f, 35:36, :] = coef_ref[NF, near : near + 1, :]
            ref[f, 36:40, :] = jnp.zeros((4, LAT), F32)


def first_a_kernel(
    state_ref, below_ref, above_ref, coef_ref, lat_weight_ref, lon_weight_ref, inner_ref, values_ref, line_ref
):
    for f in range(NF):
        for r in range(LV):
            base = (f * LV + r) * BLOCK + 8
            line_ref[base : base + CP, :] = state_ref[f * TILE + r * CP : f * TILE + (r + 1) * CP, :]
        line_ref[pl.ds(f * LV * BLOCK + 7, LV, BLOCK), :] = below_ref[0, f]
        line_ref[pl.ds(f * LV * BLOCK + 24, LV, BLOCK), :] = above_ref[0, f]
    zero = jnp.zeros((8, LAT), F32)
    for r in range(LV):
        for t in range(2):

            def row(f, level=r):
                return f * TILE + level * CP + 8 * t

            def neighbours(f):
                line = (f * LV + r) * BLOCK + 8 + 8 * t
                return (
                    state_ref[row(f, r + 1) : row(f, r + 1) + 8, :] if r < LV - 1 else zero,
                    state_ref[row(f, r - 1) : row(f, r - 1) + 8, :] if r else zero,
                    line_ref[line + 1 : line + 9, :],
                    line_ref[line - 1 : line + 7, :],
                )

            center = [state_ref[row(f) : row(f) + 8, :] for f in range(NF)]
            rates = increments(
                center, neighbours, lambda f: coef_ref[f, r : r + 1, :], coef_ref[NF, r : r + 1, :], step_size
            )
            for f in range(NF):
                inner_ref[row(f) : row(f) + 8, :] = center[f] + rates[f]
    values_ref[...] = interpolate(inner_ref[...], lat_weight_ref, lon_weight_ref)


def first_b_kernel(
    state_ref, below_ref, above_ref, coef_ref, rad_below_ref, rad_above_ref, lat_weight_ref, lon_weight_ref,
    inner_ref, values_ref, edge_ref, ring_ref, send_ref, line_ref, column_ref, outside_ref, donors_ref,
):
    rad, ang = lax.axis_index("rad"), lax.axis_index("ang")
    keep_rad = [jnp.where(rad == 0, 0.0, 1.0), jnp.where(rad == lax.axis_size("rad") - 1, 0.0, 1.0)]
    keep_ang = [jnp.where(ang == 0, 0.0, 1.0), jnp.where(ang == lax.axis_size("ang") - 1, 0.0, 1.0)]
    radial = (rad_below_ref, rad_above_ref)

    for e, ref in enumerate(radial):
        level = e * (LV - 1) * CP
        sign = (0.5 - e) * step_size
        u = sign * state_ref[level : level + CP, :]
        b = sign * state_ref[3 * TILE + level : 3 * TILE + level + CP, :]
        near = [ref[f, 0:CP, :] for f in range(NF)]
        for f in range(NF):
            row = f * TILE + level
            gain = (step_size * coef_ref[f, e * (LV - 1) : e * (LV - 1) + 1, :] + u) * near[f]
            if f < 6:
                gain = gain - b * near[(f + 3) % 6]
            outside_ref[(e * 8 + f) * CP : (e * 8 + f + 1) * CP, :] = gain
            edge_ref[((e + 1) * 8 + f) * CP : ((e + 1) * 8 + f + 1) * CP, :] = inner_ref[row : row + CP, :] + gain
        outside_ref[(e * 8 + NF) * CP : (e * 8 + 8) * CP, :] = jnp.zeros((CP, LAT), F32)
    edges = interpolate(outside_ref[...], lat_weight_ref, lon_weight_ref)
    donors_ref[0 : NF * LV, :] = values_ref[...]
    donors_ref[NF * LV : 128, :] = jnp.zeros((128 - NF * LV, 128), F32)
    for f in range(NF):
        for e in range(2):
            row = f * LV + e * (LV - 1)
            donors_ref[row : row + 1, :] = values_ref[row : row + 1, :] + edges[e * 8 + f : e * 8 + f + 1]
    send_ref[...] = jnp.transpose(donors_ref[...])

    for f in range(NF):
        for e, ref in enumerate(radial):
            base = (e * NF + f) * BLOCK + 8
            line_ref[base : base + CP, :] = ref[f, 0:CP, :]
            line_ref[base - 1 : base, :] = ref[f, 33:34, :]
            line_ref[base + CP : base + CP + 1, :] = ref[f, 32:33, :]
        for side, ref in ((0, below_ref.at[0]), (1, above_ref.at[0])):
            base = (side * NF + f) * BLOCK + 8
            column_ref[base : base + LV, :] = ref[f]
            column_ref[base - 1 : base, :] = rad_below_ref[f, 33 - side : 34 - side, :]
            column_ref[base + LV : base + LV + 1, :] = rad_above_ref[f, 33 - side : 34 - side, :]

    for e, source in enumerate(radial):
        for t in range(2):
            part = slice(8 * t, 8 * t + 8)

            def neighbours(f):
                line = (e * NF + f) * BLOCK + 8 + 8 * t
                start = f * TILE + e * (LV - 1) * CP + 8 * t
                inside, outside = state_ref[start : start + 8, :], source[f, CP + 8 * t : CP + 8 * t + 8, :]
                up, down = (inside, outside) if e == 0 else (outside, inside)
                return up, down, line_ref[line + 1 : line + 9, :], line_ref[line - 1 : line + 7, :]

            center = [source[f, part, :] for f in range(NF)]
            rates = increments(center, neighbours, lambda f: source[f, 34:35, :], source[0, 35:36, :], step_size)
            for f in range(NF):
                base = (e * 24 + f) * CP + 8 * t
                edge_ref[base : base + 8, :] = keep_rad[e] * (center[f] + rates[f])

    for side in range(2):
        for t in range(2):
            part = slice(8 * t, 8 * t + 8)

            def neighbours(f):
                column = (side * NF + f) * BLOCK + 8 + 8 * t
                near = state_ref[pl.ds(f * TILE + 8 * t * CP + side * (CP - 1), 8, CP), :]
                if side == 0:
                    east, west = near, below_ref[1, f, part, :]
                else:
                    east, west = above_ref[1, f, part, :], near
                return column_ref[column + 1 : column + 9, :], column_ref[column - 1 : column + 7, :], east, west

            center = [(below_ref[0, f, part, :] if side == 0 else above_ref[0, f, part, :]) for f in range(NF)]
            rates = increments(center, neighbours, lambda f: coef_ref[f, part, :], coef_ref[NF, part, :], step_size)
            for f in range(NF):
                ring_ref[side, f, part, :] = keep_ang[side] * (center[f] + rates[f])


def first_at(inner_ref, edge_ref, f, r):
    if 1 <= r <= LV - 2:
        return inner_ref[f * TILE + r * CP : f * TILE + (r + 1) * CP, :]
    e = {-1: 0, 0: 1, LV - 1: 2, LV: 3}[r]
    return edge_ref[(e * 8 + f) * CP : (e * 8 + f + 1) * CP, :]


def second_a_kernel(
    state_ref, coef_ref, inner_ref, edge_ref, ring_ref, lat_weight_ref, lon_weight_ref, next_ref, mid_ref, line_ref
):
    lane = lax.broadcasted_iota(jnp.int32, (CP, LAT), 1)
    row = lax.broadcasted_iota(jnp.int32, (CP, LAT), 0)
    ends = (lane == 0) | (lane == LAT - 1)
    for i, f in enumerate((2, 5)):
        for r in range(LV):
            own = (0.25 * step_size) * first_at(inner_ref, edge_ref, f, r)
            low = jnp.where(lane == row, own[:, 1:2], 0.0)
            high = jnp.where(lane == row + CP, own[:, LAT - 2 : LAT - 1], 0.0)
            mid_ref[NF * LV + i * LV + r : NF * LV + i * LV + r + 1, :] = jnp.sum(low - high, axis=0, keepdims=True)
    for f in range(NF):
        for r in range(-1, LV + 1):
            base = (f * (LV + 2) + r + 1) * BLOCK + 8
            own = first_at(inner_ref, edge_ref, f, r)
            line_ref[base : base + CP, :] = jnp.where(ends, 0.0, own) if 0 <= r < LV else own
        start = (f * (LV + 2) + 1) * BLOCK
        line_ref[pl.ds(start + 7, LV, BLOCK), :] = ring_ref[0, f]
        line_ref[pl.ds(start + 24, LV, BLOCK), :] = ring_ref[1, f]

    for r in range(LV):
        for t in range(2):

            def line(f, level=r):
                return (f * (LV + 2) + level + 1) * BLOCK + 8 + 8 * t

            def neighbours(f):
                return (
                    line_ref[line(f, r + 1) : line(f, r + 1) + 8, :],
                    line_ref[line(f, r - 1) : line(f, r - 1) + 8, :],
                    line_ref[line(f) + 1 : line(f) + 9, :],
                    line_ref[line(f) - 1 : line(f) + 7, :],
                )

            center = [line_ref[line(f) : line(f) + 8, :] for f in range(NF)]
            rates = increments(
                center, neighbours, lambda f: coef_ref[f, r : r + 1, :], coef_ref[NF, r : r + 1, :], 0.5 * step_size
            )
            for f in range(NF):
                row = f * TILE + r * CP + 8 * t
                next_ref[row : row + 8, :] = 0.5 * (state_ref[row : row + 8, :] + center[f]) + rates[f]
    mid_ref[0 : NF * LV, :] = interpolate(next_ref[...], lat_weight_ref, lon_weight_ref)


def second_b_kernel(
    coef_ref, recv_ref, placed_ref, mid_ref, beside_weight_ref, beside_ref, send_ref
):
    ends = lax.dot_general(
        recv_ref[...], placed_ref[...], (((0,), (1,)), ((), ())), precision=HIGHEST, preferred_element_type=F32
    )
    ends = [ends[f * LV : (f + 1) * LV] for f in range(NF)]
    u = mid_ref[NF * LV : (NF + 1) * LV, 0 : 2 * CP]
    b = mid_ref[(NF + 1) * LV : (NF + 2) * LV, 0 : 2 * CP]
    gains = []
    for f in range(NF):
        gain = ((0.5 * step_size) * coef_ref[f, :, 0 : 2 * CP] + u) * ends[f]
        gains.append(gain - b * ends[(f + 3) % 6] if f < 6 else gain)
    gains = jnp.concatenate(gains, axis=0)
    added = jnp.dot(gains, beside_weight_ref[...], precision=HIGHEST, preferred_element_type=F32)
    blank = jnp.zeros((128 - NF * LV, 128), F32)
    send_ref[...] = jnp.transpose(jnp.concatenate([mid_ref[0 : NF * LV, :] + added, blank], axis=0))
    gains = jnp.concatenate([gains, jnp.zeros((NF * LV, 128 - 2 * CP), F32)], axis=1)
    beside_ref[...] = jnp.transpose(jnp.concatenate([gains, blank], axis=0))[0 : 2 * CP]


def last_kernel(next_ref, beside_ref, recv_ref, placed_ref, out_ref, done_ref, sems):
    values = jnp.dot(placed_ref[...], recv_ref[...], precision=HIGHEST, preferred_element_type=F32)
    parts = [
        values[0:CP],
        pltpu.roll(beside_ref[0:CP], 1, 1),
        pltpu.roll(beside_ref[CP : 2 * CP], LAT - 2, 1),
        pltpu.roll(values[CP : 2 * CP], LAT - 1, 1),
    ]
    lane = lax.broadcasted_iota(jnp.int32, (CP, LAT), 1)
    mixed = []
    for q in range(4):
        place = (lane - q) & 3
        mixed.append(
            jnp.where(place < 2, jnp.where(place == 0, parts[0], parts[1]), jnp.where(place == 2, parts[2], parts[3]))
        )
    ends = (lane == 0) | (lane == LAT - 1)
    near = (lane < 2) | (lane >= LAT - 2)
    copies = []
    for f in range(NF):
        for r in range(LV):
            row, point = f * TILE + r * CP, f * LV + r
            rows = mixed[point % 4]
            if point:
                rows = pltpu.roll(rows, LAT - point, 1)
            own = next_ref[row : row + CP, :]
            done_ref[row : row + CP, :] = jnp.where(ends, 0.0, own) + jnp.where(near, rows, 0.0)
        part = pl.ds(f * TILE, TILE)
        copies.append(pltpu.make_async_copy(done_ref.at[part, :], out_ref.at[part, :], sems.at[f]))
        copies[-1].start()
    for copy in copies:
        copy.wait()


def shift(value, axis, step):
    count = lax.axis_size(axis)
    pairs = [(i, i + step) for i in range(count) if 0 <= i + step < count]
    return lax.ppermute(value, axis, pairs)


def swap(value, axis, first):
    count = lax.axis_size(axis)
    low = range(first, count - 1, 2)
    return lax.ppermute(value, axis, [(i, i + 1) for i in low] + [(i + 1, i) for i in low])


def exchange(values):
    n = values.shape[0] // 2
    got = lax.all_to_all(values.reshape(n, 2, 128), ("panel", "ang"), 0, 0, tiled=True)
    return got.reshape(2 * n, 128)


def call(kernel, name, outs, scratch, flops, *operands):
    return pl.pallas_call(
        kernel,
        out_shape=outs,
        in_specs=[VMEM] * len(operands),
        out_specs=(VMEM,) * len(outs),
        scratch_shapes=scratch,
        compiler_params=params(),
        cost_estimate=cost(flops) if isinstance(flops, int) else flops,
        name=name,
    )(*operands)


def rows(count):
    return pltpu.VMEM((count, LAT), F32)


def body(state, kappa, buoyancy, donor_lon, donor_lat, fractions):
    n_send = 4 * donor_lon.shape[1] // CP
    halo, message = shape(2, NF, LV, LAT), shape(NF, MESSAGE, LAT)
    own, outer, inner = pl.pallas_call(
        cut_kernel,
        out_shape=(shape(NF * TILE, LAT), halo, halo),
        in_specs=[pl.BlockSpec(memory_space=pl.ANY)],
        out_specs=(VMEM,) * 3,
        scratch_shapes=[pltpu.SemaphoreType.DMA((NF,))],
        compiler_params=pltpu.CompilerParams(vmem_limit_bytes=52 * 1024 * 1024),
        cost_estimate=pl.CostEstimate(flops=4_000_000_000, bytes_accessed=20_000_000, transcendentals=0),
        name="cut",
    )(state.reshape(NF * TILE, LAT))
    outer = swap(outer, "ang", 1)
    inner = swap(inner, "ang", 0)
    coef, lat_weight, lon_weight, beside_weight, placed = call(
        tables_kernel, "tables",
        (
            shape(NF + 1, LV, LAT), shape(LAT, n_send), shape(CP, n_send), shape(2 * CP, n_send), shape(2 * CP, n_send),
        ), [], 4_000_000, kappa, buoyancy[None], donor_lon, donor_lat, fractions,
    )

    up, down, below, above = call(
        pack_kernel, "pack", (message, message, halo, halo), [], 100_000, own, outer, inner, coef
    )
    rad_above = shift(down, "rad", -1)
    rad_below = shift(up, "rad", 1)
    middle, values = call(
        first_a_kernel, "first_a", (shape(NF * TILE, LAT), shape(NF * LV, n_send)), [rows(NF * LV * BLOCK + 8)],
        60_000_000, own, below, above, coef, lat_weight, lon_weight,
    )
    edge, ring, out = call(
        first_b_kernel, "first_b", (shape(4 * 8 * CP, LAT), halo, shape(n_send, 128)),
        [rows(2 * NF * BLOCK + 8), rows(2 * NF * BLOCK + 8), rows(2 * 8 * CP), rows(128)], 10_000_000,
        own, below, above, coef, rad_below, rad_above, lat_weight, lon_weight, middle, values,
    )
    got = exchange(out)
    following, mid = call(
        second_a_kernel, "second_a", (shape(NF * TILE, LAT), shape((NF + 2) * LV, n_send)),
        [rows(NF * (LV + 2) * BLOCK + 8)], 60_000_000, own, coef, middle, edge, ring, lat_weight, lon_weight,
    )
    beside, out = call(
        second_b_kernel, "second_b", (shape(2 * CP, LAT), shape(n_send, 128)), [], 1_000_000,
        coef, got, placed, mid, beside_weight,
    )
    got = exchange(out)
    result = pl.pallas_call(
        last_kernel,
        out_shape=shape(NF * TILE, LAT),
        in_specs=[VMEM] * 4,
        out_specs=pl.BlockSpec(memory_space=pl.ANY),
        scratch_shapes=[rows(NF * TILE), pltpu.SemaphoreType.DMA((NF,))],
        compiler_params=params(),
        name="last",
    )(following, beside, got, placed)
    return result.reshape(state.shape)


def solution(mesh):
    return jax.shard_map(
        body,
        mesh=mesh,
        in_specs=(P("panel", None, "rad", "ang", None), P(None, "rad"), P("rad"), P(), P(), P()),
        out_specs=P("panel", None, "rad", "ang", None),
        check_vma=False,
    )
```
